128 devices in a mesh: row: 8 (over x_lo, y), col: 16 (over z, x_hi, core).
Axes of the slice: x: 4 (x_hi: 2, x_lo: 2; x = x_hi * 2 + x_lo), y: 4, z: 4, core: 2. Of those that a mesh axis runs over, the one named last changes fastest.
Arguments:
- features: bfloat16 [65536, 1024], P(('row', 'col')), may hold values from -6 to 6
- walk_counts: int32 [8, 16, 64, 128, 128], P('row', 'col'), may hold values from 0 to 15
- tile_rows: int32 [8, 16, 64], P('row', 'col'), may hold values from 0 to 63
- tile_cols: int32 [8, 16, 64], P('row', 'col'), may hold values from 0 to 31
- live_tiles: int32 [8, 16], P('row', 'col'), may hold values from 8 to 64, as said below
- neigh_weight: bfloat16 [1024, 1024], replicated, may hold values from -0.1875 to 0.1875
- neigh_bias: float32 [1024], replicated, may hold values from -3 to 3
- combine_weight: bfloat16 [2048, 1024], replicated, may hold values from -0.125 to 0.125
- combine_bias: float32 [1024], replicated, may hold values from -3 to 3
Outputs:
- embeddings: float32 [65536, 1024], P(('row', 'col'))
The draws below stay inside these ranges and needn't reach their ends.
Inputs may be any that keep to these rules, and one draw needn't show every extreme that they name: Slots from live_tiles on are unused; some device has all 64 slots used in every draw.
All inputs are finite; a program needn't handle non-finite values.
Results may differ from the reference program's by a relative error of at most 0.0055.
Values may be sent and summed in bfloat16 or wider, within the bound.
No kernel may reach another device: no remote copies, remote signals or barrier semaphores. Data moves between devices by JAX's collectives and lax.ppermute only.
A program may use at most 320 MiB of HBM per device.

```python
import jax
import jax.numpy as jnp
from jax import lax

F = 1024
TILE = 128
NODE_DEV = 512
SLOTS = 64
NODES = 65536
BAND_BLK = 64
PANEL_BLK = 32
N_ROW = 8
N_COL = 16


def draw_live_tiles(key, part):
    first, second = jax.random.split(jax.random.fold_in(key, 7))
    lowest = max(SLOTS // 8, 1)
    live = jax.random.randint(first, (N_ROW * N_COL,), lowest, SLOTS + 1)
    chosen = jax.random.randint(second, (), 0, N_ROW * N_COL)
    live = jnp.where(jnp.arange(N_ROW * N_COL) == chosen, SLOTS, live)
    return live.reshape(N_ROW, N_COL).astype(jnp.int32)


def plant(result, rng, smallest, high):
    longest = result.shape.index(max(result.shape))
    spots = []
    for shift in (0, 1):
        where = [jax.random.randint(jax.random.fold_in(rng, axis), (), 0, length) for axis, length in enumerate(result.shape)]
        where[longest] = (where[longest] + shift) % result.shape[longest]
        spots.append(tuple(where))
    return result.at[spots[0]].set(smallest).at[spots[1]].set(high)


def block_levels(own_key, shape, shards, low, top_value):
    gain = 1.0
    for axis_at, blocks in shards:
        steps = jax.random.uniform(jax.random.fold_in(jax.random.fold_in(own_key, 6), axis_at), (blocks,), jnp.float32, low / len(shards), top_value / len(shards))
        gain = gain * jnp.repeat(jnp.exp(steps), shape[axis_at] // blocks).reshape((-1,) + (1,) * (len(shape) - 1 - axis_at))
    return gain


def scatter_about(own_key, dims, scale, bound, shards=(), held_as=jnp.bfloat16):
    loudness = block_levels(own_key, dims, shards, -0.22, 0.18) if shards else 1.0
    values = jax.random.normal(own_key, dims, jnp.float32) * scale * loudness
    return jnp.minimum(jnp.maximum(values, -bound), bound).astype(held_as)


def setup_inputs(seed: int = 0) -> dict:
    keys = jax.random.split(jax.random.key(seed), 10)
    return {
        "features": scatter_about(keys[0], (NODES, F), 1.0, 6.0, ((0, 128),)),
        "walk_counts": plant(jax.random.randint(keys[1], (N_ROW, N_COL, SLOTS, TILE, TILE), 0, 16), jax.random.fold_in(keys[1], 1), 0, 15).astype(jnp.int32),
        "tile_rows": plant(jax.random.randint(keys[2], (N_ROW, N_COL, SLOTS), 0, BAND_BLK), jax.random.fold_in(keys[2], 1), 0, BAND_BLK - 1).astype(jnp.int32),
        "tile_cols": plant(jax.random.randint(keys[3], (N_ROW, N_COL, SLOTS), 0, PANEL_BLK), jax.random.fold_in(keys[3], 1), 0, PANEL_BLK - 1).astype(jnp.int32),
        "live_tiles": draw_live_tiles(jax.random.fold_in(keys[9], 71), 0),
        "neigh_weight": scatter_about(keys[5], (F, F), F ** -0.5, 0.1875),
        "neigh_bias": scatter_about(keys[6], (F,), 0.5, 3.0, (), jnp.float32),
        "combine_weight": scatter_about(keys[7], (2 * F, F), (2 * F) ** -0.5, 0.125),
        "combine_bias": scatter_about(keys[8], (F,), 0.5, 3.0, (), jnp.float32),
    }


def reference(features, walk_counts, tile_rows, tile_cols, live_tiles, neigh_weight, neigh_bias, combine_weight, combine_bias):
    messages = jax.nn.relu(jnp.dot(features, neigh_weight, preferred_element_type=jnp.float32) + neigh_bias).astype(jnp.bfloat16)
    per_dev = NODE_DEV // TILE
    blocks = messages.reshape(NODES // TILE, TILE, F)
    slot_ids = jnp.arange(SLOTS, dtype=jnp.int32)

    def one_device(carry, index):
        pooled, degree = carry
        row_id = index // N_COL
        col_id = index % N_COL
        counts = walk_counts[row_id, col_id]
        live = slot_ids < live_tiles[row_id, col_id]
        kcol = tile_cols[row_id, col_id]
        source = (kcol // per_dev * N_COL + col_id) * per_dev + kcol % per_dev
        target = tile_rows[row_id, col_id]
        weights = jnp.where(live[:, None, None], counts, 0).astype(jnp.float32)
        terms = jnp.einsum('sij,sjf->sif', weights, blocks[source.astype(jnp.int32)].astype(jnp.float32))
        band = jnp.zeros((BAND_BLK, TILE, F), jnp.float32).at[target.astype(jnp.int32)].add(terms)
        band_degree = jnp.zeros((BAND_BLK, TILE), jnp.float32).at[target.astype(jnp.int32)].add(lax.optimization_barrier(jnp.sum(weights, axis=2)))
        pooled = pooled.at[row_id].add(band)
        degree = degree.at[row_id].add(band_degree)
        return ((pooled, degree), None)
    start = (jnp.zeros((N_ROW, BAND_BLK, TILE, F), jnp.float32), jnp.zeros((N_ROW, BAND_BLK, TILE), jnp.float32))
    (pooled, degree), unused = lax.scan(one_device, start, jnp.arange(N_ROW * N_COL, dtype=jnp.int32))
    neighbours = (pooled / (1.0 + degree)[..., None]).reshape(NODES, F).astype(jnp.bfloat16)
    joined = jnp.concatenate([features, neighbours], axis=1)
    hidden = jax.nn.relu(jnp.dot(joined, combine_weight, preferred_element_type=jnp.float32) + combine_bias)
    return hidden / jnp.sqrt(lax.optimization_barrier(jnp.mean(hidden * hidden, axis=1, keepdims=True)) + 1e-06)
```

```python
import jax
import jax.numpy as jnp
from jax import lax
from jax.experimental import pallas as pl
from jax.experimental.pallas import tpu as pltpu
from jax.sharding import Mesh, PartitionSpec as P

AXES = ("x_lo", "y", "z", "x_hi", "core")
SIZES = (2, 4, 4, 2, 2)
CHUNKS = 4
GROUP = 8


def shift(x, axis, step):
    n = lax.axis_size(axis)
    return lax.ppermute(x, axis, [(i, (i + step) % n) for i in range(n)])


def swap_low(x):
    return lax.ppermute(x, "z", [(i, i ^ 1) for i in range(4)])


def swap_far(x):
    return lax.ppermute(x, "z", [(i, 3 - i) for i in range(4)])


def gather_pieces(own):
    def along_y(piece):
        left = shift(piece, "y", 1)
        right = shift(piece, "y", -1)
        far0 = shift(left[0], "y", 1)
        far1 = shift(right[1], "y", -1)
        return [piece, right, far0, far1, left]

    other = shift(own, "x_lo", 1)
    return along_y(own) + along_y(other)


def tile_kernel(
    src_ref,
    dst_ref,
    live_ref,
    c_own,
    c_other,
    p0,
    p1,
    p2a,
    p2b,
    p3,
    q0,
    q1,
    q2a,
    q2b,
    q3,
    send_a,
    keep_a,
    send_b,
    keep_b,
    panel,
    acc,
    sems,
):
    plan = []
    for dx, group in enumerate(((p0, p1, p2a, p2b, p3), (q0, q1, q2a, q2b, q3))):
        base = dx * 32
        plan += [
            (group[0], base, 8),
            (group[1], base + 8, 8),
            (group[2], base + 16, 4),
            (group[3], base + 20, 4),
            (group[4], base + 24, 8),
        ]
    copies = []
    for n, (ref, at, size) in enumerate(plan):
        copies.append(pltpu.make_async_copy(ref, panel.at[pl.ds(at, size)], sems.at[n]))
        copies[-1].start()

    @pl.loop(0, 64)
    def _(i):
        acc[i] = jnp.zeros(acc.shape[1:], jnp.float32)

    for copy in copies:
        copy.wait()

    slots = c_own.shape[0]
    for q, counts in enumerate((c_own, c_other)):

        def body(g, carry, q=q, counts=counts):
            terms = []
            for i in range(GROUP):
                s = g * GROUP + i
                terms.append(
                    jnp.dot(
                        counts[s],
                        panel[src_ref[q * slots + s]],
                        preferred_element_type=jnp.float32,
                    )
                )
            for i in range(GROUP):
                at = dst_ref[q * slots + g * GROUP + i]
                acc[at] = acc[at] + terms[i]
            return carry

        lax.fori_loop(0, (live_ref[q] + GROUP - 1) // GROUP, body, 0)

    for first, out in ((0, send_a), (16, keep_a), (32, send_b), (48, keep_b)):

        @pl.loop(0, 16)
        def _(i, first=first, out=out):
            out[i] = acc[first + i].astype(out.dtype)


def tile_sums(src, dst, live, c_own, c_other, pieces):
    tile, w = pieces[0].shape[-2:]
    flat = [p.reshape(-1, tile, w) for p in pieces]
    any_spec = pl.BlockSpec(memory_space=pl.ANY)
    vmem = pl.BlockSpec(memory_space=pltpu.VMEM)
    smem = pl.BlockSpec(memory_space=pltpu.SMEM)
    slots = c_own.shape[0]
    out = lambda dt: jax.ShapeDtypeStruct((16, tile, w), dt)
    return pl.pallas_call(
        tile_kernel,
        out_shape=(out(jnp.bfloat16), out(jnp.float32), out(jnp.bfloat16), out(jnp.float32)),
        in_specs=[smem] * 3 + [vmem] * 2 + [any_spec] * len(flat),
        out_specs=(vmem,) * 4,
        scratch_shapes=[
            pltpu.VMEM((64, tile, w), jnp.bfloat16),
            pltpu.VMEM((64, tile, w), jnp.float32),
            pltpu.SemaphoreType.DMA((10,)),
        ],
        compiler_params=pltpu.CompilerParams(vmem_limit_bytes=32 * 1024 * 1024),
        cost_estimate=pl.CostEstimate(
            flops=2 * 2 * slots * tile * tile * w * 4,
            bytes_accessed=64 * tile * w * 8,
            transcendentals=0,
        ),
    )(src, dst, live, c_own, c_other, *flat)


def scatter_sum(send_a, keep_a, send_b, keep_b):
    shape = (2, 8) + send_a.shape[1:]
    dt = send_a.dtype
    sum_a = swap_low(send_a).reshape(shape).astype(jnp.float32) + keep_a.reshape(shape)
    sum_b = swap_far(send_b).reshape(shape).astype(jnp.float32) + keep_b.reshape(shape)
    got_a = swap_far(sum_a[0].astype(dt))
    got_b = swap_low(sum_b[0].astype(dt))
    end_a = sum_a[1] + got_a.astype(jnp.float32)
    end_b = sum_b[1] + got_b.astype(jnp.float32)
    both = jnp.stack([end_a, end_b]).reshape((2, 2, 4) + send_a.shape[1:])
    got = shift(both[:, 0].astype(dt), "x_hi", 1)
    return both[:, 1] + got.astype(jnp.float32)


def local(
    features,
    walk_counts,
    tile_rows,
    tile_cols,
    live_tiles,
    neigh_weight,
    neigh_bias,
    combine_weight,
    combine_bias,
):
    rows_dev, width = features.shape
    tile = walk_counts.shape[3]
    slots = walk_counts.shape[2]
    half = width // 2
    cw = half // CHUNKS
    x_lo, y, z, x_hi, core = (lax.axis_index(a) for a in AXES)

    messages = jax.nn.relu(
        jnp.dot(features, neigh_weight, preferred_element_type=jnp.float32) + neigh_bias
    ).astype(jnp.bfloat16)
    mine = lax.dynamic_slice_in_dim(messages, core * half, half, 1)
    theirs = shift(lax.dynamic_slice_in_dim(messages, (1 - core) * half, half, 1), "core", 1)

    live = live_tiles[0, 0]
    used = jnp.arange(slots, dtype=jnp.int32) < live
    c_own = jnp.where(used[:, None, None], walk_counts[0, 0], 0).astype(jnp.bfloat16)
    meta = jnp.stack(
        [
            jnp.where(used, tile_rows[0, 0], 0),
            jnp.where(used, tile_cols[0, 0], 0),
            jnp.full((slots,), live, jnp.int32),
        ]
    )
    c_other = shift(c_own, "core", 1)
    metas = jnp.stack([meta, shift(meta, "core", 1)])
    k = metas[:, 1]
    src = (
        ((k // 16) ^ x_lo) * 32
        + (((k // 4) % 4 - y) % 4) * 8
        + jnp.arange(2, dtype=jnp.int32)[:, None] * 4
        + k % 4
    ).reshape(-1)

    def place(b):
        dest = b // 16
        theirs_b = ((b // 4) % 2) ^ core
        near = z ^ 1
        far = 3 - z
        slot_a = jnp.where(
            dest == z, 3, jnp.where(dest == far, 2, jnp.where(dest == near, 1, 0))
        )
        slot_b = jnp.where(
            dest == z, 3, jnp.where(dest == near, 2, jnp.where(dest == far, 1, 0))
        )
        slot = jnp.where(theirs_b == 1, slot_b, slot_a)
        x_slot = 1 - (((b // 8) % 2) ^ x_hi)
        return ((theirs_b * 4 + slot) * 2 + x_slot) * 4 + b % 4

    dst = place(metas[:, 0])
    lives = metas[:, 2, 0]

    row_sums = jnp.sum(c_own.astype(jnp.float32), axis=2)
    row_sums = jnp.concatenate([row_sums, shift(row_sums, "core", 1)])
    dst = dst.reshape(-1)
    onehot = (jnp.arange(64, dtype=jnp.int32)[:, None] == dst[None, :]).astype(jnp.float32)
    deg = jnp.dot(onehot, row_sums, precision=lax.Precision.HIGHEST)
    scale = 1.0 / (1.0 + scatter_sum(*jnp.split(deg, 4)))

    hidden = (
        jnp.dot(features, combine_weight[:width], preferred_element_type=jnp.float32)
        + combine_bias
    )
    w_own = lax.dynamic_slice_in_dim(combine_weight, width + core * half, half, 0)
    w_other = lax.dynamic_slice_in_dim(combine_weight, width + (1 - core) * half, half, 0)
    blocks = rows_dev // tile
    for j in range(CHUNKS):
        cols = slice(j * cw, (j + 1) * cw)
        own = jnp.stack(
            [mine[:, cols].reshape(blocks, tile, cw), theirs[:, cols].reshape(blocks, tile, cw)]
        )
        pieces = gather_pieces(own)
        pooled = scatter_sum(*tile_sums(src, dst, lives, c_own, c_other, pieces))
        near = (pooled * scale[..., None]).astype(jnp.bfloat16).reshape(2, rows_dev, cw)
        got = shift(near[1], "core", 1)
        hidden = hidden + jnp.dot(near[0], w_own[cols], preferred_element_type=jnp.float32)
        hidden = hidden + jnp.dot(got, w_other[cols], preferred_element_type=jnp.float32)
    hidden = jax.nn.relu(hidden)
    return hidden / jnp.sqrt(jnp.mean(hidden * hidden, axis=1, keepdims=True) + 1e-06)


def solution(mesh):
    fine = Mesh(mesh.devices.reshape(SIZES), AXES)
    row = AXES[:2]
    col = AXES[2:]
    return jax.shard_map(
        local,
        mesh=fine,
        in_specs=(
            P(AXES, None),
            P(row, col, None, None, None),
            P(row, col, None),
            P(row, col, None),
            P(row, col),
            P(),
            P(),
            P(),
            P(),
        ),
        out_specs=P(AXES, None),
        check_vma=False,
    )
```

```python
import jax
import jax.numpy as jnp
from jax import lax
from jax.experimental import pallas as pl
from jax.experimental.pallas import tpu as pltpu
from jax.sharding import Mesh, PartitionSpec as P

AXES = ("x_lo", "y", "z", "x_hi", "core")
SIZES = (2, 4, 4, 2, 2)
CHUNKS = 4
GROUP = 8


def swap(x, axis):
    return lax.ppermute(x, axis, [(0, 1), (1, 0)])


def step(x, axis, second):
    pairs = []
    for i in range(4):
        for c in range(2):
            to = i ^ 1 if c == second else 3 - i
            pairs.append((i * 2 + c, to * 2 + c))
    return lax.ppermute(x, (axis, "core"), pairs)


def after(x, *earlier):
    return lax.optimization_barrier((x, *earlier))[0]


def ring_slot(place, here, core):
    first = jnp.where(core == 0, here ^ 1, 3 - here)
    second = jnp.where(core == 0, 3 - here, here ^ 1)
    return jnp.where(
        place == here, 0, jnp.where(place == first, 1, jnp.where(place == second, 2, 3))
    )


def tile_kernel(src_ref, dst_ref, live_ref, c_own, c_other, pieces_ref, near, far, *refs):
    send, pass_on, stay, panel, acc, sems = refs[-6:]
    copies = [
        pltpu.make_async_copy(near, panel.at[pl.ds(0, 32)], sems.at[0]),
        pltpu.make_async_copy(far, panel.at[pl.ds(32, 32)], sems.at[1]),
    ]
    for copy in copies:
        copy.start()

    @pl.loop(0, 64)
    def _(i):
        acc[i] = jnp.zeros(acc.shape[1:], jnp.float32)

    for copy in copies:
        copy.wait()

    slots, tile = c_own.shape[:2]
    for q, counts in enumerate((c_own, c_other)):

        def body(g, carry, q=q, counts=counts):
            terms = []
            for i in range(GROUP):
                s = g * GROUP + i
                terms.append(
                    jnp.dot(
                        counts[s],
                        panel[src_ref[q * slots + s]],
                        preferred_element_type=jnp.float32,
                    )
                )
            for i in range(GROUP):
                at = dst_ref[q * slots + g * GROUP + i]
                acc[at] = acc[at] + terms[i]
            return carry

        lax.fori_loop(0, (live_ref[q] + GROUP - 1) // GROUP, body, 0)

    size = stay.shape[0] // 2
    extra = size - 8 * tile
    for part in range(8):
        out = (send, send, send, send, pass_on, pass_on, stay, stay)[part]
        base = (part if part < 4 else part % 2) * size

        @pl.loop(0, 8)
        def _(i, part=part, out=out, base=base):
            at = pl.multiple_of(base + i * tile, 16)
            out[pl.ds(at, tile)] = acc[part * 8 + i].astype(out.dtype)

        if extra:
            out[pl.ds(base + 8 * tile, extra)] = pieces_ref[pl.ds(part * extra, extra)].astype(
                out.dtype
            )


def tile_sums(src, dst, live, c_own, c_other, pieces, with_pieces, near, far, earlier):
    tile, w = near.shape[-2:]
    any_spec = pl.BlockSpec(memory_space=pl.ANY)
    vmem = pl.BlockSpec(memory_space=pltpu.VMEM)
    smem = pl.BlockSpec(memory_space=pltpu.SMEM)
    slots = c_own.shape[0]
    size = 8 * tile + (pieces.shape[0] // 8 if with_pieces else 0)
    return pl.pallas_call(
        tile_kernel,
        out_shape=(
            jax.ShapeDtypeStruct((4 * size, w), jnp.bfloat16),
            jax.ShapeDtypeStruct((2 * size, w), jnp.float32),
            jax.ShapeDtypeStruct((2 * size, w), jnp.float32),
        ),
        in_specs=[smem] * 3 + [vmem] * 3 + [any_spec] * (2 + len(earlier)),
        out_specs=(vmem,) * 3,
        scratch_shapes=[
            pltpu.VMEM((64, tile, w), jnp.bfloat16),
            pltpu.VMEM((64, tile, w), jnp.float32),
            pltpu.SemaphoreType.DMA((2,)),
        ],
        compiler_params=pltpu.CompilerParams(vmem_limit_bytes=32 * 1024 * 1024),
        cost_estimate=pl.CostEstimate(
            flops=2 * 2 * slots * tile * tile * w * 4,
            bytes_accessed=64 * tile * w * 8,
            transcendentals=0,
        ),
    )(src, dst, live, c_own, c_other, pieces, near, far, *earlier)


def local(
    features,
    walk_counts,
    tile_rows,
    tile_cols,
    live_tiles,
    neigh_weight,
    neigh_bias,
    combine_weight,
    combine_bias,
):
    rows_dev, width = features.shape
    tile = walk_counts.shape[3]
    slots = walk_counts.shape[2]
    half = width // 2
    cw = half // CHUNKS
    blocks = rows_dev // tile
    x_lo, y, z, x_hi, core = (lax.axis_index(a) for a in AXES)

    def transform(which):
        weight = lax.dynamic_slice_in_dim(neigh_weight, which * half, half, 1)
        bias = lax.dynamic_slice_in_dim(neigh_bias, which * half, half, 0)
        out = jnp.dot(features, weight, preferred_element_type=jnp.float32) + bias
        return jax.nn.relu(out).astype(jnp.bfloat16)

    theirs = swap(transform(1 - core), "core")
    mine = transform(core)

    def own_chunk(j):
        cols = slice(j * cw, (j + 1) * cw)
        return jnp.concatenate(
            [mine[:, cols].reshape(blocks, tile, cw), theirs[:, cols].reshape(blocks, tile, cw)]
        )

    live = live_tiles[0, 0]
    used = jnp.arange(slots, dtype=jnp.int32) < live
    c_own = jnp.where(used[:, None, None], walk_counts[0, 0], 0).astype(jnp.bfloat16)
    rows_own = jnp.where(used, tile_rows[0, 0], 0)
    meta = jnp.stack(
        [rows_own, jnp.where(used, tile_cols[0, 0], 0), jnp.full((slots,), live, jnp.int32)]
    )
    c_other = swap(after(c_own, theirs), "core")
    metas = jnp.stack([meta, swap(meta, "core")])
    k = metas[:, 1]
    src = (
        (ring_slot((k // 4) % 4, y, core) * 2 + ((k // 16) ^ x_lo)) * 8
        + jnp.arange(2, dtype=jnp.int32)[:, None] * 4
        + k % 4
    ).reshape(-1)
    b = metas[:, 0]
    ring = ring_slot(b // 16, z, core)
    ring = jnp.where(ring == 0, 3, jnp.where(ring == 3, 0, ring))
    dst = (
        ((ring * 2 + 1 - (((b // 8) % 2) ^ x_hi)) * 2)
        + (((b // 4) % 2) ^ core)
    ) * 4 + b % 4
    dst = dst.reshape(-1)
    lives = metas[:, 2, 0]

    row_sums = jnp.concatenate(
        [jnp.sum(c_own.astype(jnp.float32), axis=2), jnp.sum(c_other.astype(jnp.float32), axis=2)]
    )
    onehot = (jnp.arange(64, dtype=jnp.int32)[:, None] == dst[None, :]).astype(jnp.float32)
    deg = jnp.dot(onehot, row_sums, precision=lax.Precision.HIGHEST).astype(jnp.int32)
    parts = (deg[:, None, :] >> (5 * jnp.arange(4, dtype=jnp.int32))[None, :, None]) & 31
    parts = parts.astype(jnp.bfloat16).reshape(256, tile)

    hidden = (
        jnp.dot(features, combine_weight[:width], preferred_element_type=jnp.float32)
        + combine_bias
    )
    w_own = lax.dynamic_slice_in_dim(combine_weight, width + core * half, half, 0)
    w_other = lax.dynamic_slice_in_dim(combine_weight, width + (1 - core) * half, half, 0)

    own = [own_chunk(j) for j in range(CHUNKS)]
    first = swap(own[0], "x_lo")
    rest = swap(jnp.stack(own[1:]), "x_lo")
    partner = [first] + [rest[j] for j in range(CHUNKS - 1)]

    f32, bf16 = jnp.float32, jnp.bfloat16
    near_all, part_all, pass_all, zb_all, swap_all = [], [], [], [], []
    scale = None
    for j in range(CHUNKS):
        pair = jnp.concatenate([own[j], partner[j]])
        if j >= 2:
            pair = after(pair, near_all[j - 1], part_all[j - 2][0])
        elif j == 1:
            pair = after(pair, near_all[0])
        near = jnp.concatenate([pair, step(pair, "y", 0)])
        near_all.append(near)
        far = step(near, "y", 1)
        earlier = ()
        if j >= 2:
            earlier += (pass_all[j - 2],)
        if j >= 3:
            earlier += (zb_all[j - 3],)
        send, pass_on, stay = tile_sums(
            src, dst, lives, c_own, c_other, parts, j == 0, near, far, earlier
        )
        part_all.append((send, pass_on, stay))
        size = stay.shape[0] // 2
        got = step(send, "z", 0)
        passed = (got[: 2 * size].astype(f32) + pass_on).astype(bf16)
        pass_all.append(passed)
        stay = got[2 * size :].astype(f32) + stay
        if j == CHUNKS - 1:
            passed = after(passed, swap_all[j - 2])
        got = step(passed, "z", 1)
        zb_all.append(got)
        passed = (got[:size].astype(f32) + stay[:size]).astype(bf16)
        stay = got[size:].astype(f32) + stay[size:]
        if j == CHUNKS - 1:
            passed = after(passed, swap_all[j - 1])
        pooled = swap(passed, "x_hi").astype(f32) + stay
        if j == 0:
            deg = jnp.sum(
                pooled[8 * tile :].reshape(8, 4, tile)
                * jnp.array([1, 32, 1024, 32768], f32)[None, :, None],
                axis=1,
            )
            scale = 1.0 / (1.0 + deg)
            pooled = pooled[: 8 * tile]
        mean = (pooled.reshape(8, tile, cw) * scale[..., None]).astype(bf16)
        mean = mean.reshape(2, rows_dev, cw)
        got = swap(mean[1], "core")
        swap_all.append(got)
        cols = slice(j * cw, (j + 1) * cw)
        hidden = hidden + jnp.dot(mean[0], w_own[cols], preferred_element_type=f32)
        hidden = hidden + jnp.dot(got, w_other[cols], preferred_element_type=f32)
    hidden = jax.nn.relu(hidden)
    return hidden / jnp.sqrt(jnp.mean(hidden * hidden, axis=1, keepdims=True) + 1e-06)


def solution(mesh):
    fine = Mesh(mesh.devices.reshape(SIZES), AXES)
    row = AXES[:2]
    col = AXES[2:]
    return jax.shard_map(
        local,
        mesh=fine,
        in_specs=(
            P(AXES, None),
            P(row, col, None, None, None),
            P(row, col, None),
            P(row, col, None),
            P(row, col),
            P(),
            P(),
            P(),
            P(),
        ),
        out_specs=P(AXES, None),
        check_vma=False,
    )
```

```python
import jax
import jax.numpy as jnp
from jax import lax
from jax.experimental import pallas as pl
from jax.experimental.pallas import tpu as pltpu
from jax.sharding import Mesh, PartitionSpec as P

AXES = ("x_lo", "y", "z", "x_hi", "core")
SIZES = (2, 4, 4, 2, 2)
CHUNKS = 4
GROUP = 8


def swap(x, axis):
    return lax.ppermute(x, axis, [(0, 1), (1, 0)])


def step(x, axis, second):
    pairs = []
    for i in range(4):
        for c in range(2):
            to = i ^ 1 if c == second else 3 - i
            pairs.append((i * 2 + c, to * 2 + c))
    return lax.ppermute(x, (axis, "core"), pairs)


def after(x, *earlier):
    return lax.optimization_barrier((x, *earlier))[0]


def ring_slot(place, here, core):
    first = jnp.where(core == 0, here ^ 1, 3 - here)
    second = jnp.where(core == 0, 3 - here, here ^ 1)
    return jnp.where(
        place == here, 0, jnp.where(place == first, 1, jnp.where(place == second, 2, 3))
    )


def tile_kernel(src_ref, dst_ref, live_ref, c_own, c_other, pieces_ref, near, far, *refs):
    send, pass_on, stay, panel, acc, sems = refs[-6:]
    copies = [
        pltpu.make_async_copy(near, panel.at[pl.ds(0, 32)], sems.at[0]),
        pltpu.make_async_copy(far, panel.at[pl.ds(32, 32)], sems.at[1]),
    ]
    for copy in copies:
        copy.start()

    @pl.loop(0, 64)
    def _(i):
        acc[i] = jnp.zeros(acc.shape[1:], jnp.float32)

    for copy in copies:
        copy.wait()

    slots, tile = c_own.shape[:2]
    for q, counts in enumerate((c_own, c_other)):

        def body(g, carry, q=q, counts=counts):
            terms = []
            for i in range(GROUP):
                s = g * GROUP + i
                terms.append(
                    jnp.dot(
                        counts[s],
                        panel[src_ref[q * slots + s]],
                        preferred_element_type=jnp.float32,
                    )
                )
            for i in range(GROUP):
                at = dst_ref[q * slots + g * GROUP + i]
                acc[at] = acc[at] + terms[i]
            return carry

        lax.fori_loop(0, (live_ref[q] + GROUP - 1) // GROUP, body, 0)

    size = stay.shape[0] // 2
    extra = size - 8 * tile
    for part in range(8):
        out = (send, send, send, send, pass_on, pass_on, stay, stay)[part]
        base = (part if part < 4 else part % 2) * size

        @pl.loop(0, 8)
        def _(i, part=part, out=out, base=base):
            at = pl.multiple_of(base + i * tile, 16)
            out[pl.ds(at, tile)] = acc[part * 8 + i].astype(out.dtype)

        if extra:
            out[pl.ds(base + 8 * tile, extra)] = pieces_ref[pl.ds(part * extra, extra)].astype(
                out.dtype
            )


def tile_sums(src, dst, live, c_own, c_other, pieces, with_pieces, near, far, earlier):
    tile, w = near.shape[-2:]
    any_spec = pl.BlockSpec(memory_space=pl.ANY)
    vmem = pl.BlockSpec(memory_space=pltpu.VMEM)
    smem = pl.BlockSpec(memory_space=pltpu.SMEM)
    slots = c_own.shape[0]
    size = 8 * tile + (pieces.shape[0] // 8 if with_pieces else 0)
    return pl.pallas_call(
        tile_kernel,
        out_shape=(
            jax.ShapeDtypeStruct((4 * size, w), jnp.bfloat16),
            jax.ShapeDtypeStruct((2 * size, w), jnp.float32),
            jax.ShapeDtypeStruct((2 * size, w), jnp.float32),
        ),
        in_specs=[smem] * 3 + [vmem] * 3 + [any_spec] * (2 + len(earlier)),
        out_specs=(vmem,) * 3,
        scratch_shapes=[
            pltpu.VMEM((64, tile, w), jnp.bfloat16),
            pltpu.VMEM((64, tile, w), jnp.float32),
            pltpu.SemaphoreType.DMA((2,)),
        ],
        compiler_params=pltpu.CompilerParams(vmem_limit_bytes=32 * 1024 * 1024),
        cost_estimate=pl.CostEstimate(
            flops=2 * 2 * slots * tile * tile * w * 4,
            bytes_accessed=64 * tile * w * 8,
            transcendentals=0,
        ),
    )(src, dst, live, c_own, c_other, pieces, near, far, *earlier)


def local(
    features,
    walk_counts,
    tile_rows,
    tile_cols,
    live_tiles,
    neigh_weight,
    neigh_bias,
    combine_weight,
    combine_bias,
):
    rows_dev, width = features.shape
    tile = walk_counts.shape[3]
    slots = walk_counts.shape[2]
    half = width // 2
    cw = half // CHUNKS
    blocks = rows_dev // tile
    x_lo, y, z, x_hi, core = (lax.axis_index(a) for a in AXES)

    def transform(features, which, first, size):
        weight = lax.dynamic_slice_in_dim(neigh_weight, which * half + first, size, 1)
        bias = jnp.where(
            which == 0,
            neigh_bias[first : first + size],
            neigh_bias[half + first : half + first + size],
        )
        out = jnp.dot(features, weight, preferred_element_type=jnp.float32) + bias
        return jax.nn.relu(out).astype(jnp.bfloat16)

    def as_blocks(a, b):
        return jnp.concatenate([a.reshape(blocks, tile, cw), b.reshape(blocks, tile, cw)])

    theirs0 = transform(features, 1 - core, 0, cw)
    later = after(features, theirs0)
    mine0 = transform(later, core, 0, cw)
    own = [as_blocks(mine0, swap(theirs0, "core"))]
    later = after(later, mine0)
    theirs = swap(transform(later, 1 - core, cw, half - cw), "core")
    mine = transform(later, core, cw, half - cw)
    for j in range(CHUNKS - 1):
        cols = slice(j * cw, (j + 1) * cw)
        own.append(as_blocks(mine[:, cols], theirs[:, cols]))
    first = swap(own[0], "x_lo")

    live = live_tiles[0, 0]
    used = jnp.arange(slots, dtype=jnp.int32) < live
    c_own = jnp.where(used[:, None, None], walk_counts[0, 0], 0).astype(jnp.bfloat16)
    rows_own = jnp.where(used, tile_rows[0, 0], 0)
    meta = jnp.stack(
        [rows_own, jnp.where(used, tile_cols[0, 0], 0), jnp.full((slots,), live, jnp.int32)]
    )
    c_other = swap(after(c_own, theirs, own[0]), "core")
    metas = jnp.stack([meta, swap(meta, "core")])
    k = metas[:, 1]
    src = (
        (ring_slot((k // 4) % 4, y, core) * 2 + ((k // 16) ^ x_lo)) * 8
        + jnp.arange(2, dtype=jnp.int32)[:, None] * 4
        + k % 4
    ).reshape(-1)
    b = metas[:, 0]
    ring = ring_slot(b // 16, z, core)
    ring = jnp.where(ring == 0, 3, jnp.where(ring == 3, 0, ring))
    dst = (
        ((ring * 2 + 1 - (((b // 8) % 2) ^ x_hi)) * 2)
        + (((b // 4) % 2) ^ core)
    ) * 4 + b % 4
    dst = dst.reshape(-1)
    lives = metas[:, 2, 0]

    row_sums = jnp.concatenate(
        [jnp.sum(c_own.astype(jnp.float32), axis=2), jnp.sum(c_other.astype(jnp.float32), axis=2)]
    )
    onehot = (jnp.arange(64, dtype=jnp.int32)[:, None] == dst[None, :]).astype(jnp.float32)
    deg = jnp.dot(onehot, row_sums, precision=lax.Precision.HIGHEST).astype(jnp.int32)
    parts = (deg[:, None, :] >> (5 * jnp.arange(4, dtype=jnp.int32))[None, :, None]) & 31
    parts = parts.astype(jnp.bfloat16).reshape(256, tile)

    hidden = (
        jnp.dot(features, combine_weight[:width], preferred_element_type=jnp.float32)
        + combine_bias
    )
    w_own = lax.dynamic_slice_in_dim(combine_weight, width + core * half, half, 0)
    w_other = lax.dynamic_slice_in_dim(combine_weight, width + (1 - core) * half, half, 0)

    second = swap(after(own[1], first), "x_lo")
    rest = swap(after(jnp.stack(own[2:]), second), "x_lo")
    partner = [first, second] + [rest[j] for j in range(CHUNKS - 2)]

    f32, bf16 = jnp.float32, jnp.bfloat16
    near_all, part_all, pass_all, zb_all, hidden_all = [], [], [], [], []
    scale = None
    for j in range(CHUNKS):
        pair = jnp.concatenate([own[j], partner[j]])
        if j >= 2:
            pair = after(pair, near_all[j - 1], part_all[j - 2][0])
        elif j == 1:
            pair = after(pair, near_all[0])
        near = jnp.concatenate([pair, step(pair, "y", 0)])
        near_all.append(near)
        far = step(near, "y", 1)
        earlier = ()
        if j >= 2:
            earlier += (pass_all[j - 2], zb_all[j - 2])
        send, pass_on, stay = tile_sums(
            src, dst, lives, c_own, c_other, parts, j == 0, near, far, earlier
        )
        part_all.append((send, pass_on, stay))
        if j >= 1:
            send = after(send, pass_all[j - 1])
        size = stay.shape[0] // 2
        got = step(send, "z", 0)
        passed = (got[: 2 * size].astype(f32) + pass_on).astype(bf16)
        pass_all.append(passed)
        stay = got[2 * size :].astype(f32) + stay
        got = step(passed, "z", 1)
        zb_all.append(got)
        passed = (got[:size].astype(f32) + stay[:size]).astype(bf16)
        stay = got[size:].astype(f32) + stay[size:]
        if j == CHUNKS - 1:
            passed = after(passed, hidden_all[j - 2])
        pooled = swap(passed, "x_hi").astype(f32) + stay
        if j == 0:
            deg = jnp.sum(
                pooled[8 * tile :].reshape(8, 4, tile)
                * jnp.array([1, 32, 1024, 32768], f32)[None, :, None],
                axis=1,
            )
            scale = 1.0 / (1.0 + deg)
            pooled = pooled[: 8 * tile]
        factor = after(scale, passed)[..., None]
        mean = (pooled.reshape(8, tile, cw) * factor).astype(bf16)
        mean = mean.reshape(2, rows_dev, cw)
        got = swap(mean[1], "core")
        cols = slice(j * cw, (j + 1) * cw)
        hidden = hidden + jnp.dot(mean[0], w_own[cols], preferred_element_type=f32)
        hidden = hidden + jnp.dot(got, w_other[cols], preferred_element_type=f32)
        hidden_all.append(hidden)
    hidden = jax.nn.relu(hidden)
    return hidden / jnp.sqrt(jnp.mean(hidden * hidden, axis=1, keepdims=True) + 1e-06)


def solution(mesh):
    fine = Mesh(mesh.devices.reshape(SIZES), AXES)
    row = AXES[:2]
    col = AXES[2:]
    return jax.shard_map(
        local,
        mesh=fine,
        in_specs=(
            P(AXES, None),
            P(row, col, None, None, None),
            P(row, col, None),
            P(row, col, None),
            P(row, col),
            P(),
            P(),
            P(),
            P(),
        ),
        out_specs=P(AXES, None),
        check_vma=False,
    )
```

```python
import functools

import jax
import jax.numpy as jnp
from jax import lax
from jax.experimental import pallas as pl
from jax.experimental.pallas import tpu as pltpu
from jax.sharding import Mesh, PartitionSpec as P

AXES = ("x_lo", "y", "z", "x_hi", "core")
SIZES = (2, 4, 4, 2, 2)
CHUNKS = 4
GROUP = 8


def swap(x, axis, name):
    with jax.named_scope(name):
        return lax.ppermute(x, axis, [(0, 1), (1, 0)])


def step(x, axis, second, name):
    pairs = []
    for i in range(4):
        for c in range(2):
            to = i ^ 1 if c == second else 3 - i
            pairs.append((i * 2 + c, to * 2 + c))
    with jax.named_scope(name):
        return lax.ppermute(x, (axis, "core"), pairs)


def after(x, *earlier):
    return lax.optimization_barrier((x, *earlier))[0]


def ring_slot(place, here, core):
    first = jnp.where(core == 0, here ^ 1, 3 - here)
    second = jnp.where(core == 0, 3 - here, here ^ 1)
    return jnp.where(
        place == here, 0, jnp.where(place == first, 1, jnp.where(place == second, 2, 3))
    )


def tile_kernel(src_ref, dst_ref, live_ref, c_own, c_other, pieces_ref, near, far, *refs):
    send, pass_on, stay, panel, acc, sems = refs[-6:]
    copies = [
        pltpu.make_async_copy(near, panel.at[pl.ds(0, 32)], sems.at[0]),
        pltpu.make_async_copy(far, panel.at[pl.ds(32, 32)], sems.at[1]),
    ]
    for copy in copies:
        copy.start()

    @pl.loop(0, 64)
    def _(i):
        acc[i] = jnp.zeros(acc.shape[1:], jnp.float32)

    for copy in copies:
        copy.wait()

    slots, tile = c_own.shape[:2]
    for q, counts in enumerate((c_own, c_other)):

        def body(g, carry, q=q, counts=counts):
            terms = []
            for i in range(GROUP):
                s = g * GROUP + i
                terms.append(
                    jnp.dot(
                        counts[s],
                        panel[src_ref[q * slots + s]],
                        preferred_element_type=jnp.float32,
                    )
                )
            for i in range(GROUP):
                at = dst_ref[q * slots + g * GROUP + i]
                acc[at] = acc[at] + terms[i]
            return carry

        lax.fori_loop(0, (live_ref[q] + GROUP - 1) // GROUP, body, 0)

    size = stay.shape[0] // 2
    extra = size - 8 * tile
    for part in range(8):
        out = (send, send, send, send, pass_on, pass_on, stay, stay)[part]
        base = (part if part < 4 else part % 2) * size

        @pl.loop(0, 8)
        def _(i, part=part, out=out, base=base):
            at = pl.multiple_of(base + i * tile, 16)
            out[pl.ds(at, tile)] = acc[part * 8 + i].astype(out.dtype)

        if extra:
            out[pl.ds(base + 8 * tile, extra)] = pieces_ref[pl.ds(part * extra, extra)].astype(
                out.dtype
            )


def tile_sums(src, dst, live, c_own, c_other, pieces, with_pieces, near, far, earlier):
    tile, w = near.shape[-2:]
    any_spec = pl.BlockSpec(memory_space=pl.ANY)
    vmem = pl.BlockSpec(memory_space=pltpu.VMEM)
    smem = pl.BlockSpec(memory_space=pltpu.SMEM)
    slots = c_own.shape[0]
    size = 8 * tile + (pieces.shape[0] // 8 if with_pieces else 0)
    return pl.pallas_call(
        tile_kernel,
        out_shape=(
            jax.ShapeDtypeStruct((4 * size, w), jnp.bfloat16),
            jax.ShapeDtypeStruct((2 * size, w), jnp.float32),
            jax.ShapeDtypeStruct((2 * size, w), jnp.float32),
        ),
        in_specs=[smem] * 3 + [vmem] * 3 + [any_spec] * (2 + len(earlier)),
        out_specs=(vmem,) * 3,
        scratch_shapes=[
            pltpu.VMEM((64, tile, w), jnp.bfloat16),
            pltpu.VMEM((64, tile, w), jnp.float32),
            pltpu.SemaphoreType.DMA((2,)),
        ],
        compiler_params=pltpu.CompilerParams(vmem_limit_bytes=32 * 1024 * 1024),
        cost_estimate=pl.CostEstimate(
            flops=2 * 2 * slots * tile * tile * w * 4,
            bytes_accessed=64 * tile * w * 8,
            transcendentals=0,
        ),
    )(src, dst, live, c_own, c_other, pieces, near, far, *earlier)


def message_kernel(first, core_ref, x, weight, bias, theirs, mine, held, sems):
    core = core_ref[0]
    chunks, blocks, tile, w = mine.shape
    half = weight.shape[1] // 2
    size = chunks * w
    starts = [
        pl.multiple_of((1 - core) * half + first, 128),
        pl.multiple_of(core * half + first, 128),
    ]
    copies = [
        pltpu.make_async_copy(weight.at[:, pl.ds(starts[i], size)], held.at[i], sems.at[i])
        for i in range(2)
    ]
    for copy in copies:
        copy.start()
    for i, out in enumerate((theirs, mine)):
        copies[i].wait()
        row = bias[:, pl.ds(starts[i], size)]
        for j in range(chunks):
            cols = slice(j * w, (j + 1) * w)
            total = jnp.dot(x[...], held[i, :, cols], preferred_element_type=jnp.float32)
            total = jnp.maximum(total + row[:, cols], 0.0)
            out[j] = total.astype(out.dtype).reshape(blocks, tile, w)


def transform(core, features, weight, bias, first, chunks, tile, w):
    vmem = pl.BlockSpec(memory_space=pltpu.VMEM)
    out = jax.ShapeDtypeStruct((chunks, features.shape[0] // tile, tile, w), jnp.bfloat16)
    return pl.pallas_call(
        functools.partial(message_kernel, first),
        out_shape=(out, out),
        in_specs=[
            pl.BlockSpec(memory_space=pltpu.SMEM),
            vmem,
            pl.BlockSpec(memory_space=pl.ANY),
            vmem,
        ],
        out_specs=(vmem, vmem),
        scratch_shapes=[
            pltpu.VMEM((2, features.shape[1], chunks * w), jnp.bfloat16),
            pltpu.SemaphoreType.DMA((2,)),
        ],
        compiler_params=pltpu.CompilerParams(vmem_limit_bytes=32 * 1024 * 1024),
        cost_estimate=pl.CostEstimate(
            flops=4 * features.size * chunks * w,
            bytes_accessed=2 * features.size + 4 * features.shape[1] * chunks * w,
            transcendentals=0,
        ),
    )(core.astype(jnp.int32).reshape(1), features, weight, bias.reshape(1, -1))


def local(
    features,
    walk_counts,
    tile_rows,
    tile_cols,
    live_tiles,
    neigh_weight,
    neigh_bias,
    combine_weight,
    combine_bias,
):
    rows_dev, width = features.shape
    tile = walk_counts.shape[3]
    slots = walk_counts.shape[2]
    half = width // 2
    cw = half // CHUNKS
    blocks = rows_dev // tile
    x_lo, y, z, x_hi, core = (lax.axis_index(a) for a in AXES)

    make = functools.partial(transform, core)
    theirs, mine = make(features, neigh_weight, neigh_bias, 0, 1, tile, cw)
    own = [jnp.concatenate([mine[0], swap(theirs[0], "core", "other_core_0")])]
    first = swap(own[0], "x_lo", "gather_x_0")
    theirs, mine = make(
        after(features, theirs), neigh_weight, neigh_bias, cw, CHUNKS - 1, tile, cw
    )
    theirs = swap(after(theirs, own[0]), "core", "other_core_rest")
    own += [jnp.concatenate([mine[j], theirs[j]]) for j in range(CHUNKS - 1)]

    live = live_tiles[0, 0]
    used = jnp.arange(slots, dtype=jnp.int32) < live
    counts = after(walk_counts, own[0])[0, 0]
    c_own = jnp.where(used[:, None, None], counts, 0).astype(jnp.bfloat16)
    pair0 = jnp.concatenate([own[0], after(first, c_own)])
    rows_own = jnp.where(used, tile_rows[0, 0], 0)
    meta = jnp.stack(
        [rows_own, jnp.where(used, tile_cols[0, 0], 0), jnp.full((slots,), live, jnp.int32)]
    )
    c_other = swap(after(c_own, theirs), "core", "other_tiles")
    metas = jnp.stack([meta, swap(after(meta, own[0]), "core", "other_meta")])
    k = metas[:, 1]
    src = (
        (ring_slot((k // 4) % 4, y, core) * 2 + ((k // 16) ^ x_lo)) * 8
        + jnp.arange(2, dtype=jnp.int32)[:, None] * 4
        + k % 4
    ).reshape(-1)
    b = metas[:, 0]
    ring = ring_slot(b // 16, z, core)
    ring = jnp.where(ring == 0, 3, jnp.where(ring == 3, 0, ring))
    dst = (
        ((ring * 2 + 1 - (((b // 8) % 2) ^ x_hi)) * 2)
        + (((b // 4) % 2) ^ core)
    ) * 4 + b % 4
    dst = dst.reshape(-1)
    lives = metas[:, 2, 0]

    row_sums = jnp.concatenate(
        [jnp.sum(c_own.astype(jnp.float32), axis=2), jnp.sum(c_other.astype(jnp.float32), axis=2)]
    )
    onehot = (jnp.arange(64, dtype=jnp.int32)[:, None] == dst[None, :]).astype(jnp.float32)
    deg = jnp.dot(onehot, row_sums, precision=lax.Precision.HIGHEST).astype(jnp.int32)
    parts = (deg[:, None, :] >> (5 * jnp.arange(4, dtype=jnp.int32))[None, :, None]) & 31
    parts = parts.astype(jnp.bfloat16).reshape(256, tile)

    hidden = (
        jnp.dot(features, combine_weight[:width], preferred_element_type=jnp.float32)
        + combine_bias
    )
    w_own = lax.dynamic_slice_in_dim(combine_weight, width + core * half, half, 0)
    w_other = lax.dynamic_slice_in_dim(combine_weight, width + (1 - core) * half, half, 0)

    second = swap(after(own[1], first), "x_lo", "gather_x_1")
    rest = swap(after(jnp.stack(own[2:]), second), "x_lo", "gather_x_rest")
    partner = [first, second] + [rest[j] for j in range(CHUNKS - 2)]

    f32, bf16 = jnp.float32, jnp.bfloat16
    near_all, far_all, part_all, pass_all, zb_all, hidden_all = [], [], [], [], [], []
    scale = None

    def gather(j):
        pair = jnp.concatenate([own[j], partner[j]]) if j else pair0
        if j >= 2:
            pair = after(pair, near_all[j - 1], part_all[j - 2][0])
        elif j == 1:
            pair = after(pair, near_all[0])
        near_all.append(jnp.concatenate([pair, step(pair, "y", 0, f"gather_near_{j}")]))
        far_all.append(step(near_all[j], "y", 1, f"gather_far_{j}"))

    def tiles(j):
        earlier = (rest,) if j == 0 else ()
        if j + 1 < CHUNKS:
            earlier += (near_all[j + 1],)
        if j >= 2:
            earlier += (pass_all[j - 2],)
        if j >= 3:
            earlier += (zb_all[j - 3],)
        with jax.named_scope(f"tiles_{j}"):
            part_all.append(
                tile_sums(
                    src, dst, lives, c_own, c_other, parts, j == 0, near_all[j], far_all[j], earlier
                )
            )
        if j + 2 < CHUNKS:
            gather(j + 2)

    gather(0)
    gather(1)
    tiles(0)
    for j in range(CHUNKS):
        send, pass_on, stay = part_all[j]
        size = stay.shape[0] // 2
        if j >= 1:
            send = after(send, pass_all[j - 1])
        got = step(send, "z", 0, f"sum_near_{j}")
        if j + 1 < CHUNKS:
            tiles(j + 1)
            got = after(got, part_all[j + 1][0])
        passed = (got[: 2 * size].astype(f32) + pass_on).astype(bf16)
        pass_all.append(passed)
        stay = got[2 * size :].astype(f32) + stay
        got = step(passed, "z", 1, f"sum_far_{j}")
        zb_all.append(got)
        passed = (got[:size].astype(f32) + stay[:size]).astype(bf16)
        stay = got[size:].astype(f32) + stay[size:]
        if j == CHUNKS - 1:
            passed = after(passed, hidden_all[j - 2])
        pooled = swap(passed, "x_hi", f"sum_x_{j}").astype(f32) + stay
        if j == 0:
            deg = jnp.sum(
                pooled[8 * tile :].reshape(8, 4, tile)
                * jnp.array([1, 32, 1024, 32768], f32)[None, :, None],
                axis=1,
            )
            scale = 1.0 / (1.0 + deg)
            pooled = pooled[: 8 * tile]
        factor = after(scale, passed)[..., None]
        mean = (pooled.reshape(8, tile, cw) * factor).astype(bf16)
        mean = mean.reshape(2, rows_dev, cw)
        got = swap(mean[1], "core", f"mean_core_{j}")
        cols = slice(j * cw, (j + 1) * cw)
        hidden = hidden + jnp.dot(mean[0], w_own[cols], preferred_element_type=f32)
        hidden = hidden + jnp.dot(got, w_other[cols], preferred_element_type=f32)
        hidden_all.append(hidden)
    hidden = jax.nn.relu(hidden)
    return hidden / jnp.sqrt(jnp.mean(hidden * hidden, axis=1, keepdims=True) + 1e-06)


def solution(mesh):
    fine = Mesh(mesh.devices.reshape(SIZES), AXES)
    row = AXES[:2]
    col = AXES[2:]
    return jax.shard_map(
        local,
        mesh=fine,
        in_specs=(
            P(AXES, None),
            P(row, col, None, None, None),
            P(row, col, None),
            P(row, col, None),
            P(row, col),
            P(),
            P(),
            P(),
            P(),
        ),
        out_specs=P(AXES, None),
        check_vma=False,
    )
```

```python
import functools

import jax
import jax.numpy as jnp
from jax import lax
from jax.experimental import pallas as pl
from jax.experimental.pallas import tpu as pltpu
from jax.sharding import Mesh, PartitionSpec as P

AXES = ("x_lo", "y", "z", "x_hi", "core")
SIZES = (2, 4, 4, 2, 2)
CHUNKS = 4
GROUP = 8


def swap(x, axis, name):
    with jax.named_scope(name):
        return lax.ppermute(x, axis, [(0, 1), (1, 0)])


def step(x, axis, second, name):
    pairs = []
    for i in range(4):
        for c in range(2):
            to = i ^ 1 if c == second else 3 - i
            pairs.append((i * 2 + c, to * 2 + c))
    with jax.named_scope(name):
        return lax.ppermute(x, (axis, "core"), pairs)


def after(x, *earlier):
    return lax.optimization_barrier((x, *earlier))[0]


def ring_slot(place, here, core):
    first = jnp.where(core == 0, here ^ 1, 3 - here)
    second = jnp.where(core == 0, 3 - here, here ^ 1)
    return jnp.where(
        place == here, 0, jnp.where(place == first, 1, jnp.where(place == second, 2, 3))
    )


def tile_kernel(src_ref, dst_ref, live_ref, c_own, c_other, pieces_ref, near, far, *refs):
    send, pass_on, stay, panel, acc, sems = refs[-6:]
    copies = [
        pltpu.make_async_copy(near, panel.at[pl.ds(0, 32)], sems.at[0]),
        pltpu.make_async_copy(far, panel.at[pl.ds(32, 32)], sems.at[1]),
    ]
    for copy in copies:
        copy.start()

    @pl.loop(0, 64)
    def _(i):
        acc[i] = jnp.zeros(acc.shape[1:], jnp.float32)

    for copy in copies:
        copy.wait()

    slots, tile = c_own.shape[:2]
    for q, counts in enumerate((c_own, c_other)):

        def body(g, carry, q=q, counts=counts):
            terms = []
            for i in range(GROUP):
                s = g * GROUP + i
                terms.append(
                    jnp.dot(
                        counts[s],
                        panel[src_ref[q * slots + s]],
                        preferred_element_type=jnp.float32,
                    )
                )
            for i in range(GROUP):
                at = dst_ref[q * slots + g * GROUP + i]
                acc[at] = acc[at] + terms[i]
            return carry

        lax.fori_loop(0, (live_ref[q] + GROUP - 1) // GROUP, body, 0)

    size = stay.shape[0] // 2
    extra = size - 8 * tile
    for part in range(8):
        out = (send, send, send, send, pass_on, pass_on, stay, stay)[part]
        base = (part if part < 4 else part % 2) * size

        @pl.loop(0, 8)
        def _(i, part=part, out=out, base=base):
            at = pl.multiple_of(base + i * tile, 16)
            out[pl.ds(at, tile)] = acc[part * 8 + i].astype(out.dtype)

        if extra:
            out[pl.ds(base + 8 * tile, extra)] = pieces_ref[pl.ds(part * extra, extra)].astype(
                out.dtype
            )


def tile_sums(src, dst, live, c_own, c_other, pieces, with_pieces, near, far, earlier, cost):
    tile, w = near.shape[-2:]
    any_spec = pl.BlockSpec(memory_space=pl.ANY)
    vmem = pl.BlockSpec(memory_space=pltpu.VMEM)
    smem = pl.BlockSpec(memory_space=pltpu.SMEM)
    slots = c_own.shape[0]
    size = 8 * tile + (pieces.shape[0] // 8 if with_pieces else 0)
    return pl.pallas_call(
        tile_kernel,
        out_shape=(
            jax.ShapeDtypeStruct((4 * size, w), jnp.bfloat16),
            jax.ShapeDtypeStruct((2 * size, w), jnp.float32),
            jax.ShapeDtypeStruct((2 * size, w), jnp.float32),
        ),
        in_specs=[smem] * 3 + [vmem] * 3 + [any_spec] * (2 + len(earlier)),
        out_specs=(vmem,) * 3,
        scratch_shapes=[
            pltpu.VMEM((64, tile, w), jnp.bfloat16),
            pltpu.VMEM((64, tile, w), jnp.float32),
            pltpu.SemaphoreType.DMA((2,)),
        ],
        compiler_params=pltpu.CompilerParams(vmem_limit_bytes=32 * 1024 * 1024),
        cost_estimate=pl.CostEstimate(
            flops=cost, bytes_accessed=64 * tile * w, transcendentals=0
        ),
    )(src, dst, live, c_own, c_other, pieces, near, far, *earlier)


def message_kernel(first, core_ref, x_hbm, weight, bias, theirs, mine, x, held, row, sems):
    core = core_ref[0]
    chunks, blocks, tile, w = mine.shape
    half = weight.shape[1] // 2
    size = chunks * w
    starts = [
        pl.multiple_of((1 - core) * half + first, 128),
        pl.multiple_of(core * half + first, 128),
    ]
    copies = [
        pltpu.make_async_copy(weight.at[:, pl.ds(starts[i], size)], held.at[i], sems.at[i])
        for i in range(2)
    ]
    whole = [
        pltpu.make_async_copy(x_hbm, x, sems.at[2]),
        pltpu.make_async_copy(bias, row, sems.at[3]),
    ]
    copies[0].start()
    whole[0].start()
    whole[1].start()
    copies[1].start()
    whole[0].wait()
    whole[1].wait()
    for i, out in enumerate((theirs, mine)):
        copies[i].wait()
        for j in range(chunks):
            total = jnp.dot(
                x[...], held[i, :, j * w : (j + 1) * w], preferred_element_type=jnp.float32
            )
            total = jnp.maximum(total + row[:, pl.ds(starts[i] + j * w, w)], 0.0)
            out[j] = total.astype(out.dtype).reshape(blocks, tile, w)


def transform(core, features, weight, bias, first, chunks, tile, w):
    vmem = pl.BlockSpec(memory_space=pltpu.VMEM)
    any_spec = pl.BlockSpec(memory_space=pl.ANY)
    out = jax.ShapeDtypeStruct((chunks, features.shape[0] // tile, tile, w), jnp.bfloat16)
    return pl.pallas_call(
        functools.partial(message_kernel, first),
        out_shape=(out, out),
        in_specs=[pl.BlockSpec(memory_space=pltpu.SMEM), any_spec, any_spec, any_spec],
        out_specs=(vmem, vmem),
        scratch_shapes=[
            pltpu.VMEM(features.shape, jnp.bfloat16),
            pltpu.VMEM((2, features.shape[1], chunks * w), jnp.bfloat16),
            pltpu.VMEM((1, bias.shape[0]), jnp.float32),
            pltpu.SemaphoreType.DMA((4,)),
        ],
        compiler_params=pltpu.CompilerParams(vmem_limit_bytes=60 * 1024 * 1024),
        cost_estimate=pl.CostEstimate(
            flops=4 * features.size * chunks * w,
            bytes_accessed=2 * features.size + 4 * features.shape[1] * chunks * w,
            transcendentals=0,
        ),
    )(core.astype(jnp.int32).reshape(1), features, weight, bias.reshape(1, -1))


def local(
    features,
    walk_counts,
    tile_rows,
    tile_cols,
    live_tiles,
    neigh_weight,
    neigh_bias,
    combine_weight,
    combine_bias,
):
    rows_dev, width = features.shape
    tile = walk_counts.shape[3]
    slots = walk_counts.shape[2]
    half = width // 2
    cw = half // CHUNKS
    blocks = rows_dev // tile
    x_lo, y, z, x_hi, core = (lax.axis_index(a) for a in AXES)

    make = functools.partial(transform, core)
    theirs, mine = make(features, neigh_weight, neigh_bias, 0, 1, tile, cw)
    own = [jnp.concatenate([mine[0], swap(theirs[0], "core", "other_core_0")])]
    first = swap(own[0], "x_lo", "gather_x_0")
    theirs, mine = make(
        after(features, theirs), neigh_weight, neigh_bias, cw, CHUNKS - 1, tile, cw
    )
    theirs = swap(after(theirs, own[0]), "core", "other_core_rest")
    own += [jnp.concatenate([mine[j], theirs[j]]) for j in range(CHUNKS - 1)]

    live = live_tiles[0, 0]
    used = jnp.arange(slots, dtype=jnp.int32) < live
    counts = after(walk_counts, own[0])[0, 0]
    c_own = jnp.where(used[:, None, None], counts, 0).astype(jnp.bfloat16)
    pair0 = jnp.concatenate([own[0], after(first, c_own)])
    rows_own = jnp.where(used, tile_rows[0, 0], 0)
    meta = jnp.stack(
        [rows_own, jnp.where(used, tile_cols[0, 0], 0), jnp.full((slots,), live, jnp.int32)]
    )
    c_other = swap(after(c_own, theirs), "core", "other_tiles")
    metas = jnp.stack([meta, swap(after(meta, own[0]), "core", "other_meta")])
    k = metas[:, 1]
    src = (
        (ring_slot((k // 4) % 4, y, core) * 2 + ((k // 16) ^ x_lo)) * 8
        + jnp.arange(2, dtype=jnp.int32)[:, None] * 4
        + k % 4
    ).reshape(-1)
    b = metas[:, 0]
    ring = ring_slot(b // 16, z, core)
    ring = jnp.where(ring == 0, 3, jnp.where(ring == 3, 0, ring))
    dst = (
        ((ring * 2 + 1 - (((b // 8) % 2) ^ x_hi)) * 2)
        + (((b // 4) % 2) ^ core)
    ) * 4 + b % 4
    dst = dst.reshape(-1)
    lives = metas[:, 2, 0]

    row_sums = jnp.concatenate(
        [jnp.sum(c_own.astype(jnp.float32), axis=2), jnp.sum(c_other.astype(jnp.float32), axis=2)]
    )
    onehot = (jnp.arange(64, dtype=jnp.int32)[:, None] == dst[None, :]).astype(jnp.float32)
    deg = jnp.dot(onehot, row_sums, precision=lax.Precision.HIGHEST).astype(jnp.int32)
    parts = (deg[:, None, :] >> (5 * jnp.arange(4, dtype=jnp.int32))[None, :, None]) & 31
    parts = parts.astype(jnp.bfloat16).reshape(256, tile)

    hidden = (
        jnp.dot(features, combine_weight[:width], preferred_element_type=jnp.float32)
        + combine_bias
    )
    w_own = lax.dynamic_slice_in_dim(combine_weight, width + core * half, half, 0)
    w_other = lax.dynamic_slice_in_dim(combine_weight, width + (1 - core) * half, half, 0)

    second = swap(after(own[1], first), "x_lo", "gather_x_1")
    rest = swap(after(jnp.stack(own[2:]), second), "x_lo", "gather_x_rest")
    f32, bf16 = jnp.float32, jnp.bfloat16
    near_all, far_all, part_all, pass_all, zb_all, hidden_all = [], [], [], [], [], []
    scale = None

    def far(pair, got, j):
        near_all.append(jnp.concatenate([pair, got]))
        far_all.append(step(near_all[j], "y", 1, f"gather_far_{j}"))

    far(pair0, step(pair0, "y", 0, "gather_near_0"), 0)
    pair = after(jnp.concatenate([own[1], second]), near_all[0])
    far(pair, step(pair, "y", 0, "gather_near_1"), 1)
    pairs = jnp.stack([jnp.concatenate([own[j], rest[j - 2]]) for j in range(2, CHUNKS)])
    pairs = after(pairs, near_all[1])
    got = step(pairs, "y", 0, "gather_near_rest")
    for j in range(2, CHUNKS):
        far(pairs[j - 2], got[j - 2], j)

    def tiles(j):
        earlier = (rest, near_all[1]) if j == 0 else ()
        if j == 1:
            earlier += tuple(near_all[2:])
        if j >= 2:
            earlier += (pass_all[j - 2],)
        with jax.named_scope(f"tiles_{j}"):
            part_all.append(
                tile_sums(
                    src, dst, lives, c_own, c_other, parts, j == 0, near_all[j], far_all[j], earlier,
                    2**31 if j < 2 else 2**20,
                )
            )

    tiles(0)
    for j in range(CHUNKS):
        send, pass_on, stay = part_all[j]
        size = stay.shape[0] // 2
        if j >= 1:
            send = after(send, pass_all[j - 1])
        got = step(send, "z", 0, f"sum_near_{j}")
        if j == 0:
            tiles(1)
        if j + 1 < CHUNKS:
            got = after(got, part_all[j + 1][0])
        passed = (got[: 2 * size].astype(f32) + pass_on).astype(bf16)
        pass_all.append(passed)
        stay = got[2 * size :].astype(f32) + stay
        got = step(passed, "z", 1, f"sum_far_{j}")
        if j + 2 < CHUNKS:
            tiles(j + 2)
            got = after(got, part_all[j + 2][0])
        zb_all.append(got)
        passed = (got[:size].astype(f32) + stay[:size]).astype(bf16)
        stay = got[size:].astype(f32) + stay[size:]
        if j == CHUNKS - 1:
            passed = after(passed, hidden_all[j - 2])
        pooled = swap(passed, "x_hi", f"sum_x_{j}").astype(f32) + stay
        if j == 0:
            deg = jnp.sum(
                pooled[8 * tile :].reshape(8, 4, tile)
                * jnp.array([1, 32, 1024, 32768], f32)[None, :, None],
                axis=1,
            )
            scale = 1.0 / (1.0 + deg)
            pooled = pooled[: 8 * tile]
        factor = after(scale, passed)[..., None]
        mean = (pooled.reshape(8, tile, cw) * factor).astype(bf16)
        mean = mean.reshape(2, rows_dev, cw)
        got = swap(mean[1], "core", f"mean_core_{j}")
        cols = slice(j * cw, (j + 1) * cw)
        hidden = hidden + jnp.dot(mean[0], w_own[cols], preferred_element_type=f32)
        hidden = hidden + jnp.dot(got, w_other[cols], preferred_element_type=f32)
        hidden_all.append(hidden)
    hidden = jax.nn.relu(hidden)
    return hidden / jnp.sqrt(jnp.mean(hidden * hidden, axis=1, keepdims=True) + 1e-06)


def solution(mesh):
    fine = Mesh(mesh.devices.reshape(SIZES), AXES)
    row = AXES[:2]
    col = AXES[2:]
    return jax.shard_map(
        local,
        mesh=fine,
        in_specs=(
            P(AXES, None),
            P(row, col, None, None, None),
            P(row, col, None),
            P(row, col, None),
            P(row, col),
            P(),
            P(),
            P(),
            P(),
        ),
        out_specs=P(AXES, None),
        check_vma=False,
    )
```

```python
import functools

import jax
import jax.numpy as jnp
from jax import lax
from jax.experimental import pallas as pl
from jax.experimental.pallas import tpu as pltpu
from jax.sharding import Mesh, PartitionSpec as P

AXES = ("x_lo", "y", "z", "x_hi", "core")
SIZES = (2, 4, 4, 2, 2)
CHUNKS = 4
GROUP = 8


def swap(x, axis, name):
    with jax.named_scope(name):
        return lax.ppermute(x, axis, [(0, 1), (1, 0)])


def step(x, axis, second, name):
    pairs = []
    for i in range(4):
        for c in range(2):
            to = i ^ 1 if c == second else 3 - i
            pairs.append((i * 2 + c, to * 2 + c))
    with jax.named_scope(name):
        return lax.ppermute(x, (axis, "core"), pairs)


def after(x, *earlier):
    return lax.optimization_barrier((x, *earlier))[0]


def ring_slot(place, here, core):
    first = jnp.where(core == 0, here ^ 1, 3 - here)
    second = jnp.where(core == 0, 3 - here, here ^ 1)
    return jnp.where(
        place == here, 0, jnp.where(place == first, 1, jnp.where(place == second, 2, 3))
    )


def tile_kernel(src_ref, dst_ref, live_ref, c_own, c_other, pieces_ref, near, far, *refs):
    send, pass_on, stay, panel, acc, sems = refs[-6:]
    copies = [
        pltpu.make_async_copy(near, panel.at[pl.ds(0, 32)], sems.at[0]),
        pltpu.make_async_copy(far, panel.at[pl.ds(32, 32)], sems.at[1]),
    ]
    for copy in copies:
        copy.start()

    @pl.loop(0, 64)
    def _(i):
        acc[i] = jnp.zeros(acc.shape[1:], jnp.float32)

    for copy in copies:
        copy.wait()

    slots, tile = c_own.shape[:2]
    for q, counts in enumerate((c_own, c_other)):

        def body(g, carry, q=q, counts=counts):
            terms = []
            for i in range(GROUP):
                s = g * GROUP + i
                terms.append(
                    jnp.dot(
                        counts[s],
                        panel[src_ref[q * slots + s]],
                        preferred_element_type=jnp.float32,
                    )
                )
            for i in range(GROUP):
                at = dst_ref[q * slots + g * GROUP + i]
                acc[at] = acc[at] + terms[i]
            return carry

        lax.fori_loop(0, (live_ref[q] + GROUP - 1) // GROUP, body, 0)

    size = stay.shape[0] // 2
    extra = size - 8 * tile
    for part in range(8):
        out = (send, send, send, send, pass_on, pass_on, stay, stay)[part]
        base = (part if part < 4 else part % 2) * size

        @pl.loop(0, 8)
        def _(i, part=part, out=out, base=base):
            at = pl.multiple_of(base + i * tile, 16)
            out[pl.ds(at, tile)] = acc[part * 8 + i].astype(out.dtype)

        if extra:
            out[pl.ds(base + 8 * tile, extra)] = pieces_ref[pl.ds(part * extra, extra)].astype(
                out.dtype
            )


def tile_sums(src, dst, live, c_own, c_other, pieces, with_pieces, near, far, earlier, cost):
    tile, w = near.shape[-2:]
    any_spec = pl.BlockSpec(memory_space=pl.ANY)
    vmem = pl.BlockSpec(memory_space=pltpu.VMEM)
    smem = pl.BlockSpec(memory_space=pltpu.SMEM)
    slots = c_own.shape[0]
    size = 8 * tile + (pieces.shape[0] // 8 if with_pieces else 0)
    return pl.pallas_call(
        tile_kernel,
        out_shape=(
            jax.ShapeDtypeStruct((4 * size, w), jnp.bfloat16),
            jax.ShapeDtypeStruct((2 * size, w), jnp.float32),
            jax.ShapeDtypeStruct((2 * size, w), jnp.float32),
        ),
        in_specs=[smem] * 3 + [vmem] * 3 + [any_spec] * (2 + len(earlier)),
        out_specs=(vmem,) * 3,
        scratch_shapes=[
            pltpu.VMEM((64, tile, w), jnp.bfloat16),
            pltpu.VMEM((64, tile, w), jnp.float32),
            pltpu.SemaphoreType.DMA((2,)),
        ],
        compiler_params=pltpu.CompilerParams(vmem_limit_bytes=32 * 1024 * 1024),
        cost_estimate=pl.CostEstimate(
            flops=cost, bytes_accessed=64 * tile * w, transcendentals=0
        ),
    )(src, dst, live, c_own, c_other, pieces, near, far, *earlier)


def message_kernel(first, core_ref, x_hbm, weight, bias, theirs, mine, x, held, row, sems):
    core = core_ref[0]
    tile, w = mine.shape[1:]
    blocks = x.shape[0] // tile
    chunks = mine.shape[0] // blocks
    half = weight.shape[1] // 2
    size = chunks * w
    starts = [
        pl.multiple_of((1 - core) * half + first, 128),
        pl.multiple_of(core * half + first, 128),
    ]
    copies = [
        pltpu.make_async_copy(weight.at[:, pl.ds(starts[i], size)], held.at[i], sems.at[i])
        for i in range(2)
    ]
    whole = [
        pltpu.make_async_copy(x_hbm, x, sems.at[2]),
        pltpu.make_async_copy(bias, row, sems.at[3]),
    ]
    copies[0].start()
    whole[0].start()
    whole[1].start()
    copies[1].start()
    whole[0].wait()
    whole[1].wait()
    for i, out in enumerate((theirs, mine)):
        copies[i].wait()
        for j in range(chunks):
            total = jnp.dot(
                x[...], held[i, :, j * w : (j + 1) * w], preferred_element_type=jnp.float32
            )
            total = jnp.maximum(total + row[:, pl.ds(starts[i] + j * w, w)], 0.0)
            out[j * blocks : (j + 1) * blocks] = total.astype(out.dtype).reshape(blocks, tile, w)


def transform(core, features, weight, bias, first, chunks, tile, w):
    vmem = pl.BlockSpec(memory_space=pltpu.VMEM)
    any_spec = pl.BlockSpec(memory_space=pl.ANY)
    out = jax.ShapeDtypeStruct((chunks * features.shape[0] // tile, tile, w), jnp.bfloat16)
    return pl.pallas_call(
        functools.partial(message_kernel, first),
        out_shape=(out, out),
        in_specs=[pl.BlockSpec(memory_space=pltpu.SMEM), any_spec, any_spec, any_spec],
        out_specs=(vmem, vmem),
        scratch_shapes=[
            pltpu.VMEM(features.shape, jnp.bfloat16),
            pltpu.VMEM((2, features.shape[1], chunks * w), jnp.bfloat16),
            pltpu.VMEM((1, bias.shape[0]), jnp.float32),
            pltpu.SemaphoreType.DMA((4,)),
        ],
        compiler_params=pltpu.CompilerParams(vmem_limit_bytes=60 * 1024 * 1024),
        cost_estimate=pl.CostEstimate(
            flops=32 * features.size * chunks * w,
            bytes_accessed=2 * features.size + 4 * features.shape[1] * chunks * w,
            transcendentals=0,
        ),
    )(core.astype(jnp.int32).reshape(1), features, weight, bias.reshape(1, -1))


def local(
    features,
    walk_counts,
    tile_rows,
    tile_cols,
    live_tiles,
    neigh_weight,
    neigh_bias,
    combine_weight,
    combine_bias,
):
    rows_dev, width = features.shape
    tile = walk_counts.shape[3]
    slots = walk_counts.shape[2]
    half = width // 2
    cw = half // CHUNKS
    blocks = rows_dev // tile
    x_lo, y, z, x_hi, core = (lax.axis_index(a) for a in AXES)

    make = functools.partial(transform, core)
    theirs, mine = make(features, neigh_weight, neigh_bias, 0, 1, tile, cw)
    mine0 = mine
    own = [jnp.concatenate([mine, swap(theirs, "core", "other_core_0")])]
    first = swap(own[0], "x_lo", "gather_x_0")
    theirs, mine = make(
        after(features, own[0]), neigh_weight, neigh_bias, cw, CHUNKS - 1, tile, cw
    )
    theirs = swap(theirs, "core", "other_core_rest")
    for j in range(CHUNKS - 1):
        part = slice(j * blocks, (j + 1) * blocks)
        own.append(jnp.concatenate([mine[part], theirs[part]]))

    live = live_tiles[0, 0]
    used = jnp.arange(slots, dtype=jnp.int32) < live
    counts = after(walk_counts, mine0)[0, 0]
    c_own = jnp.where(used[:, None, None], counts, 0).astype(jnp.bfloat16)
    pair0 = jnp.concatenate([own[0], first])
    rows_own = jnp.where(used, tile_rows[0, 0], 0)
    meta = jnp.stack(
        [rows_own, jnp.where(used, tile_cols[0, 0], 0), jnp.full((slots,), live, jnp.int32)]
    )
    c_other = swap(after(c_own, theirs), "core", "other_tiles")
    metas = jnp.stack([meta, swap(after(meta, own[0]), "core", "other_meta")])
    k = metas[:, 1]
    src = (
        (ring_slot((k // 4) % 4, y, core) * 2 + ((k // 16) ^ x_lo)) * 8
        + jnp.arange(2, dtype=jnp.int32)[:, None] * 4
        + k % 4
    ).reshape(-1)
    b = metas[:, 0]
    ring = ring_slot(b // 16, z, core)
    ring = jnp.where(ring == 0, 3, jnp.where(ring == 3, 0, ring))
    dst = (
        ((ring * 2 + 1 - (((b // 8) % 2) ^ x_hi)) * 2)
        + (((b // 4) % 2) ^ core)
    ) * 4 + b % 4
    dst = dst.reshape(-1)
    lives = metas[:, 2, 0]

    row_sums = jnp.concatenate(
        [jnp.sum(c_own.astype(jnp.float32), axis=2), jnp.sum(c_other.astype(jnp.float32), axis=2)]
    )
    onehot = (jnp.arange(64, dtype=jnp.int32)[:, None] == dst[None, :]).astype(jnp.float32)
    deg = jnp.dot(onehot, row_sums, precision=lax.Precision.HIGHEST).astype(jnp.int32)
    parts = (deg[:, None, :] >> (5 * jnp.arange(4, dtype=jnp.int32))[None, :, None]) & 31
    parts = parts.astype(jnp.bfloat16).reshape(256, tile)

    hidden = (
        jnp.dot(features, combine_weight[:width], preferred_element_type=jnp.float32)
        + combine_bias
    )
    w_own = lax.dynamic_slice_in_dim(combine_weight, width + core * half, half, 0)
    w_other = lax.dynamic_slice_in_dim(combine_weight, width + (1 - core) * half, half, 0)

    second = swap(after(own[1], first), "x_lo", "gather_x_1")
    rest = swap(after(jnp.stack(own[2:]), second), "x_lo", "gather_x_rest")
    f32, bf16 = jnp.float32, jnp.bfloat16
    near_all, far_all, part_all, pass_all, hidden_all = [], [], [], [], []
    scale = None

    def far(pair, got, j):
        near_all.append(jnp.concatenate([pair, got]))
        far_all.append(step(near_all[j], "y", 1, f"gather_far_{j}"))

    far(pair0, step(pair0, "y", 0, "gather_near_0"), 0)
    pair = after(jnp.concatenate([own[1], second]), near_all[0])
    far(pair, step(pair, "y", 0, "gather_near_1"), 1)
    pairs = jnp.stack([jnp.concatenate([own[j], rest[j - 2]]) for j in range(2, CHUNKS)])
    pairs = after(pairs, near_all[1], far_all[0])
    got = step(pairs, "y", 0, "gather_near_rest")
    for j in range(2, CHUNKS):
        far(pairs[j - 2], got[j - 2], j)

    def tiles(j):
        earlier = (rest, near_all[1]) if j == 0 else ()
        if j == 1:
            earlier += tuple(near_all[2:])
        if j >= 2:
            earlier += (pass_all[0],)
        with jax.named_scope(f"tiles_{j}"):
            part_all.append(
                tile_sums(
                    src, dst, lives, c_own, c_other, parts, j == 0, near_all[j], far_all[j], earlier,
                    2**31 if j < 2 else 2**20,
                )
            )

    tiles(0)
    for j in range(CHUNKS):
        send, pass_on, stay = part_all[j]
        size = stay.shape[0] // 2
        got = step(send, "z", 0, f"sum_near_{j}")
        if j == 0:
            tiles(1)
            got = after(got, part_all[1][0])
        else:
            got = after(got, part_all[-1][0])
        passed = (got[: 2 * size].astype(f32) + pass_on).astype(bf16)
        pass_all.append(passed)
        stay = got[2 * size :].astype(f32) + stay
        got = step(passed, "z", 1, f"sum_far_{j}")
        if j == 0:
            for i in range(2, CHUNKS):
                tiles(i)
            got = after(got, part_all[-1][0])
        passed = (got[:size].astype(f32) + stay[:size]).astype(bf16)
        stay = got[size:].astype(f32) + stay[size:]
        if j == CHUNKS - 1:
            passed = after(passed, hidden_all[j - 2])
        pooled = swap(passed, "x_hi", f"sum_x_{j}").astype(f32) + stay
        if j == 0:
            deg = jnp.sum(
                pooled[8 * tile :].reshape(8, 4, tile)
                * jnp.array([1, 32, 1024, 32768], f32)[None, :, None],
                axis=1,
            )
            scale = 1.0 / (1.0 + deg)
            pooled = pooled[: 8 * tile]
        factor = after(scale, passed)[..., None]
        mean = (pooled.reshape(8, tile, cw) * factor).astype(bf16)
        mean = mean.reshape(2, rows_dev, cw)
        got = swap(mean[1], "core", f"mean_core_{j}")
        cols = slice(j * cw, (j + 1) * cw)
        hidden = hidden + jnp.dot(mean[0], w_own[cols], preferred_element_type=f32)
        hidden = hidden + jnp.dot(got, w_other[cols], preferred_element_type=f32)
        hidden_all.append(hidden)
    hidden = jax.nn.relu(hidden)
    return hidden / jnp.sqrt(jnp.mean(hidden * hidden, axis=1, keepdims=True) + 1e-06)


def solution(mesh):
    fine = Mesh(mesh.devices.reshape(SIZES), AXES)
    row = AXES[:2]
    col = AXES[2:]
    return jax.shard_map(
        local,
        mesh=fine,
        in_specs=(
            P(AXES, None),
            P(row, col, None, None, None),
            P(row, col, None),
            P(row, col, None),
            P(row, col),
            P(),
            P(),
            P(),
            P(),
        ),
        out_specs=P(AXES, None),
        check_vma=False,
    )
```

```python
import functools

import jax
import jax.numpy as jnp
from jax import lax
from jax.experimental import pallas as pl
from jax.experimental.pallas import tpu as pltpu
from jax.sharding import Mesh, PartitionSpec as P

AXES = ("x_lo", "y", "z", "x_hi", "core")
SIZES = (2, 4, 4, 2, 2)
CHUNKS = 4
GROUP = 8


def swap(x, axis, name):
    with jax.named_scope(name):
        return lax.ppermute(x, axis, [(0, 1), (1, 0)])


def step(x, axis, second, name):
    pairs = []
    for i in range(4):
        for c in range(2):
            to = i ^ 1 if c == second else 3 - i
            pairs.append((i * 2 + c, to * 2 + c))
    with jax.named_scope(name):
        return lax.ppermute(x, (axis, "core"), pairs)


def after(x, *earlier):
    return lax.optimization_barrier((x, *earlier))[0]


def ring_slot(place, here, core):
    first = jnp.where(core == 0, here ^ 1, 3 - here)
    second = jnp.where(core == 0, 3 - here, here ^ 1)
    return jnp.where(
        place == here, 0, jnp.where(place == first, 1, jnp.where(place == second, 2, 3))
    )


def tile_kernel(src_ref, dst_ref, live_ref, c_own, c_other, pieces_ref, near, far, *refs):
    send, pass_on, stay, panel, acc, sems = refs[-6:]
    copies = [
        pltpu.make_async_copy(near, panel.at[pl.ds(0, 32)], sems.at[0]),
        pltpu.make_async_copy(far, panel.at[pl.ds(32, 32)], sems.at[1]),
    ]
    for copy in copies:
        copy.start()

    @pl.loop(0, 64)
    def _(i):
        acc[i] = jnp.zeros(acc.shape[1:], jnp.float32)

    for copy in copies:
        copy.wait()

    slots, tile = c_own.shape[:2]
    for q, counts in enumerate((c_own, c_other)):

        def body(g, carry, q=q, counts=counts):
            terms = []
            for i in range(GROUP):
                s = g * GROUP + i
                terms.append(
                    jnp.dot(
                        counts[s],
                        panel[src_ref[q * slots + s]],
                        preferred_element_type=jnp.float32,
                    )
                )
            for i in range(GROUP):
                at = dst_ref[q * slots + g * GROUP + i]
                acc[at] = acc[at] + terms[i]
            return carry

        lax.fori_loop(0, (live_ref[q] + GROUP - 1) // GROUP, body, 0)

    size = stay.shape[0] // 2
    extra = size - 8 * tile
    for part in range(8):
        out = (send, send, send, send, pass_on, pass_on, stay, stay)[part]
        base = (part if part < 4 else part % 2) * size

        @pl.loop(0, 8)
        def _(i, part=part, out=out, base=base):
            at = pl.multiple_of(base + i * tile, 16)
            out[pl.ds(at, tile)] = acc[part * 8 + i].astype(out.dtype)

        if extra:
            out[pl.ds(base + 8 * tile, extra)] = pieces_ref[pl.ds(part * extra, extra)].astype(
                out.dtype
            )


def tile_sums(src, dst, live, c_own, c_other, pieces, with_pieces, near, far, earlier, cost):
    tile, w = near.shape[-2:]
    any_spec = pl.BlockSpec(memory_space=pl.ANY)
    vmem = pl.BlockSpec(memory_space=pltpu.VMEM)
    smem = pl.BlockSpec(memory_space=pltpu.SMEM)
    slots = c_own.shape[0]
    size = 8 * tile + (pieces.shape[0] // 8 if with_pieces else 0)
    return pl.pallas_call(
        tile_kernel,
        out_shape=(
            jax.ShapeDtypeStruct((4 * size, w), jnp.bfloat16),
            jax.ShapeDtypeStruct((2 * size, w), jnp.float32),
            jax.ShapeDtypeStruct((2 * size, w), jnp.float32),
        ),
        in_specs=[smem] * 3 + [vmem] * 3 + [any_spec] * (2 + len(earlier)),
        out_specs=(vmem,) * 3,
        scratch_shapes=[
            pltpu.VMEM((64, tile, w), jnp.bfloat16),
            pltpu.VMEM((64, tile, w), jnp.float32),
            pltpu.SemaphoreType.DMA((2,)),
        ],
        compiler_params=pltpu.CompilerParams(vmem_limit_bytes=32 * 1024 * 1024),
        cost_estimate=pl.CostEstimate(
            flops=cost, bytes_accessed=64 * tile * w, transcendentals=0
        ),
    )(src, dst, live, c_own, c_other, pieces, near, far, *earlier)


def message_kernel(first, core_ref, x_hbm, weight, bias, theirs, mine, x, held, row, sems):
    core = core_ref[0]
    tile, w = mine.shape[1:]
    blocks = x.shape[0] // tile
    chunks = mine.shape[0] // blocks
    half = weight.shape[1] // 2
    size = chunks * w
    starts = [
        pl.multiple_of((1 - core) * half + first, 128),
        pl.multiple_of(core * half + first, 128),
    ]
    copies = [
        pltpu.make_async_copy(weight.at[:, pl.ds(starts[i], size)], held.at[i], sems.at[i])
        for i in range(2)
    ]
    whole = [
        pltpu.make_async_copy(x_hbm, x, sems.at[2]),
        pltpu.make_async_copy(bias, row, sems.at[3]),
    ]
    copies[0].start()
    whole[0].start()
    whole[1].start()
    copies[1].start()
    whole[0].wait()
    whole[1].wait()
    for i, out in enumerate((theirs, mine)):
        copies[i].wait()
        for j in range(chunks):
            total = jnp.dot(
                x[...], held[i, :, j * w : (j + 1) * w], preferred_element_type=jnp.float32
            )
            total = jnp.maximum(total + row[:, pl.ds(starts[i] + j * w, w)], 0.0)
            out[j * blocks : (j + 1) * blocks] = total.astype(out.dtype).reshape(blocks, tile, w)


def transform(core, features, weight, bias, first, chunks, tile, w):
    vmem = pl.BlockSpec(memory_space=pltpu.VMEM)
    any_spec = pl.BlockSpec(memory_space=pl.ANY)
    out = jax.ShapeDtypeStruct((chunks * features.shape[0] // tile, tile, w), jnp.bfloat16)
    return pl.pallas_call(
        functools.partial(message_kernel, first),
        out_shape=(out, out),
        in_specs=[pl.BlockSpec(memory_space=pltpu.SMEM), any_spec, any_spec, any_spec],
        out_specs=(vmem, vmem),
        scratch_shapes=[
            pltpu.VMEM(features.shape, jnp.bfloat16),
            pltpu.VMEM((2, features.shape[1], chunks * w), jnp.bfloat16),
            pltpu.VMEM((1, bias.shape[0]), jnp.float32),
            pltpu.SemaphoreType.DMA((4,)),
        ],
        compiler_params=pltpu.CompilerParams(vmem_limit_bytes=60 * 1024 * 1024),
        cost_estimate=pl.CostEstimate(
            flops=32 * features.size * chunks * w,
            bytes_accessed=2 * features.size + 4 * features.shape[1] * chunks * w,
            transcendentals=0,
        ),
    )(core.astype(jnp.int32).reshape(1), features, weight, bias.reshape(1, -1))


def finish_kernel(hidden, near, got, weight, out):
    total = hidden[...]
    w = near.shape[1]
    total += jnp.dot(near[...], weight[:w], preferred_element_type=jnp.float32)
    total += jnp.dot(got[...], weight[w:], preferred_element_type=jnp.float32)
    total = jnp.maximum(total, 0.0)
    mean = jnp.mean(total * total, axis=1, keepdims=True)
    out[...] = total / jnp.sqrt(mean + 1e-06)


def finish(hidden, near, got, weight):
    rows, width = hidden.shape
    block = 128
    by_row = lambda w: pl.BlockSpec((block, w), lambda i: (i, 0))
    return pl.pallas_call(
        finish_kernel,
        grid=(rows // block,),
        out_shape=jax.ShapeDtypeStruct(hidden.shape, jnp.float32),
        in_specs=[
            by_row(width),
            by_row(near.shape[1]),
            by_row(near.shape[1]),
            pl.BlockSpec(weight.shape, lambda i: (0, 0)),
        ],
        out_specs=by_row(width),
        compiler_params=pltpu.CompilerParams(vmem_limit_bytes=32 * 1024 * 1024),
    )(hidden, near, got, weight)


def local(
    features,
    walk_counts,
    tile_rows,
    tile_cols,
    live_tiles,
    neigh_weight,
    neigh_bias,
    combine_weight,
    combine_bias,
):
    rows_dev, width = features.shape
    tile = walk_counts.shape[3]
    slots = walk_counts.shape[2]
    half = width // 2
    cw = half // CHUNKS
    blocks = rows_dev // tile
    x_lo, y, z, x_hi, core = (lax.axis_index(a) for a in AXES)

    make = functools.partial(transform, core)
    theirs, mine = make(features, neigh_weight, neigh_bias, 0, 1, tile, cw)
    own = [jnp.concatenate([mine, swap(theirs, "core", "other_core_0")])]
    first = swap(own[0], "x_lo", "gather_x_0")
    theirs, mine = make(
        after(features, theirs), neigh_weight, neigh_bias, cw, CHUNKS - 1, tile, cw
    )
    theirs = swap(theirs, "core", "other_core_rest")
    for j in range(CHUNKS - 1):
        part = slice(j * blocks, (j + 1) * blocks)
        own.append(jnp.concatenate([mine[part], theirs[part]]))

    live = live_tiles[0, 0]
    used = jnp.arange(slots, dtype=jnp.int32) < live
    counts = after(walk_counts, own[0])[0, 0]
    c_own = jnp.where(used[:, None, None], counts, 0).astype(jnp.bfloat16)
    pair0 = jnp.concatenate([own[0], after(first, c_own)])
    rows_own = jnp.where(used, tile_rows[0, 0], 0)
    meta = jnp.stack(
        [rows_own, jnp.where(used, tile_cols[0, 0], 0), jnp.full((slots,), live, jnp.int32)]
    )
    c_other = swap(after(c_own, theirs), "core", "other_tiles")
    metas = jnp.stack([meta, swap(after(meta, own[0]), "core", "other_meta")])
    k = metas[:, 1]
    src = (
        (ring_slot((k // 4) % 4, y, core) * 2 + ((k // 16) ^ x_lo)) * 8
        + jnp.arange(2, dtype=jnp.int32)[:, None] * 4
        + k % 4
    ).reshape(-1)
    b = metas[:, 0]
    ring = ring_slot(b // 16, z, core)
    ring = jnp.where(ring == 0, 3, jnp.where(ring == 3, 0, ring))
    dst = (
        ((ring * 2 + 1 - (((b // 8) % 2) ^ x_hi)) * 2)
        + (((b // 4) % 2) ^ core)
    ) * 4 + b % 4
    dst = dst.reshape(-1)
    lives = metas[:, 2, 0]

    row_sums = jnp.concatenate(
        [jnp.sum(c_own.astype(jnp.float32), axis=2), jnp.sum(c_other.astype(jnp.float32), axis=2)]
    )
    onehot = (jnp.arange(64, dtype=jnp.int32)[:, None] == dst[None, :]).astype(jnp.float32)
    deg = jnp.dot(onehot, row_sums, precision=lax.Precision.HIGHEST).astype(jnp.int32)
    parts = (deg[:, None, :] >> (5 * jnp.arange(4, dtype=jnp.int32))[None, :, None]) & 31
    parts = parts.astype(jnp.bfloat16).reshape(256, tile)

    hidden = (
        jnp.dot(features, combine_weight[:width], preferred_element_type=jnp.float32)
        + combine_bias
    )
    w_own = lax.dynamic_slice_in_dim(combine_weight, width + core * half, half, 0)
    w_other = lax.dynamic_slice_in_dim(combine_weight, width + (1 - core) * half, half, 0)

    second = swap(after(own[1], first), "x_lo", "gather_x_1")
    f32, bf16 = jnp.float32, jnp.bfloat16
    near_all, far_all, part_all, pass_all, hidden_all = [], [], [], [], []
    scale = None

    def far(pair, got, j):
        near_all.append(jnp.concatenate([pair, got]))
        far_all.append(step(near_all[j], "y", 1, f"gather_far_{j}"))

    far(pair0, step(pair0, "y", 0, "gather_near_0"), 0)
    second = after(second, near_all[0])
    rest = swap(after(jnp.stack(own[2:]), second), "x_lo", "gather_x_rest")
    partner = [first, second] + [rest[j] for j in range(CHUNKS - 2)]
    for j in range(1, CHUNKS):
        pair = jnp.concatenate([own[j], partner[j]])
        pair = after(pair, near_all[j - 1], *far_all[: j - 1])
        far(pair, step(pair, "y", 0, f"gather_near_{j}"), j)

    def tiles(j):
        earlier = (rest, near_all[1]) if j == 0 else ()
        if 0 < j < CHUNKS - 1:
            earlier += (near_all[j + 1],)
        if j >= 2:
            earlier += (pass_all[0],)
        with jax.named_scope(f"tiles_{j}"):
            part_all.append(
                tile_sums(
                    src, dst, lives, c_own, c_other, parts, j == 0, near_all[j], far_all[j], earlier,
                    2**31 if j < 2 else 2**20,
                )
            )

    tiles(0)
    for j in range(CHUNKS):
        send, pass_on, stay = part_all[j]
        size = stay.shape[0] // 2
        got = step(send, "z", 0, f"sum_near_{j}")
        if j == 0:
            tiles(1)
            got = after(got, part_all[1][0])
        else:
            got = after(got, part_all[-1][0])
        passed = (got[: 2 * size].astype(f32) + pass_on).astype(bf16)
        pass_all.append(passed)
        stay = got[2 * size :].astype(f32) + stay
        got = step(passed, "z", 1, f"sum_far_{j}")
        if j == 0:
            for i in range(2, CHUNKS):
                tiles(i)
            got = after(got, part_all[-1][0])
        passed = (got[:size].astype(f32) + stay[:size]).astype(bf16)
        stay = got[size:].astype(f32) + stay[size:]
        if j == CHUNKS - 1:
            passed = after(passed, hidden_all[j - 2])
        pooled = swap(passed, "x_hi", f"sum_x_{j}").astype(f32) + stay
        if j == 0:
            deg = jnp.sum(
                pooled[8 * tile :].reshape(8, 4, tile)
                * jnp.array([1, 32, 1024, 32768], f32)[None, :, None],
                axis=1,
            )
            scale = 1.0 / (1.0 + deg)
            pooled = pooled[: 8 * tile]
        factor = after(scale, passed)[..., None]
        mean = (pooled.reshape(8, tile, cw) * factor).astype(bf16)
        mean = mean.reshape(2, rows_dev, cw)
        got = swap(mean[1], "core", f"mean_core_{j}")
        cols = slice(j * cw, (j + 1) * cw)
        if j == CHUNKS - 1:
            weight = jnp.concatenate([w_own[cols], w_other[cols]])
            return finish(hidden, mean[0], got, weight)
        hidden = hidden + jnp.dot(mean[0], w_own[cols], preferred_element_type=f32)
        hidden = hidden + jnp.dot(got, w_other[cols], preferred_element_type=f32)
        hidden_all.append(hidden)


def solution(mesh):
    fine = Mesh(mesh.devices.reshape(SIZES), AXES)
    row = AXES[:2]
    col = AXES[2:]
    return jax.shard_map(
        local,
        mesh=fine,
        in_specs=(
            P(AXES, None),
            P(row, col, None, None, None),
            P(row, col, None),
            P(row, col, None),
            P(row, col),
            P(),
            P(),
            P(),
            P(),
        ),
        out_specs=P(AXES, None),
        check_vma=False,
    )
```

```python
import functools

import jax
import jax.numpy as jnp
from jax import lax
from jax.experimental import pallas as pl
from jax.experimental.pallas import tpu as pltpu
from jax.sharding import Mesh, PartitionSpec as P

AXES = ("x_lo", "y", "z", "x_hi", "core")
SIZES = (2, 4, 4, 2, 2)
CHUNKS = 4
GROUP = 8


def swap(x, axis, name):
    with jax.named_scope(name):
        return lax.ppermute(x, axis, [(0, 1), (1, 0)])


def step(x, axis, second, name):
    pairs = []
    for i in range(4):
        for c in range(2):
            to = i ^ 1 if c == second else 3 - i
            pairs.append((i * 2 + c, to * 2 + c))
    with jax.named_scope(name):
        return lax.ppermute(x, (axis, "core"), pairs)


def after(x, *earlier):
    return lax.optimization_barrier((x, *earlier))[0]


def ring_slot(place, here, core):
    first = jnp.where(core == 0, here ^ 1, 3 - here)
    second = jnp.where(core == 0, 3 - here, here ^ 1)
    return jnp.where(
        place == here, 0, jnp.where(place == first, 1, jnp.where(place == second, 2, 3))
    )


def tile_kernel(src_ref, dst_ref, live_ref, c_own, c_other, pieces_ref, near, far, *refs):
    send, pass_on, stay, panel, acc, sems = refs
    copies = [
        pltpu.make_async_copy(near, panel.at[pl.ds(0, 32)], sems.at[0]),
        pltpu.make_async_copy(far, panel.at[pl.ds(32, 32)], sems.at[1]),
    ]
    for copy in copies:
        copy.start()

    @pl.loop(0, 64)
    def _(i):
        acc[i] = jnp.zeros(acc.shape[1:], jnp.float32)

    for copy in copies:
        copy.wait()

    slots, tile = c_own.shape[:2]
    for q, counts in enumerate((c_own, c_other)):

        def body(g, carry, q=q, counts=counts):
            terms = []
            for i in range(GROUP):
                s = g * GROUP + i
                terms.append(
                    jnp.dot(
                        counts[s],
                        panel[src_ref[q * slots + s]],
                        preferred_element_type=jnp.float32,
                    )
                )
            for i in range(GROUP):
                at = dst_ref[q * slots + g * GROUP + i]
                acc[at] = acc[at] + terms[i]
            return carry

        lax.fori_loop(0, (live_ref[q] + GROUP - 1) // GROUP, body, 0)

    size = stay.shape[0] // 2
    extra = size - 8 * tile
    for part in range(8):
        out = (send, send, send, send, pass_on, pass_on, stay, stay)[part]
        base = (part if part < 4 else part % 2) * size

        @pl.loop(0, 8)
        def _(i, part=part, out=out, base=base):
            at = pl.multiple_of(base + i * tile, 16)
            out[pl.ds(at, tile)] = acc[part * 8 + i].astype(out.dtype)

        if extra:
            out[pl.ds(base + 8 * tile, extra)] = pieces_ref[pl.ds(part * extra, extra)].astype(
                out.dtype
            )


def tile_sums(src, dst, live, c_own, c_other, pieces, with_pieces, near, far, cost):
    tile, w = near.shape[-2:]
    any_spec = pl.BlockSpec(memory_space=pl.ANY)
    vmem = pl.BlockSpec(memory_space=pltpu.VMEM)
    smem = pl.BlockSpec(memory_space=pltpu.SMEM)
    slots = c_own.shape[0]
    size = 8 * tile + (pieces.shape[0] // 8 if with_pieces else 0)
    return pl.pallas_call(
        tile_kernel,
        out_shape=(
            jax.ShapeDtypeStruct((4 * size, w), jnp.bfloat16),
            jax.ShapeDtypeStruct((2 * size, w), jnp.bfloat16),
            jax.ShapeDtypeStruct((2 * size, w), jnp.bfloat16),
        ),
        in_specs=[smem] * 3 + [vmem] * 3 + [any_spec] * 2,
        out_specs=(vmem,) * 3,
        scratch_shapes=[
            pltpu.VMEM((64, tile, w), jnp.bfloat16),
            pltpu.VMEM((64, tile, w), jnp.float32),
            pltpu.SemaphoreType.DMA((2,)),
        ],
        compiler_params=pltpu.CompilerParams(vmem_limit_bytes=16 * 1024 * 1024),
        cost_estimate=pl.CostEstimate(
            flops=cost, bytes_accessed=64 * tile * w, transcendentals=0
        ),
    )(src, dst, live, c_own, c_other, pieces, near, far)


def message_kernel(first, core_ref, x_own, x_other, weight, bias, *refs):
    outs, (x, held, row, sems) = refs[:-4], refs[-4:]
    half = weight.shape[1] // 2
    rows, size = x_own.shape[0], held.shape[1]
    tile, w = outs[0].shape[1:]
    at = pl.multiple_of(core_ref[0] * half + first, 128)
    copies = [
        pltpu.make_async_copy(x_own, x.at[pl.ds(0, rows)], sems.at[0]),
        pltpu.make_async_copy(weight.at[:, pl.ds(at, size)], held, sems.at[1]),
        pltpu.make_async_copy(bias, row, sems.at[2]),
        pltpu.make_async_copy(x_other, x.at[pl.ds(rows, rows)], sems.at[3]),
    ]
    for copy in copies:
        copy.start()
    for copy in copies:
        copy.wait()
    blocks = 2 * rows // tile
    chunk = 0
    for out in outs:
        for j in range(out.shape[0] // blocks):
            total = jnp.dot(
                x[...], held[:, chunk * w : (chunk + 1) * w], preferred_element_type=jnp.float32
            )
            total = jnp.maximum(total + row[:, pl.ds(at + chunk * w, w)], 0.0)
            total = total.astype(out.dtype).reshape(blocks, tile, w)
            out[j * blocks : (j + 1) * blocks] = total
            chunk += 1


def transform(core, x_own, x_other, weight, bias, first, sizes, tile, w, limit):
    any_spec = pl.BlockSpec(memory_space=pl.ANY)
    rows, width = x_own.shape
    blocks = 2 * rows // tile
    chunks = sum(sizes)
    return pl.pallas_call(
        functools.partial(message_kernel, first),
        out_shape=tuple(jax.ShapeDtypeStruct((n * blocks, tile, w), jnp.bfloat16) for n in sizes),
        in_specs=[pl.BlockSpec(memory_space=pltpu.SMEM)] + [any_spec] * 4,
        out_specs=tuple(pl.BlockSpec(memory_space=pltpu.VMEM) for n in sizes),
        scratch_shapes=[
            pltpu.VMEM((2 * rows, width), jnp.bfloat16),
            pltpu.VMEM((width, chunks * w), jnp.bfloat16),
            pltpu.VMEM((1, bias.shape[0]), jnp.float32),
            pltpu.SemaphoreType.DMA((4,)),
        ],
        compiler_params=pltpu.CompilerParams(vmem_limit_bytes=limit * 1024 * 1024),
        cost_estimate=pl.CostEstimate(
            flops=32 * rows * width * chunks * w,
            bytes_accessed=4 * rows * width + 2 * width * chunks * w,
            transcendentals=0,
        ),
    )(core.astype(jnp.int32).reshape(1), x_own, x_other, weight, bias.reshape(1, -1))


def finish_kernel(hidden, near, got, weight, out):
    total = hidden[...]
    w = near.shape[1]
    total += jnp.dot(near[...], weight[:w], preferred_element_type=jnp.float32)
    total += jnp.dot(got[...], weight[w:], preferred_element_type=jnp.float32)
    total = jnp.maximum(total, 0.0)
    mean = jnp.mean(total * total, axis=1, keepdims=True)
    out[...] = total / jnp.sqrt(mean + 1e-06)


def finish(hidden, near, got, weight):
    rows, width = hidden.shape
    block = 128
    by_row = lambda w: pl.BlockSpec((block, w), lambda i: (i, 0))
    return pl.pallas_call(
        finish_kernel,
        grid=(rows // block,),
        out_shape=jax.ShapeDtypeStruct(hidden.shape, jnp.float32),
        in_specs=[
            by_row(width),
            by_row(near.shape[1]),
            by_row(near.shape[1]),
            pl.BlockSpec(weight.shape, lambda i: (0, 0)),
        ],
        out_specs=by_row(width),
        compiler_params=pltpu.CompilerParams(vmem_limit_bytes=8 * 1024 * 1024),
    )(hidden, near, got, weight)


def local(
    features,
    walk_counts,
    tile_rows,
    tile_cols,
    live_tiles,
    neigh_weight,
    neigh_bias,
    combine_weight,
    combine_bias,
):
    rows_dev, width = features.shape
    tile = walk_counts.shape[3]
    slots = walk_counts.shape[2]
    half = width // 2
    cw = half // CHUNKS
    blocks = rows_dev // tile
    x_lo, y, z, x_hi, core = (lax.axis_index(a) for a in AXES)

    x_other = swap(features, "core", "other_features_0")
    own0 = transform(
        core, features, x_other, neigh_weight, neigh_bias, 0, (1,), tile, cw, 12
    )[0]
    first = swap(own0, "x_lo", "gather_x_0")
    own1, own_rest = transform(
        core,
        after(features, own0),
        x_other,
        neigh_weight,
        neigh_bias,
        cw,
        (1, CHUNKS - 2),
        tile,
        cw,
        14,
    )

    live = live_tiles[0, 0]
    used = jnp.arange(slots, dtype=jnp.int32) < live
    counts = walk_counts[0, 0]
    c_own = jnp.where(used[:, None, None], counts, 0).astype(jnp.bfloat16)
    pair0 = after(jnp.concatenate([own0, after(first, own1)]), own1)
    rows_own = jnp.where(used, tile_rows[0, 0], 0)
    meta = jnp.stack(
        [rows_own, jnp.where(used, tile_cols[0, 0], 0), jnp.full((slots,), live, jnp.int32)]
    )
    c_other = swap(after(c_own, own0), "core", "other_tiles")
    metas = jnp.stack([meta, swap(after(meta, own0), "core", "other_meta")])
    k = metas[:, 1]
    src = (
        (ring_slot((k // 4) % 4, y, core) * 2 + ((k // 16) ^ x_lo)) * 8
        + jnp.arange(2, dtype=jnp.int32)[:, None] * 4
        + k % 4
    ).reshape(-1)
    b = metas[:, 0]
    ring = ring_slot(b // 16, z, core)
    ring = jnp.where(ring == 0, 3, jnp.where(ring == 3, 0, ring))
    dst = (
        ((ring * 2 + 1 - (((b // 8) % 2) ^ x_hi)) * 2)
        + (((b // 4) % 2) ^ core)
    ) * 4 + b % 4
    dst = dst.reshape(-1)
    lives = metas[:, 2, 0]

    row_sums = jnp.concatenate(
        [jnp.sum(c_own.astype(jnp.float32), axis=2), jnp.sum(c_other.astype(jnp.float32), axis=2)]
    )
    onehot = (jnp.arange(64, dtype=jnp.int32)[:, None] == dst[None, :]).astype(jnp.float32)
    deg = jnp.dot(onehot, row_sums, precision=lax.Precision.HIGHEST).astype(jnp.int32)
    parts = (deg[:, None, :] >> (5 * jnp.arange(4, dtype=jnp.int32))[None, :, None]) & 31
    parts = parts.astype(jnp.bfloat16).reshape(256, tile)

    hidden = (
        jnp.dot(features, combine_weight[:width], preferred_element_type=jnp.float32)
        + combine_bias
    )
    w_own = lax.dynamic_slice_in_dim(combine_weight, width + core * half, half, 0)
    w_other = lax.dynamic_slice_in_dim(combine_weight, width + (1 - core) * half, half, 0)

    second = swap(after(own1, first), "x_lo", "gather_x_1")
    f32, bf16 = jnp.float32, jnp.bfloat16
    near_all, far_all, part_all, pass_all, hidden_all = [], [], [], [], []
    scale = None

    def far(pair, got, j):
        near_all.append(jnp.concatenate([pair, got]))
        far_all.append(step(near_all[j], "y", 1, f"gather_far_{j}"))

    far(pair0, step(pair0, "y", 0, "gather_near_0"), 0)
    second = after(second, near_all[0])
    rest = swap(after(own_rest, second), "x_lo", "gather_x_rest")
    size = own0.shape[0]
    split = lambda x: [x[i * size : (i + 1) * size] for i in range(CHUNKS - 2)]
    own = [own0, own1] + split(own_rest)
    partner = [first, second] + split(rest)
    for j in range(1, CHUNKS):
        pair = jnp.concatenate([own[j], partner[j]])
        pair = after(pair, near_all[j - 1], *far_all[: j - 1])
        far(pair, step(pair, "y", 0, f"gather_near_{j}"), j)

    def tiles(j):
        earlier = (rest, near_all[1]) if j == 0 else ()
        if 0 < j < CHUNKS - 1:
            earlier += (near_all[j + 1],)
        if j >= 2:
            earlier += (pass_all[0],)
        with jax.named_scope(f"tiles_{j}"):
            part_all.append(
                tile_sums(
                    after(src, *earlier) if earlier else src,
                    dst,
                    lives,
                    c_own,
                    c_other,
                    parts,
                    j == 0,
                    near_all[j],
                    far_all[j],
                    2**31 if j < 2 else 2**20,
                )
            )

    tiles(0)
    for j in range(CHUNKS):
        send, pass_on, stay = part_all[j]
        size = stay.shape[0] // 2
        got = step(send, "z", 0, f"sum_near_{j}")
        if j == 0:
            tiles(1)
            got = after(got, part_all[1][0])
        else:
            got = after(got, part_all[-1][0])
        passed = (got[: 2 * size].astype(f32) + pass_on.astype(f32)).astype(bf16)
        pass_all.append(passed)
        stay = got[2 * size :].astype(f32) + stay.astype(f32)
        got = step(passed, "z", 1, f"sum_far_{j}")
        if j == 0:
            for i in range(2, CHUNKS):
                tiles(i)
            got = after(got, part_all[-1][0])
        passed = (got[:size].astype(f32) + stay[:size]).astype(bf16)
        stay = got[size:].astype(f32) + stay[size:]
        if j == CHUNKS - 1:
            passed = after(passed, hidden_all[j - 2])
        pooled = swap(passed, "x_hi", f"sum_x_{j}").astype(f32) + stay
        if j == 0:
            deg = jnp.sum(
                pooled[8 * tile :].reshape(8, 4, tile)
                * jnp.array([1, 32, 1024, 32768], f32)[None, :, None],
                axis=1,
            )
            scale = 1.0 / (1.0 + deg)
            pooled = pooled[: 8 * tile]
        factor = after(scale, passed)[..., None]
        mean = (pooled.reshape(8, tile, cw) * factor).astype(bf16)
        mean = mean.reshape(2, rows_dev, cw)
        got = swap(mean[1], "core", f"mean_core_{j}")
        cols = slice(j * cw, (j + 1) * cw)
        if j == CHUNKS - 1:
            weight = jnp.concatenate([w_own[cols], w_other[cols]])
            return finish(hidden, mean[0], got, weight)
        hidden = hidden + jnp.dot(mean[0], w_own[cols], preferred_element_type=f32)
        hidden = hidden + jnp.dot(got, w_other[cols], preferred_element_type=f32)
        hidden_all.append(hidden)


def solution(mesh):
    fine = Mesh(mesh.devices.reshape(SIZES), AXES)
    row = AXES[:2]
    col = AXES[2:]
    return jax.shard_map(
        local,
        mesh=fine,
        in_specs=(
            P(AXES, None),
            P(row, col, None, None, None),
            P(row, col, None),
            P(row, col, None),
            P(row, col),
            P(),
            P(),
            P(),
            P(),
        ),
        out_specs=P(AXES, None),
        check_vma=False,
    )
```

```python
import functools

import jax
import jax.numpy as jnp
from jax import lax
from jax.experimental import pallas as pl
from jax.experimental.pallas import tpu as pltpu
from jax.sharding import Mesh, PartitionSpec as P

AXES = ("x_lo", "y", "z", "x_hi", "core")
SIZES = (2, 4, 4, 2, 2)
CHUNKS = 4
GROUP = 8


def swap(x, axis, name):
    with jax.named_scope(name):
        return lax.ppermute(x, axis, [(0, 1), (1, 0)])


def step(x, axis, second, name):
    pairs = []
    for i in range(4):
        for c in range(2):
            to = i ^ 1 if c == second else 3 - i
            pairs.append((i * 2 + c, to * 2 + c))
    with jax.named_scope(name):
        return lax.ppermute(x, (axis, "core"), pairs)


def after(x, *earlier):
    return lax.optimization_barrier((x, *earlier))[0]


def ring_slot(place, here, core):
    first = jnp.where(core == 0, here ^ 1, 3 - here)
    second = jnp.where(core == 0, 3 - here, here ^ 1)
    return jnp.where(
        place == here, 0, jnp.where(place == first, 1, jnp.where(place == second, 2, 3))
    )


def tile_kernel(src_ref, dst_ref, live_ref, c_own, c_other, pieces_ref, near, far, *refs):
    send, pass_on, stay, acc = refs

    @pl.loop(0, 64)
    def _(i):
        acc[i] = jnp.zeros(acc.shape[1:], jnp.float32)

    slots, tile = c_own.shape[:2]
    for q, counts in enumerate((c_own, c_other)):

        def body(g, carry, q=q, counts=counts):
            terms = []
            for i in range(GROUP):
                s = g * GROUP + i
                at = src_ref[q * slots + s]
                block = lax.select(at < 32, near[at & 31], far[at & 31])
                terms.append(jnp.dot(counts[s], block, preferred_element_type=jnp.float32))
            for i in range(GROUP):
                at = dst_ref[q * slots + g * GROUP + i]
                acc[at] = acc[at] + terms[i]
            return carry

        lax.fori_loop(0, (live_ref[q] + GROUP - 1) // GROUP, body, 0)

    size = stay.shape[0] // 2
    extra = size - 8 * tile
    for part in range(8):
        out = (send, send, send, send, pass_on, pass_on, stay, stay)[part]
        base = (part if part < 4 else part % 2) * size

        @pl.loop(0, 8)
        def _(i, part=part, out=out, base=base):
            at = pl.multiple_of(base + i * tile, 16)
            out[pl.ds(at, tile)] = acc[part * 8 + i].astype(out.dtype)

        if extra:
            out[pl.ds(base + 8 * tile, extra)] = pieces_ref[pl.ds(part * extra, extra)].astype(
                out.dtype
            )


def tile_sums(src, dst, live, c_own, c_other, pieces, with_pieces, near, far, cost):
    tile, w = near.shape[-2:]
    vmem = pl.BlockSpec(memory_space=pltpu.VMEM)
    smem = pl.BlockSpec(memory_space=pltpu.SMEM)
    slots = c_own.shape[0]
    size = 8 * tile + (pieces.shape[0] // 8 if with_pieces else 0)
    return pl.pallas_call(
        tile_kernel,
        out_shape=(
            jax.ShapeDtypeStruct((4 * size, w), jnp.bfloat16),
            jax.ShapeDtypeStruct((2 * size, w), jnp.bfloat16),
            jax.ShapeDtypeStruct((2 * size, w), jnp.bfloat16),
        ),
        in_specs=[smem] * 3 + [vmem] * 5,
        out_specs=(vmem,) * 3,
        scratch_shapes=[pltpu.VMEM((64, tile, w), jnp.float32)],
        compiler_params=pltpu.CompilerParams(vmem_limit_bytes=48 * 1024 * 1024),
        cost_estimate=pl.CostEstimate(
            flops=cost, bytes_accessed=64 * tile * w, transcendentals=0
        ),
    )(src, dst, live, c_own, c_other, pieces, near, far)


def message_kernel(first, core_ref, x_own, x_other, weight, bias, *refs):
    outs, (x, held, row, sems) = refs[:-4], refs[-4:]
    half = weight.shape[1] // 2
    rows, size = x_own.shape[0], held.shape[1]
    tile, w = outs[0].shape[1:]
    at = pl.multiple_of(core_ref[0] * half + first, 128)
    copies = [
        pltpu.make_async_copy(x_own, x.at[pl.ds(0, rows)], sems.at[0]),
        pltpu.make_async_copy(weight.at[:, pl.ds(at, size)], held, sems.at[1]),
        pltpu.make_async_copy(bias, row, sems.at[2]),
        pltpu.make_async_copy(x_other, x.at[pl.ds(rows, rows)], sems.at[3]),
    ]
    for copy in copies:
        copy.start()
    for copy in copies:
        copy.wait()
    blocks = 2 * rows // tile
    chunk = 0
    for out in outs:
        for j in range(out.shape[0] // blocks):
            total = jnp.dot(
                x[...], held[:, chunk * w : (chunk + 1) * w], preferred_element_type=jnp.float32
            )
            total = jnp.maximum(total + row[:, pl.ds(at + chunk * w, w)], 0.0)
            total = total.astype(out.dtype).reshape(blocks, tile, w)
            out[j * blocks : (j + 1) * blocks] = total
            chunk += 1


def transform(core, x_own, x_other, weight, bias, first, sizes, tile, w, limit):
    any_spec = pl.BlockSpec(memory_space=pl.ANY)
    rows, width = x_own.shape
    blocks = 2 * rows // tile
    chunks = sum(sizes)
    return pl.pallas_call(
        functools.partial(message_kernel, first),
        out_shape=tuple(jax.ShapeDtypeStruct((n * blocks, tile, w), jnp.bfloat16) for n in sizes),
        in_specs=[pl.BlockSpec(memory_space=pltpu.SMEM)] + [any_spec] * 4,
        out_specs=tuple(pl.BlockSpec(memory_space=pltpu.VMEM) for n in sizes),
        scratch_shapes=[
            pltpu.VMEM((2 * rows, width), jnp.bfloat16),
            pltpu.VMEM((width, chunks * w), jnp.bfloat16),
            pltpu.VMEM((1, bias.shape[0]), jnp.float32),
            pltpu.SemaphoreType.DMA((4,)),
        ],
        compiler_params=pltpu.CompilerParams(vmem_limit_bytes=limit * 1024 * 1024),
        cost_estimate=pl.CostEstimate(
            flops=32 * rows * width * chunks * w,
            bytes_accessed=4 * rows * width + 2 * width * chunks * w,
            transcendentals=0,
        ),
    )(core.astype(jnp.int32).reshape(1), x_own, x_other, weight, bias.reshape(1, -1))


def finish_kernel(hidden, near, got, weight, out):
    total = hidden[...]
    w = near.shape[1]
    total += jnp.dot(near[...], weight[:w], preferred_element_type=jnp.float32)
    total += jnp.dot(got[...], weight[w:], preferred_element_type=jnp.float32)
    total = jnp.maximum(total, 0.0)
    mean = jnp.mean(total * total, axis=1, keepdims=True)
    out[...] = total / jnp.sqrt(mean + 1e-06)


def finish(hidden, near, got, weight):
    rows, width = hidden.shape
    block = 128
    by_row = lambda w: pl.BlockSpec((block, w), lambda i: (i, 0))
    return pl.pallas_call(
        finish_kernel,
        grid=(rows // block,),
        out_shape=jax.ShapeDtypeStruct(hidden.shape, jnp.float32),
        in_specs=[
            by_row(width),
            by_row(near.shape[1]),
            by_row(near.shape[1]),
            pl.BlockSpec(weight.shape, lambda i: (0, 0)),
        ],
        out_specs=by_row(width),
        compiler_params=pltpu.CompilerParams(vmem_limit_bytes=8 * 1024 * 1024),
    )(hidden, near, got, weight)


def local(
    features,
    walk_counts,
    tile_rows,
    tile_cols,
    live_tiles,
    neigh_weight,
    neigh_bias,
    combine_weight,
    combine_bias,
):
    rows_dev, width = features.shape
    tile = walk_counts.shape[3]
    slots = walk_counts.shape[2]
    half = width // 2
    cw = half // CHUNKS
    blocks = rows_dev // tile
    x_lo, y, z, x_hi, core = (lax.axis_index(a) for a in AXES)

    x_other = swap(features, "core", "other_features_0")
    own0 = transform(
        core, features, x_other, neigh_weight, neigh_bias, 0, (1,), tile, cw, 12
    )[0]
    first = swap(own0, "x_lo", "gather_x_0")
    own1, own_rest = transform(
        core,
        after(features, own0),
        x_other,
        neigh_weight,
        neigh_bias,
        cw,
        (1, CHUNKS - 2),
        tile,
        cw,
        14,
    )

    live = live_tiles[0, 0]
    used = jnp.arange(slots, dtype=jnp.int32) < live
    counts = walk_counts[0, 0]
    c_own = jnp.where(used[:, None, None], counts, 0).astype(jnp.bfloat16)
    pair0 = after(jnp.concatenate([own0, after(first, own1)]), own1)
    rows_own = jnp.where(used, tile_rows[0, 0], 0)
    meta = jnp.stack(
        [rows_own, jnp.where(used, tile_cols[0, 0], 0), jnp.full((slots,), live, jnp.int32)]
    )
    c_other = swap(after(c_own, own0), "core", "other_tiles")
    metas = jnp.stack([meta, swap(after(meta, own0), "core", "other_meta")])
    k = metas[:, 1]
    src = (
        (ring_slot((k // 4) % 4, y, core) * 2 + ((k // 16) ^ x_lo)) * 8
        + jnp.arange(2, dtype=jnp.int32)[:, None] * 4
        + k % 4
    ).reshape(-1)
    b = metas[:, 0]
    ring = ring_slot(b // 16, z, core)
    ring = jnp.where(ring == 0, 3, jnp.where(ring == 3, 0, ring))
    dst = (
        ((ring * 2 + 1 - (((b // 8) % 2) ^ x_hi)) * 2)
        + (((b // 4) % 2) ^ core)
    ) * 4 + b % 4
    dst = dst.reshape(-1)
    lives = metas[:, 2, 0]

    row_sums = jnp.concatenate(
        [jnp.sum(c_own.astype(jnp.float32), axis=2), jnp.sum(c_other.astype(jnp.float32), axis=2)]
    )
    onehot = (jnp.arange(64, dtype=jnp.int32)[:, None] == dst[None, :]).astype(jnp.float32)
    deg = jnp.dot(onehot, row_sums, precision=lax.Precision.HIGHEST).astype(jnp.int32)
    parts = (deg[:, None, :] >> (5 * jnp.arange(4, dtype=jnp.int32))[None, :, None]) & 31
    parts = parts.astype(jnp.bfloat16).reshape(256, tile)

    hidden = (
        jnp.dot(features, combine_weight[:width], preferred_element_type=jnp.float32)
        + combine_bias
    )
    w_own = lax.dynamic_slice_in_dim(combine_weight, width + core * half, half, 0)
    w_other = lax.dynamic_slice_in_dim(combine_weight, width + (1 - core) * half, half, 0)

    second = swap(after(own1, first), "x_lo", "gather_x_1")
    f32, bf16 = jnp.float32, jnp.bfloat16
    near_all, far_all, part_all, pass_all, hidden_all = [], [], [], [], []
    scale = None

    def far(pair, got, j):
        near_all.append(jnp.concatenate([pair, got]))
        far_all.append(step(near_all[j], "y", 1, f"gather_far_{j}"))

    far(pair0, step(pair0, "y", 0, "gather_near_0"), 0)
    second = after(second, near_all[0])
    rest = swap(after(own_rest, second), "x_lo", "gather_x_rest")
    size = own0.shape[0]
    split = lambda x: [x[i * size : (i + 1) * size] for i in range(CHUNKS - 2)]
    own = [own0, own1] + split(own_rest)
    partner = [first, second] + split(rest)
    for j in range(1, CHUNKS):
        pair = jnp.concatenate([own[j], partner[j]])
        pair = after(pair, near_all[j - 1], *far_all[: j - 1])
        far(pair, step(pair, "y", 0, f"gather_near_{j}"), j)

    last = slice((CHUNKS - 1) * cw, CHUNKS * cw)
    last_weight = jnp.concatenate([w_own[last], w_other[last]])

    def tiles(j):
        earlier = (rest, near_all[1], hidden, last_weight) if j == 0 else ()
        if 0 < j < CHUNKS - 1:
            earlier += (near_all[j + 1],)
        if j >= 2:
            earlier += (pass_all[0],)
        with jax.named_scope(f"tiles_{j}"):
            part_all.append(
                tile_sums(
                    after(src, *earlier) if earlier else src,
                    dst,
                    lives,
                    c_own,
                    c_other,
                    parts,
                    j == 0,
                    near_all[j],
                    far_all[j],
                    2**31 if j < 2 else 2**20,
                )
            )

    tiles(0)
    for j in range(CHUNKS):
        send, pass_on, stay = part_all[j]
        size = stay.shape[0] // 2
        got = step(send, "z", 0, f"sum_near_{j}")
        if j == 0:
            tiles(1)
            got = after(got, part_all[1][0])
        else:
            got = after(got, part_all[-1][0])
        passed = (got[: 2 * size].astype(f32) + pass_on.astype(f32)).astype(bf16)
        pass_all.append(passed)
        stay = got[2 * size :].astype(f32) + stay.astype(f32)
        got = step(passed, "z", 1, f"sum_far_{j}")
        if j == 0:
            for i in range(2, CHUNKS):
                tiles(i)
            got = after(got, part_all[-1][0])
        passed = (got[:size].astype(f32) + stay[:size]).astype(bf16)
        stay = got[size:].astype(f32) + stay[size:]
        if j == CHUNKS - 1:
            passed = after(passed, hidden_all[j - 2])
        pooled = swap(passed, "x_hi", f"sum_x_{j}").astype(f32) + stay
        if j == 0:
            deg = jnp.sum(
                pooled[8 * tile :].reshape(8, 4, tile)
                * jnp.array([1, 32, 1024, 32768], f32)[None, :, None],
                axis=1,
            )
            scale = 1.0 / (1.0 + deg)
            pooled = pooled[: 8 * tile]
        factor = after(scale, passed)[..., None]
        mean = (pooled.reshape(8, tile, cw) * factor).astype(bf16)
        mean = mean.reshape(2, rows_dev, cw)
        got = swap(mean[1], "core", f"mean_core_{j}")
        cols = slice(j * cw, (j + 1) * cw)
        if j == CHUNKS - 1:
            return finish(hidden, mean[0], got, last_weight)
        hidden = hidden + jnp.dot(mean[0], w_own[cols], preferred_element_type=f32)
        hidden = hidden + jnp.dot(got, w_other[cols], preferred_element_type=f32)
        hidden_all.append(hidden)


def solution(mesh):
    fine = Mesh(mesh.devices.reshape(SIZES), AXES)
    row = AXES[:2]
    col = AXES[2:]
    return jax.shard_map(
        local,
        mesh=fine,
        in_specs=(
            P(AXES, None),
            P(row, col, None, None, None),
            P(row, col, None),
            P(row, col, None),
            P(row, col),
            P(),
            P(),
            P(),
            P(),
        ),
        out_specs=P(AXES, None),
        check_vma=False,
    )
```

```python
import functools

import jax
import jax.numpy as jnp
from jax import lax
from jax.experimental import pallas as pl
from jax.experimental.pallas import tpu as pltpu
from jax.sharding import Mesh, PartitionSpec as P

AXES = ("x_lo", "y", "z", "x_hi", "core")
SIZES = (2, 4, 4, 2, 2)
CHUNKS = 4
GROUP = 8


def swap(x, axis, name):
    with jax.named_scope(name):
        return lax.ppermute(x, axis, [(0, 1), (1, 0)])


def step(x, axis, second, name):
    pairs = []
    for i in range(4):
        for c in range(2):
            to = i ^ 1 if c == second else 3 - i
            pairs.append((i * 2 + c, to * 2 + c))
    with jax.named_scope(name):
        return lax.ppermute(x, (axis, "core"), pairs)


def after(x, *earlier):
    return lax.optimization_barrier((x, *earlier))[0]


def ring_slot(place, here, core):
    first = jnp.where(core == 0, here ^ 1, 3 - here)
    second = jnp.where(core == 0, 3 - here, here ^ 1)
    return jnp.where(
        place == here, 0, jnp.where(place == first, 1, jnp.where(place == second, 2, 3))
    )


def tile_kernel(src_ref, dst_ref, live_ref, c_own, c_other, pieces_ref, near, far, *refs):
    send, pass_on, stay, acc = refs

    @pl.loop(0, 64)
    def _(i):
        acc[i] = jnp.zeros(acc.shape[1:], jnp.float32)

    slots, tile = c_own.shape[:2]
    for q, counts in enumerate((c_own, c_other)):

        def body(g, carry, q=q, counts=counts):
            terms = []
            for i in range(GROUP):
                s = g * GROUP + i
                at = src_ref[q * slots + s]
                block = lax.select(at < 32, near[at & 31], far[at & 31])
                terms.append(jnp.dot(counts[s], block, preferred_element_type=jnp.float32))
            for i in range(GROUP):
                at = dst_ref[q * slots + g * GROUP + i]
                acc[at] = acc[at] + terms[i]
            return carry

        lax.fori_loop(0, (live_ref[q] + GROUP - 1) // GROUP, body, 0)

    size = stay.shape[0] // 2
    extra = size - 8 * tile
    for part in range(8):
        out = (send, send, send, send, pass_on, pass_on, stay, stay)[part]
        base = (part if part < 4 else part % 2) * size

        @pl.loop(0, 8)
        def _(i, part=part, out=out, base=base):
            at = pl.multiple_of(base + i * tile, 16)
            out[pl.ds(at, tile)] = acc[part * 8 + i].astype(out.dtype)

        if extra:
            out[pl.ds(base + 8 * tile, extra)] = pieces_ref[pl.ds(part * extra, extra)].astype(
                out.dtype
            )


def tile_sums(src, dst, live, c_own, c_other, pieces, with_pieces, near, far, cost):
    tile, w = near.shape[-2:]
    vmem = pl.BlockSpec(memory_space=pltpu.VMEM)
    smem = pl.BlockSpec(memory_space=pltpu.SMEM)
    slots = c_own.shape[0]
    size = 8 * tile + (pieces.shape[0] // 8 if with_pieces else 0)
    return pl.pallas_call(
        tile_kernel,
        out_shape=(
            jax.ShapeDtypeStruct((4 * size, w), jnp.bfloat16),
            jax.ShapeDtypeStruct((2 * size, w), jnp.bfloat16),
            jax.ShapeDtypeStruct((2 * size, w), jnp.bfloat16),
        ),
        in_specs=[smem] * 3 + [vmem] * 5,
        out_specs=(vmem,) * 3,
        scratch_shapes=[pltpu.VMEM((64, tile, w), jnp.float32)],
        compiler_params=pltpu.CompilerParams(vmem_limit_bytes=48 * 1024 * 1024),
        cost_estimate=pl.CostEstimate(
            flops=cost, bytes_accessed=64 * tile * w, transcendentals=0
        ),
    )(src, dst, live, c_own, c_other, pieces, near, far)


def message_kernel(first, core_ref, x_own, x_other, weight, bias, *refs):
    outs, (x, held, row, sems) = refs[:-4], refs[-4:]
    half = weight.shape[1] // 2
    rows, size = x_own.shape[0], held.shape[1]
    tile, w = outs[0].shape[1:]
    at = pl.multiple_of(core_ref[0] * half + first, 128)
    copies = [
        pltpu.make_async_copy(x_own, x.at[pl.ds(0, rows)], sems.at[0]),
        pltpu.make_async_copy(weight.at[:, pl.ds(at, size)], held, sems.at[1]),
        pltpu.make_async_copy(bias, row, sems.at[2]),
        pltpu.make_async_copy(x_other, x.at[pl.ds(rows, rows)], sems.at[3]),
    ]
    for copy in copies:
        copy.start()
    for copy in copies:
        copy.wait()
    blocks = 2 * rows // tile
    chunk = 0
    for out in outs:
        for j in range(out.shape[0] // blocks):
            total = jnp.dot(
                x[...], held[:, chunk * w : (chunk + 1) * w], preferred_element_type=jnp.float32
            )
            total = jnp.maximum(total + row[:, pl.ds(at + chunk * w, w)], 0.0)
            total = total.astype(out.dtype).reshape(blocks, tile, w)
            out[j * blocks : (j + 1) * blocks] = total
            chunk += 1


def transform(core, x_own, x_other, weight, bias, first, sizes, tile, w, limit):
    any_spec = pl.BlockSpec(memory_space=pl.ANY)
    rows, width = x_own.shape
    blocks = 2 * rows // tile
    chunks = sum(sizes)
    return pl.pallas_call(
        functools.partial(message_kernel, first),
        out_shape=tuple(jax.ShapeDtypeStruct((n * blocks, tile, w), jnp.bfloat16) for n in sizes),
        in_specs=[pl.BlockSpec(memory_space=pltpu.SMEM)] + [any_spec] * 4,
        out_specs=tuple(pl.BlockSpec(memory_space=pltpu.VMEM) for n in sizes),
        scratch_shapes=[
            pltpu.VMEM((2 * rows, width), jnp.bfloat16),
            pltpu.VMEM((width, chunks * w), jnp.bfloat16),
            pltpu.VMEM((1, bias.shape[0]), jnp.float32),
            pltpu.SemaphoreType.DMA((4,)),
        ],
        compiler_params=pltpu.CompilerParams(vmem_limit_bytes=limit * 1024 * 1024),
        cost_estimate=pl.CostEstimate(
            flops=32 * rows * width * chunks * w,
            bytes_accessed=4 * rows * width + 2 * width * chunks * w,
            transcendentals=0,
        ),
    )(core.astype(jnp.int32).reshape(1), x_own, x_other, weight, bias.reshape(1, -1))


def finish_kernel(hidden, near, got, weight, out):
    total = hidden[...]
    w = near.shape[1]
    total += jnp.dot(near[...], weight[:w], preferred_element_type=jnp.float32)
    total += jnp.dot(got[...], weight[w:], preferred_element_type=jnp.float32)
    total = jnp.maximum(total, 0.0)
    mean = jnp.mean(total * total, axis=1, keepdims=True)
    out[...] = total / jnp.sqrt(mean + 1e-06)


def finish(hidden, near, got, weight):
    rows, width = hidden.shape
    block = 128
    by_row = lambda w: pl.BlockSpec((block, w), lambda i: (i, 0))
    return pl.pallas_call(
        finish_kernel,
        grid=(rows // block,),
        out_shape=jax.ShapeDtypeStruct(hidden.shape, jnp.float32),
        in_specs=[
            by_row(width),
            by_row(near.shape[1]),
            by_row(near.shape[1]),
            pl.BlockSpec(weight.shape, lambda i: (0, 0)),
        ],
        out_specs=by_row(width),
        compiler_params=pltpu.CompilerParams(vmem_limit_bytes=8 * 1024 * 1024),
    )(hidden, near, got, weight)


def local(
    features,
    walk_counts,
    tile_rows,
    tile_cols,
    live_tiles,
    neigh_weight,
    neigh_bias,
    combine_weight,
    combine_bias,
):
    rows_dev, width = features.shape
    tile = walk_counts.shape[3]
    slots = walk_counts.shape[2]
    half = width // 2
    cw = half // CHUNKS
    blocks = rows_dev // tile
    x_lo, y, z, x_hi, core = (lax.axis_index(a) for a in AXES)

    x_other = swap(features, "core", "other_features_0")
    own0 = transform(
        core, features, x_other, neigh_weight, neigh_bias, 0, (1,), tile, cw, 12
    )[0]
    first = swap(own0, "x_lo", "gather_x_0")
    own1, own_rest = transform(
        core,
        after(features, own0),
        x_other,
        neigh_weight,
        neigh_bias,
        cw,
        (1, CHUNKS - 2),
        tile,
        cw,
        14,
    )

    live = live_tiles[0, 0]
    used = jnp.arange(slots, dtype=jnp.int32) < live
    counts = walk_counts[0, 0]
    c_own = jnp.where(used[:, None, None], counts, 0).astype(jnp.bfloat16)
    pair0 = after(jnp.concatenate([own0, after(first, own1)]), own1)
    rows_own = jnp.where(used, tile_rows[0, 0], 0)
    meta = jnp.stack(
        [rows_own, jnp.where(used, tile_cols[0, 0], 0), jnp.full((slots,), live, jnp.int32)]
    )
    c_other = swap(after(c_own, own0), "core", "other_tiles")
    metas = jnp.stack([meta, swap(after(meta, own0), "core", "other_meta")])
    k = metas[:, 1]
    src = (
        (ring_slot((k // 4) % 4, y, core) * 2 + ((k // 16) ^ x_lo)) * 8
        + jnp.arange(2, dtype=jnp.int32)[:, None] * 4
        + k % 4
    ).reshape(-1)
    b = metas[:, 0]
    ring = ring_slot(b // 16, z, core)
    ring = jnp.where(ring == 0, 3, jnp.where(ring == 3, 0, ring))
    dst = (
        ((ring * 2 + 1 - (((b // 8) % 2) ^ x_hi)) * 2)
        + (((b // 4) % 2) ^ core)
    ) * 4 + b % 4
    dst = dst.reshape(-1)
    lives = metas[:, 2, 0]

    row_sums = jnp.concatenate(
        [jnp.sum(c_own.astype(jnp.float32), axis=2), jnp.sum(c_other.astype(jnp.float32), axis=2)]
    )
    onehot = (jnp.arange(64, dtype=jnp.int32)[:, None] == dst[None, :]).astype(jnp.float32)
    deg = jnp.dot(onehot, row_sums, precision=lax.Precision.HIGHEST).astype(jnp.int32)
    parts = (deg[:, None, :] >> (5 * jnp.arange(4, dtype=jnp.int32))[None, :, None]) & 31
    parts = parts.astype(jnp.bfloat16).reshape(256, tile)

    hidden = (
        jnp.dot(after(features, own0), combine_weight[:width], preferred_element_type=jnp.float32)
        + combine_bias
    )
    later_weight = after(combine_weight, own0)
    w_own = lax.dynamic_slice_in_dim(later_weight, width + core * half, half, 0)
    w_other = lax.dynamic_slice_in_dim(later_weight, width + (1 - core) * half, half, 0)

    second = swap(after(own1, first), "x_lo", "gather_x_1")
    f32, bf16 = jnp.float32, jnp.bfloat16
    near_all, far_all, part_all, pass_all = [], [], [], []
    scale = None

    def far(pair, got, j):
        near_all.append(jnp.concatenate([pair, got]))
        far_all.append(step(near_all[j], "y", 1, f"gather_far_{j}"))

    far(pair0, step(pair0, "y", 0, "gather_near_0"), 0)
    second = after(second, near_all[0])
    rest = swap(after(own_rest, second), "x_lo", "gather_x_rest")
    size = own0.shape[0]
    split = lambda x: [x[i * size : (i + 1) * size] for i in range(CHUNKS - 2)]
    own = [own0, own1] + split(own_rest)
    partner = [first, second] + split(rest)
    for j in range(1, CHUNKS):
        pair = jnp.concatenate([own[j], partner[j]])
        pair = after(pair, near_all[j - 1], *far_all[: j - 1])
        far(pair, step(pair, "y", 0, f"gather_near_{j}"), j)

    cut = (CHUNKS - 2) * cw
    last_weight = jnp.concatenate([w_own[cut:], w_other[cut:]])

    def tiles(j):
        earlier = (rest, near_all[1], hidden, last_weight) if j == 0 else ()
        if 0 < j < CHUNKS - 1:
            earlier += (near_all[j + 1],)
        if j >= 2:
            earlier += (pass_all[0],)
        with jax.named_scope(f"tiles_{j}"):
            part_all.append(
                tile_sums(
                    after(src, *earlier) if earlier else src,
                    dst,
                    lives,
                    c_own,
                    c_other,
                    parts,
                    j == 0,
                    near_all[j],
                    far_all[j],
                    2**31 if j < 2 else 2**20,
                )
            )

    tiles(0)
    stays = []
    for j in range(CHUNKS):
        send, pass_on, stay = part_all[j]
        size = stay.shape[0] // 2
        got = step(send, "z", 0, f"sum_near_{j}")
        if j == 0:
            tiles(1)
        if j + 1 < CHUNKS:
            got = after(got, part_all[j + 1][0])
        passed = (got[: 2 * size].astype(f32) + pass_on.astype(f32)).astype(bf16)
        pass_all.append(passed)
        stays.append(got[2 * size :].astype(f32) + stay.astype(f32))
        if j == 0:
            for i in range(2, CHUNKS):
                tiles(i)

    means = []
    for j in range(CHUNKS):
        stay = stays[j]
        size = stay.shape[0] // 2
        got = step(pass_all[j], "z", 1, f"sum_far_{j}")
        if j == 0:
            got = after(got, part_all[-1][0])
        elif j + 1 < CHUNKS:
            got = after(got, pass_all[j + 1])
        passed = (got[:size].astype(f32) + stay[:size]).astype(bf16)
        stay = got[size:].astype(f32) + stay[size:]
        got = swap(passed, "x_hi", f"sum_x_{j}")
        if j + 2 < CHUNKS:
            got = after(got, pass_all[j + 2])
        pooled = got.astype(f32) + stay
        if j == 0:
            deg = jnp.sum(
                pooled[8 * tile :].reshape(8, 4, tile)
                * jnp.array([1, 32, 1024, 32768], f32)[None, :, None],
                axis=1,
            )
            scale = 1.0 / (1.0 + deg)
            pooled = pooled[: 8 * tile]
        factor = after(scale, passed)[..., None]
        mean = (pooled.reshape(8, tile, cw) * factor).astype(bf16)
        means.append(mean.reshape(2, rows_dev, cw))

    def both_halves(chunks, name):
        near = jnp.concatenate([means[j][0] for j in chunks], axis=1)
        away = jnp.concatenate([means[j][1] for j in chunks], axis=1)
        return near, swap(away, "core", name)

    near, got = both_halves(range(CHUNKS - 2), "mean_core_0")
    hidden = hidden + jnp.dot(near, w_own[:cut], preferred_element_type=f32)
    hidden = hidden + jnp.dot(got, w_other[:cut], preferred_element_type=f32)
    near, got = both_halves(range(CHUNKS - 2, CHUNKS), "mean_core_1")
    return finish(hidden, near, got, last_weight)


def solution(mesh):
    fine = Mesh(mesh.devices.reshape(SIZES), AXES)
    row = AXES[:2]
    col = AXES[2:]
    return jax.shard_map(
        local,
        mesh=fine,
        in_specs=(
            P(AXES, None),
            P(row, col, None, None, None),
            P(row, col, None),
            P(row, col, None),
            P(row, col),
            P(),
            P(),
            P(),
            P(),
        ),
        out_specs=P(AXES, None),
        check_vma=False,
    )
```

```python
import functools

import jax
import jax.numpy as jnp
from jax import lax
from jax.experimental import pallas as pl
from jax.experimental.pallas import tpu as pltpu
from jax.sharding import Mesh, PartitionSpec as P

AXES = ("x_lo", "y", "z", "x_hi", "core")
SIZES = (2, 4, 4, 2, 2)
CHUNKS = 4
GROUP = 8


def swap(x, axis, name):
    with jax.named_scope(name):
        return lax.ppermute(x, axis, [(0, 1), (1, 0)])


def step(x, axis, second, name):
    pairs = []
    for i in range(4):
        for c in range(2):
            to = i ^ 1 if c == second else 3 - i
            pairs.append((i * 2 + c, to * 2 + c))
    with jax.named_scope(name):
        return lax.ppermute(x, (axis, "core"), pairs)


def after(x, *earlier):
    return lax.optimization_barrier((x, *earlier))[0]


def ring_slot(place, here, core):
    first = jnp.where(core == 0, here ^ 1, 3 - here)
    second = jnp.where(core == 0, 3 - here, here ^ 1)
    return jnp.where(
        place == here, 0, jnp.where(place == first, 1, jnp.where(place == second, 2, 3))
    )


def tile_kernel(src_ref, dst_ref, live_ref, c_own, c_other, pieces_ref, near, far, *refs):
    send, pass_on, stay, acc = refs

    @pl.loop(0, 64)
    def _(i):
        acc[i] = jnp.zeros(acc.shape[1:], jnp.float32)

    slots, tile = c_own.shape[:2]
    for q, counts in enumerate((c_own, c_other)):

        def body(g, carry, q=q, counts=counts):
            terms = []
            for i in range(GROUP):
                s = g * GROUP + i
                at = src_ref[q * slots + s]
                block = lax.select(at < 32, near[at & 31], far[at & 31])
                terms.append(jnp.dot(counts[s], block, preferred_element_type=jnp.float32))
            for i in range(GROUP):
                at = dst_ref[q * slots + g * GROUP + i]
                acc[at] = acc[at] + terms[i]
            return carry

        lax.fori_loop(0, (live_ref[q] + GROUP - 1) // GROUP, body, 0)

    size = stay.shape[0] // 2
    extra = size - 8 * tile
    for part in range(8):
        out = (send, send, send, send, pass_on, pass_on, stay, stay)[part]
        base = (part if part < 4 else part % 2) * size

        @pl.loop(0, 8)
        def _(i, part=part, out=out, base=base):
            at = pl.multiple_of(base + i * tile, 16)
            out[pl.ds(at, tile)] = acc[part * 8 + i].astype(out.dtype)

        if extra:
            out[pl.ds(base + 8 * tile, extra)] = pieces_ref[pl.ds(part * extra, extra)].astype(
                out.dtype
            )


def tile_sums(src, dst, live, c_own, c_other, pieces, with_pieces, near, far, cost):
    tile, w = near.shape[-2:]
    vmem = pl.BlockSpec(memory_space=pltpu.VMEM)
    smem = pl.BlockSpec(memory_space=pltpu.SMEM)
    slots = c_own.shape[0]
    size = 8 * tile + (pieces.shape[0] // 8 if with_pieces else 0)
    return pl.pallas_call(
        tile_kernel,
        out_shape=(
            jax.ShapeDtypeStruct((4 * size, w), jnp.bfloat16),
            jax.ShapeDtypeStruct((2 * size, w), jnp.bfloat16),
            jax.ShapeDtypeStruct((2 * size, w), jnp.bfloat16),
        ),
        in_specs=[smem] * 3 + [vmem] * 5,
        out_specs=(vmem,) * 3,
        scratch_shapes=[pltpu.VMEM((64, tile, w), jnp.float32)],
        compiler_params=pltpu.CompilerParams(vmem_limit_bytes=48 * 1024 * 1024),
        cost_estimate=pl.CostEstimate(
            flops=cost, bytes_accessed=64 * tile * w, transcendentals=0
        ),
    )(src, dst, live, c_own, c_other, pieces, near, far)


def message_kernel(first, core_ref, x_own, x_other, weight, bias, *refs):
    outs, (x, held, row, sems) = refs[:-4], refs[-4:]
    half = weight.shape[1] // 2
    rows, size = x_own.shape[0], held.shape[1]
    tile, w = outs[0].shape[1:]
    at = pl.multiple_of(core_ref[0] * half + first, 128)
    copies = [
        pltpu.make_async_copy(x_own, x.at[pl.ds(0, rows)], sems.at[0]),
        pltpu.make_async_copy(weight.at[:, pl.ds(at, size)], held, sems.at[1]),
        pltpu.make_async_copy(bias, row, sems.at[2]),
        pltpu.make_async_copy(x_other, x.at[pl.ds(rows, rows)], sems.at[3]),
    ]
    for copy in copies:
        copy.start()
    for copy in copies:
        copy.wait()
    blocks = 2 * rows // tile
    chunk = 0
    for out in outs:
        for j in range(out.shape[0] // blocks):
            total = jnp.dot(
                x[...], held[:, chunk * w : (chunk + 1) * w], preferred_element_type=jnp.float32
            )
            total = jnp.maximum(total + row[:, pl.ds(at + chunk * w, w)], 0.0)
            total = total.astype(out.dtype).reshape(blocks, tile, w)
            out[j * blocks : (j + 1) * blocks] = total
            chunk += 1


def transform(core, x_own, x_other, weight, bias, first, sizes, tile, w, limit):
    any_spec = pl.BlockSpec(memory_space=pl.ANY)
    rows, width = x_own.shape
    blocks = 2 * rows // tile
    chunks = sum(sizes)
    return pl.pallas_call(
        functools.partial(message_kernel, first),
        out_shape=tuple(jax.ShapeDtypeStruct((n * blocks, tile, w), jnp.bfloat16) for n in sizes),
        in_specs=[pl.BlockSpec(memory_space=pltpu.SMEM)] + [any_spec] * 4,
        out_specs=tuple(pl.BlockSpec(memory_space=pltpu.VMEM) for n in sizes),
        scratch_shapes=[
            pltpu.VMEM((2 * rows, width), jnp.bfloat16),
            pltpu.VMEM((width, chunks * w), jnp.bfloat16),
            pltpu.VMEM((1, bias.shape[0]), jnp.float32),
            pltpu.SemaphoreType.DMA((4,)),
        ],
        compiler_params=pltpu.CompilerParams(vmem_limit_bytes=limit * 1024 * 1024),
        cost_estimate=pl.CostEstimate(
            flops=32 * rows * width * chunks * w,
            bytes_accessed=4 * rows * width + 2 * width * chunks * w,
            transcendentals=0,
        ),
    )(core.astype(jnp.int32).reshape(1), x_own, x_other, weight, bias.reshape(1, -1))


def finish_kernel(hidden, near, got, weight, out):
    total = hidden[...]
    w = near.shape[1]
    total += jnp.dot(near[...], weight[:w], preferred_element_type=jnp.float32)
    total += jnp.dot(got[...], weight[w:], preferred_element_type=jnp.float32)
    total = jnp.maximum(total, 0.0)
    mean = jnp.mean(total * total, axis=1, keepdims=True)
    out[...] = total / jnp.sqrt(mean + 1e-06)


def finish(hidden, near, got, weight):
    rows, width = hidden.shape
    block = 128
    by_row = lambda w: pl.BlockSpec((block, w), lambda i: (i, 0))
    return pl.pallas_call(
        finish_kernel,
        grid=(rows // block,),
        out_shape=jax.ShapeDtypeStruct(hidden.shape, jnp.float32),
        in_specs=[
            by_row(width),
            by_row(near.shape[1]),
            by_row(near.shape[1]),
            pl.BlockSpec(weight.shape, lambda i: (0, 0)),
        ],
        out_specs=by_row(width),
        compiler_params=pltpu.CompilerParams(vmem_limit_bytes=8 * 1024 * 1024),
    )(hidden, near, got, weight)


def local(
    features,
    walk_counts,
    tile_rows,
    tile_cols,
    live_tiles,
    neigh_weight,
    neigh_bias,
    combine_weight,
    combine_bias,
):
    rows_dev, width = features.shape
    tile = walk_counts.shape[3]
    slots = walk_counts.shape[2]
    half = width // 2
    cw = half // CHUNKS
    blocks = rows_dev // tile
    x_lo, y, z, x_hi, core = (lax.axis_index(a) for a in AXES)

    x_other = swap(features, "core", "other_features_0")
    own0 = transform(
        core, features, x_other, neigh_weight, neigh_bias, 0, (1,), tile, cw, 12
    )[0]
    first = swap(own0, "x_lo", "gather_x_0")
    own1, own_rest = transform(
        core,
        after(features, own0),
        x_other,
        neigh_weight,
        neigh_bias,
        cw,
        (1, CHUNKS - 2),
        tile,
        cw,
        14,
    )

    live = live_tiles[0, 0]
    used = jnp.arange(slots, dtype=jnp.int32) < live
    counts = walk_counts[0, 0]
    c_own = jnp.where(used[:, None, None], counts, 0).astype(jnp.bfloat16)
    pair0 = after(jnp.concatenate([own0, after(first, own1)]), own1)
    rows_own = jnp.where(used, tile_rows[0, 0], 0)
    meta = jnp.stack(
        [rows_own, jnp.where(used, tile_cols[0, 0], 0), jnp.full((slots,), live, jnp.int32)]
    )
    c_other = swap(after(c_own, own0), "core", "other_tiles")
    metas = jnp.stack([meta, swap(after(meta, own0), "core", "other_meta")])
    k = metas[:, 1]
    src = (
        (ring_slot((k // 4) % 4, y, core) * 2 + ((k // 16) ^ x_lo)) * 8
        + jnp.arange(2, dtype=jnp.int32)[:, None] * 4
        + k % 4
    ).reshape(-1)
    b = metas[:, 0]
    ring = ring_slot(b // 16, z, core)
    ring = jnp.where(ring == 0, 3, jnp.where(ring == 3, 0, ring))
    dst = (
        ((ring * 2 + 1 - (((b // 8) % 2) ^ x_hi)) * 2)
        + (((b // 4) % 2) ^ core)
    ) * 4 + b % 4
    dst = dst.reshape(-1)
    lives = metas[:, 2, 0]

    row_sums = jnp.concatenate(
        [jnp.sum(c_own.astype(jnp.float32), axis=2), jnp.sum(c_other.astype(jnp.float32), axis=2)]
    )
    onehot = (jnp.arange(64, dtype=jnp.int32)[:, None] == dst[None, :]).astype(jnp.float32)
    deg = jnp.dot(onehot, row_sums, precision=lax.Precision.HIGHEST).astype(jnp.int32)
    parts = (deg[:, None, :] >> (5 * jnp.arange(4, dtype=jnp.int32))[None, :, None]) & 31
    parts = parts.astype(jnp.bfloat16).reshape(256, tile)

    hidden = (
        jnp.dot(after(features, own0), combine_weight[:width], preferred_element_type=jnp.float32)
        + combine_bias
    )
    later_weight = after(combine_weight, own0)
    w_own = lax.dynamic_slice_in_dim(later_weight, width + core * half, half, 0)
    w_other = lax.dynamic_slice_in_dim(later_weight, width + (1 - core) * half, half, 0)

    second = swap(after(own1, first), "x_lo", "gather_x_1")
    f32, bf16 = jnp.float32, jnp.bfloat16
    near_all, far_all, part_all, pass_all = [], [], [], []
    scale = None

    def far(pair, got, j):
        if j == 1:
            got = after(got, parts)
        near_all.append(jnp.concatenate([pair, got]))
        far_all.append(step(near_all[j], "y", 1, f"gather_far_{j}"))

    far(pair0, step(pair0, "y", 0, "gather_near_0"), 0)
    second = after(second, near_all[0])
    rest = swap(after(own_rest, second), "x_lo", "gather_x_rest")
    size = own0.shape[0]
    split = lambda x: [x[i * size : (i + 1) * size] for i in range(CHUNKS - 2)]
    own = [own0, own1] + split(own_rest)
    partner = [first, second] + split(rest)
    for j in range(1, CHUNKS):
        pair = jnp.concatenate([own[j], partner[j]])
        pair = after(pair, near_all[j - 1], *far_all[: j - 1])
        far(pair, step(pair, "y", 0, f"gather_near_{j}"), j)

    cut = (CHUNKS - 2) * cw
    last_weight = jnp.concatenate([w_own[cut:], w_other[cut:]])

    def tiles(j):
        earlier = (rest, near_all[1], hidden, last_weight) if j == 0 else ()
        if 0 < j < CHUNKS - 1:
            earlier += (near_all[j + 1],)
        if j >= 2:
            earlier += (pass_all[0],)
        with jax.named_scope(f"tiles_{j}"):
            part_all.append(
                tile_sums(
                    after(src, *earlier) if earlier else src,
                    dst,
                    lives,
                    c_own,
                    c_other,
                    parts,
                    j == 0,
                    near_all[j],
                    far_all[j],
                    2**31 if j < 2 else 2**20,
                )
            )

    tiles(0)
    stays = []
    for j in range(CHUNKS):
        send, pass_on, stay = part_all[j]
        size = stay.shape[0] // 2
        got = step(send, "z", 0, f"sum_near_{j}")
        if j == 0:
            tiles(1)
        if j + 1 < CHUNKS:
            got = after(got, part_all[j + 1][0])
        passed = (got[: 2 * size].astype(f32) + pass_on.astype(f32)).astype(bf16)
        pass_all.append(passed)
        stays.append(got[2 * size :].astype(f32) + stay.astype(f32))
        if j == 0:
            for i in range(2, CHUNKS):
                tiles(i)

    means = []
    for j in range(CHUNKS):
        stay = stays[j]
        size = stay.shape[0] // 2
        got = step(pass_all[j], "z", 1, f"sum_far_{j}")
        if j == 0:
            got = after(got, part_all[2][0])
        elif j + 1 < CHUNKS:
            got = after(got, pass_all[j + 1])
        passed = (got[:size].astype(f32) + stay[:size]).astype(bf16)
        stay = got[size:].astype(f32) + stay[size:]
        got = swap(passed, "x_hi", f"sum_x_{j}")
        if j + 2 < CHUNKS:
            got = after(got, pass_all[j + 2])
        pooled = got.astype(f32) + stay
        if j == 0:
            deg = jnp.sum(
                pooled[8 * tile :].reshape(8, 4, tile)
                * jnp.array([1, 32, 1024, 32768], f32)[None, :, None],
                axis=1,
            )
            scale = 1.0 / (1.0 + deg)
            pooled = pooled[: 8 * tile]
        factor = after(scale, passed)[..., None]
        mean = (pooled.reshape(8, tile, cw) * factor).astype(bf16)
        means.append(mean.reshape(2, rows_dev, cw))

    def both_halves(chunks, name):
        near = jnp.concatenate([means[j][0] for j in chunks], axis=1)
        away = jnp.concatenate([means[j][1] for j in chunks], axis=1)
        return near, swap(away, "core", name)

    near, got = both_halves(range(CHUNKS - 2), "mean_core_0")
    hidden = hidden + jnp.dot(near, w_own[:cut], preferred_element_type=f32)
    hidden = hidden + jnp.dot(got, w_other[:cut], preferred_element_type=f32)
    near, got = both_halves(range(CHUNKS - 2, CHUNKS), "mean_core_1")
    return finish(hidden, near, got, last_weight)


def solution(mesh):
    fine = Mesh(mesh.devices.reshape(SIZES), AXES)
    row = AXES[:2]
    col = AXES[2:]
    return jax.shard_map(
        local,
        mesh=fine,
        in_specs=(
            P(AXES, None),
            P(row, col, None, None, None),
            P(row, col, None),
            P(row, col, None),
            P(row, col),
            P(),
            P(),
            P(),
            P(),
        ),
        out_specs=P(AXES, None),
        check_vma=False,
    )
```

```python
import functools

import jax
import jax.numpy as jnp
from jax import lax
from jax.experimental import pallas as pl
from jax.experimental.pallas import tpu as pltpu
from jax.sharding import Mesh, PartitionSpec as P

AXES = ("x_lo", "y", "z", "x_hi", "core")
SIZES = (2, 4, 4, 2, 2)
CHUNKS = 4
GROUP = 8


def swap(x, axis, name):
    with jax.named_scope(name):
        return lax.ppermute(x, axis, [(0, 1), (1, 0)])


def step(x, axis, second, name):
    pairs = []
    for i in range(4):
        for c in range(2):
            to = i ^ 1 if c == second else 3 - i
            pairs.append((i * 2 + c, to * 2 + c))
    with jax.named_scope(name):
        return lax.ppermute(x, (axis, "core"), pairs)


def after(x, *earlier):
    return lax.optimization_barrier((x, *earlier))[0]


def ring_slot(place, here, core):
    first = jnp.where(core == 0, here ^ 1, 3 - here)
    second = jnp.where(core == 0, 3 - here, here ^ 1)
    return jnp.where(
        place == here, 0, jnp.where(place == first, 1, jnp.where(place == second, 2, 3))
    )


def tile_kernel(src_ref, dst_ref, live_ref, c_own, c_other, pieces_ref, near, far, *refs):
    send, pass_on, stay, acc = refs

    @pl.loop(0, 64)
    def _(i):
        acc[i] = jnp.zeros(acc.shape[1:], jnp.float32)

    slots, tile = c_own.shape[:2]
    for q, counts in enumerate((c_own, c_other)):

        def body(g, carry, q=q, counts=counts):
            terms = []
            for i in range(GROUP):
                s = g * GROUP + i
                at = src_ref[q * slots + s]
                block = lax.select(at < 32, near[at & 31], far[at & 31])
                terms.append(jnp.dot(counts[s], block, preferred_element_type=jnp.float32))
            for i in range(GROUP):
                at = dst_ref[q * slots + g * GROUP + i]
                acc[at] = acc[at] + terms[i]
            return carry

        lax.fori_loop(0, (live_ref[q] + GROUP - 1) // GROUP, body, 0)

    size = stay.shape[0] // 2
    extra = size - 8 * tile
    for part in range(8):
        out = (send, send, send, send, pass_on, pass_on, stay, stay)[part]
        base = (part if part < 4 else part % 2) * size

        @pl.loop(0, 8)
        def _(i, part=part, out=out, base=base):
            at = pl.multiple_of(base + i * tile, 16)
            out[pl.ds(at, tile)] = acc[part * 8 + i].astype(out.dtype)

        if extra:
            out[pl.ds(base + 8 * tile, extra)] = pieces_ref[pl.ds(part * extra, extra)].astype(
                out.dtype
            )


def tile_sums(src, dst, live, c_own, c_other, pieces, with_pieces, near, far, cost):
    tile, w = near.shape[-2:]
    vmem = pl.BlockSpec(memory_space=pltpu.VMEM)
    smem = pl.BlockSpec(memory_space=pltpu.SMEM)
    slots = c_own.shape[0]
    size = 8 * tile + (pieces.shape[0] // 8 if with_pieces else 0)
    return pl.pallas_call(
        tile_kernel,
        out_shape=(
            jax.ShapeDtypeStruct((4 * size, w), jnp.bfloat16),
            jax.ShapeDtypeStruct((2 * size, w), jnp.bfloat16),
            jax.ShapeDtypeStruct((2 * size, w), jnp.bfloat16),
        ),
        in_specs=[smem] * 3 + [vmem] * 5,
        out_specs=(vmem,) * 3,
        scratch_shapes=[pltpu.VMEM((64, tile, w), jnp.float32)],
        compiler_params=pltpu.CompilerParams(vmem_limit_bytes=48 * 1024 * 1024),
        cost_estimate=pl.CostEstimate(
            flops=cost, bytes_accessed=64 * tile * w, transcendentals=0
        ),
    )(src, dst, live, c_own, c_other, pieces, near, far)


def message_kernel(first, core_ref, x_own, x_other, weight, bias, *refs):
    outs, (x, held, row, sems) = refs[:-4], refs[-4:]
    half = weight.shape[1] // 2
    rows, size = x_own.shape[0], held.shape[1]
    tile, w = outs[0].shape[1:]
    at = pl.multiple_of(core_ref[0] * half + first, 128)
    copies = [
        pltpu.make_async_copy(x_own, x.at[pl.ds(0, rows)], sems.at[0]),
        pltpu.make_async_copy(weight.at[:, pl.ds(at, size)], held, sems.at[1]),
        pltpu.make_async_copy(bias, row, sems.at[2]),
        pltpu.make_async_copy(x_other, x.at[pl.ds(rows, rows)], sems.at[3]),
    ]
    for copy in copies:
        copy.start()
    for copy in copies:
        copy.wait()
    blocks = 2 * rows // tile
    chunk = 0
    for out in outs:
        for j in range(out.shape[0] // blocks):
            total = jnp.dot(
                x[...], held[:, chunk * w : (chunk + 1) * w], preferred_element_type=jnp.float32
            )
            total = jnp.maximum(total + row[:, pl.ds(at + chunk * w, w)], 0.0)
            total = total.astype(out.dtype).reshape(blocks, tile, w)
            out[j * blocks : (j + 1) * blocks] = total
            chunk += 1


def transform(core, x_own, x_other, weight, bias, first, sizes, tile, w, limit):
    any_spec = pl.BlockSpec(memory_space=pl.ANY)
    rows, width = x_own.shape
    blocks = 2 * rows // tile
    chunks = sum(sizes)
    return pl.pallas_call(
        functools.partial(message_kernel, first),
        out_shape=tuple(jax.ShapeDtypeStruct((n * blocks, tile, w), jnp.bfloat16) for n in sizes),
        in_specs=[pl.BlockSpec(memory_space=pltpu.SMEM)] + [any_spec] * 4,
        out_specs=tuple(pl.BlockSpec(memory_space=pltpu.VMEM) for n in sizes),
        scratch_shapes=[
            pltpu.VMEM((2 * rows, width), jnp.bfloat16),
            pltpu.VMEM((width, chunks * w), jnp.bfloat16),
            pltpu.VMEM((1, bias.shape[0]), jnp.float32),
            pltpu.SemaphoreType.DMA((4,)),
        ],
        compiler_params=pltpu.CompilerParams(vmem_limit_bytes=limit * 1024 * 1024),
        cost_estimate=pl.CostEstimate(
            flops=32 * rows * width * chunks * w,
            bytes_accessed=4 * rows * width + 2 * width * chunks * w,
            transcendentals=0,
        ),
    )(core.astype(jnp.int32).reshape(1), x_own, x_other, weight, bias.reshape(1, -1))


def finish_kernel(hidden, near, got, weight, out):
    total = hidden[...]
    w = near.shape[1]
    total += jnp.dot(near[...], weight[:w], preferred_element_type=jnp.float32)
    total += jnp.dot(got[...], weight[w:], preferred_element_type=jnp.float32)
    total = jnp.maximum(total, 0.0)
    mean = jnp.mean(total * total, axis=1, keepdims=True)
    out[...] = total / jnp.sqrt(mean + 1e-06)


def finish(hidden, near, got, weight):
    rows, width = hidden.shape
    block = 128
    by_row = lambda w: pl.BlockSpec((block, w), lambda i: (i, 0))
    return pl.pallas_call(
        finish_kernel,
        grid=(rows // block,),
        out_shape=jax.ShapeDtypeStruct(hidden.shape, jnp.float32),
        in_specs=[
            by_row(width),
            by_row(near.shape[1]),
            by_row(near.shape[1]),
            pl.BlockSpec(weight.shape, lambda i: (0, 0)),
        ],
        out_specs=by_row(width),
        compiler_params=pltpu.CompilerParams(vmem_limit_bytes=8 * 1024 * 1024),
    )(hidden, near, got, weight)


def local(
    features,
    walk_counts,
    tile_rows,
    tile_cols,
    live_tiles,
    neigh_weight,
    neigh_bias,
    combine_weight,
    combine_bias,
):
    rows_dev, width = features.shape
    tile = walk_counts.shape[3]
    slots = walk_counts.shape[2]
    half = width // 2
    cw = half // CHUNKS
    blocks = rows_dev // tile
    x_lo, y, z, x_hi, core = (lax.axis_index(a) for a in AXES)

    x_other = swap(features, "core", "other_features_0")
    own0 = transform(
        core, features, x_other, neigh_weight, neigh_bias, 0, (1,), tile, cw, 12
    )[0]
    first = swap(own0, "x_lo", "gather_x_0")
    own1, own_rest = transform(
        core,
        after(features, own0),
        x_other,
        neigh_weight,
        neigh_bias,
        cw,
        (1, CHUNKS - 2),
        tile,
        cw,
        14,
    )

    live = live_tiles[0, 0]
    used = jnp.arange(slots, dtype=jnp.int32) < live
    counts = walk_counts[0, 0]
    c_own = jnp.where(used[:, None, None], counts, 0).astype(jnp.bfloat16)
    pair0 = after(jnp.concatenate([own0, after(first, own1)]), own1)
    rows_own = jnp.where(used, tile_rows[0, 0], 0)
    meta = jnp.stack(
        [rows_own, jnp.where(used, tile_cols[0, 0], 0), jnp.full((slots,), live, jnp.int32)]
    )
    c_other = swap(after(c_own, own0), "core", "other_tiles")
    metas = jnp.stack([meta, swap(after(meta, own0), "core", "other_meta")])
    k = metas[:, 1]
    src = (
        (ring_slot((k // 4) % 4, y, core) * 2 + ((k // 16) ^ x_lo)) * 8
        + jnp.arange(2, dtype=jnp.int32)[:, None] * 4
        + k % 4
    ).reshape(-1)
    b = metas[:, 0]
    ring = ring_slot(b // 16, z, core)
    ring = jnp.where(ring == 0, 3, jnp.where(ring == 3, 0, ring))
    dst = (
        ((ring * 2 + 1 - (((b // 8) % 2) ^ x_hi)) * 2)
        + (((b // 4) % 2) ^ core)
    ) * 4 + b % 4
    dst = dst.reshape(-1)
    lives = metas[:, 2, 0]

    row_sums = jnp.concatenate(
        [jnp.sum(c_own.astype(jnp.float32), axis=2), jnp.sum(c_other.astype(jnp.float32), axis=2)]
    )
    onehot = (jnp.arange(64, dtype=jnp.int32)[:, None] == dst[None, :]).astype(jnp.float32)
    deg = jnp.dot(onehot, row_sums, precision=lax.Precision.HIGHEST).astype(jnp.int32)
    parts = (deg[:, None, :] >> (5 * jnp.arange(4, dtype=jnp.int32))[None, :, None]) & 31
    parts = parts.astype(jnp.bfloat16).reshape(256, tile)

    hidden = (
        jnp.dot(after(features, own0), combine_weight[:width], preferred_element_type=jnp.float32)
        + combine_bias
    )
    later_weight = after(combine_weight, own0)
    w_own = lax.dynamic_slice_in_dim(later_weight, width + core * half, half, 0)
    w_other = lax.dynamic_slice_in_dim(later_weight, width + (1 - core) * half, half, 0)

    second = swap(after(own1, first), "x_lo", "gather_x_1")
    f32, bf16 = jnp.float32, jnp.bfloat16
    near_all, far_all, part_all, pass_all = [], [], [], []
    scale = None

    def far(pair, got, j):
        if j == 1:
            got = after(got, parts)
        near_all.append(jnp.concatenate([pair, got]))
        far_all.append(step(near_all[j], "y", 1, f"gather_far_{j}"))

    far(pair0, step(pair0, "y", 0, "gather_near_0"), 0)
    second = after(second, near_all[0])
    rest = swap(after(own_rest, second), "x_lo", "gather_x_rest")
    size = own0.shape[0]
    split = lambda x: [x[i * size : (i + 1) * size] for i in range(CHUNKS - 2)]
    own = [own0, own1] + split(own_rest)
    partner = [first, second] + split(rest)
    for j in range(1, CHUNKS):
        pair = jnp.concatenate([own[j], partner[j]])
        pair = after(pair, near_all[j - 1], *far_all[: j - 1])
        far(pair, step(pair, "y", 0, f"gather_near_{j}"), j)

    cut = (CHUNKS - 2) * cw
    last_weight = jnp.concatenate([w_own[cut:], w_other[cut:]])

    def tiles(j):
        earlier = (rest, near_all[1], hidden, last_weight) if j == 0 else ()
        if j == 1:
            earlier += (near_all[j + 1],)
        if j >= 2:
            earlier += (pass_all[0],)
        with jax.named_scope(f"tiles_{j}"):
            part_all.append(
                tile_sums(
                    after(src, *earlier) if earlier else src,
                    dst,
                    lives,
                    c_own,
                    c_other,
                    parts,
                    j == 0,
                    near_all[j],
                    far_all[j],
                    2**34 if j == 1 else 2**31 if j == 0 else 2**20,
                )
            )

    tiles(0)
    stays = []
    for j in range(CHUNKS):
        send, pass_on, stay = part_all[j]
        size = stay.shape[0] // 2
        got = step(send, "z", 0, f"sum_near_{j}")
        if j == 0:
            tiles(1)
        if j + 1 < CHUNKS:
            got = after(got, part_all[j + 1][0])
        passed = (got[: 2 * size].astype(f32) + pass_on.astype(f32)).astype(bf16)
        pass_all.append(passed)
        stays.append(got[2 * size :].astype(f32) + stay.astype(f32))
        if j == 0:
            for i in range(2, CHUNKS):
                tiles(i)

    means = []
    for j in range(CHUNKS):
        stay = stays[j]
        size = stay.shape[0] // 2
        got = step(pass_all[j], "z", 1, f"sum_far_{j}")
        if j == 0:
            got = after(got, part_all[2][0])
        elif j + 1 < CHUNKS:
            got = after(got, pass_all[j + 1])
        passed = (got[:size].astype(f32) + stay[:size]).astype(bf16)
        stay = got[size:].astype(f32) + stay[size:]
        got = swap(passed, "x_hi", f"sum_x_{j}")
        if j + 2 < CHUNKS:
            got = after(got, pass_all[j + 2])
        pooled = got.astype(f32) + stay
        if j == 0:
            deg = jnp.sum(
                pooled[8 * tile :].reshape(8, 4, tile)
                * jnp.array([1, 32, 1024, 32768], f32)[None, :, None],
                axis=1,
            )
            scale = 1.0 / (1.0 + deg)
            pooled = pooled[: 8 * tile]
        factor = after(scale, passed)[..., None]
        mean = (pooled.reshape(8, tile, cw) * factor).astype(bf16)
        means.append(mean.reshape(2, rows_dev, cw))

    def both_halves(chunks, name):
        near = jnp.concatenate([means[j][0] for j in chunks], axis=1)
        away = jnp.concatenate([means[j][1] for j in chunks], axis=1)
        return near, swap(away, "core", name)

    near, got = both_halves(range(CHUNKS - 2), "mean_core_0")
    hidden = hidden + jnp.dot(near, w_own[:cut], preferred_element_type=f32)
    hidden = hidden + jnp.dot(got, w_other[:cut], preferred_element_type=f32)
    near, got = both_halves(range(CHUNKS - 2, CHUNKS), "mean_core_1")
    return finish(hidden, near, got, last_weight)


def solution(mesh):
    fine = Mesh(mesh.devices.reshape(SIZES), AXES)
    row = AXES[:2]
    col = AXES[2:]
    return jax.shard_map(
        local,
        mesh=fine,
        in_specs=(
            P(AXES, None),
            P(row, col, None, None, None),
            P(row, col, None),
            P(row, col, None),
            P(row, col),
            P(),
            P(),
            P(),
            P(),
        ),
        out_specs=P(AXES, None),
        check_vma=False,
    )
```

```python
import functools

import jax
import jax.numpy as jnp
from jax import lax
from jax.experimental import pallas as pl
from jax.experimental.pallas import tpu as pltpu
from jax.sharding import Mesh, PartitionSpec as P

AXES = ("x_lo", "y", "z", "x_hi", "core")
SIZES = (2, 4, 4, 2, 2)
CHUNKS = 4
GROUP = 8


def swap(x, axis, name):
    with jax.named_scope(name):
        return lax.ppermute(x, axis, [(0, 1), (1, 0)])


def step(x, axis, second, name):
    pairs = []
    for i in range(4):
        for c in range(2):
            to = i ^ 1 if c == second else 3 - i
            pairs.append((i * 2 + c, to * 2 + c))
    with jax.named_scope(name):
        return lax.ppermute(x, (axis, "core"), pairs)


def after(x, *earlier):
    return lax.optimization_barrier((x, *earlier))[0]


def ring_slot(place, here, core):
    first = jnp.where(core == 0, here ^ 1, 3 - here)
    second = jnp.where(core == 0, 3 - here, here ^ 1)
    return jnp.where(
        place == here, 0, jnp.where(place == first, 1, jnp.where(place == second, 2, 3))
    )


def tile_kernel(src_ref, dst_ref, live_ref, c_own, c_other, pieces_ref, near, far, *refs):
    send, pass_on, stay, acc = refs

    @pl.loop(0, 64)
    def _(i):
        acc[i] = jnp.zeros(acc.shape[1:], jnp.float32)

    slots, tile = c_own.shape[:2]
    for q, counts in enumerate((c_own, c_other)):

        def body(g, carry, q=q, counts=counts):
            terms = []
            for i in range(GROUP):
                s = g * GROUP + i
                at = src_ref[q * slots + s]
                block = lax.select(at < 32, near[at & 31], far[at & 31])
                terms.append(jnp.dot(counts[s], block, preferred_element_type=jnp.float32))
            for i in range(GROUP):
                at = dst_ref[q * slots + g * GROUP + i]
                acc[at] = acc[at] + terms[i]
            return carry

        lax.fori_loop(0, (live_ref[q] + GROUP - 1) // GROUP, body, 0)

    size = stay.shape[0] // 2
    extra = size - 8 * tile
    for part in range(8):
        out = (send, send, send, send, pass_on, pass_on, stay, stay)[part]
        base = (part if part < 4 else part % 2) * size

        @pl.loop(0, 8)
        def _(i, part=part, out=out, base=base):
            at = pl.multiple_of(base + i * tile, 16)
            out[pl.ds(at, tile)] = acc[part * 8 + i].astype(out.dtype)

        if extra:
            out[pl.ds(base + 8 * tile, extra)] = pieces_ref[pl.ds(part * extra, extra)].astype(
                out.dtype
            )


def tile_sums(src, dst, live, c_own, c_other, pieces, with_pieces, near, far, cost):
    tile, w = near.shape[-2:]
    vmem = pl.BlockSpec(memory_space=pltpu.VMEM)
    smem = pl.BlockSpec(memory_space=pltpu.SMEM)
    slots = c_own.shape[0]
    size = 8 * tile + (pieces.shape[0] // 8 if with_pieces else 0)
    return pl.pallas_call(
        tile_kernel,
        out_shape=(
            jax.ShapeDtypeStruct((4 * size, w), jnp.bfloat16),
            jax.ShapeDtypeStruct((2 * size, w), jnp.bfloat16),
            jax.ShapeDtypeStruct((2 * size, w), jnp.bfloat16),
        ),
        in_specs=[smem] * 3 + [vmem] * 5,
        out_specs=(vmem,) * 3,
        scratch_shapes=[pltpu.VMEM((64, tile, w), jnp.float32)],
        compiler_params=pltpu.CompilerParams(vmem_limit_bytes=48 * 1024 * 1024),
        cost_estimate=pl.CostEstimate(
            flops=cost, bytes_accessed=64 * tile * w, transcendentals=0
        ),
    )(src, dst, live, c_own, c_other, pieces, near, far)


def message_kernel(first, core_ref, x_own, x_other, weight, bias, *refs):
    outs, (x, held, row, sems) = refs[:-4], refs[-4:]
    half = weight.shape[1] // 2
    rows, size = x_own.shape[0], held.shape[1]
    tile, w = outs[0].shape[1:]
    at = pl.multiple_of(core_ref[0] * half + first, 128)
    copies = [
        pltpu.make_async_copy(x_own, x.at[pl.ds(0, rows)], sems.at[0]),
        pltpu.make_async_copy(weight.at[:, pl.ds(at, size)], held, sems.at[1]),
        pltpu.make_async_copy(bias, row, sems.at[2]),
        pltpu.make_async_copy(x_other, x.at[pl.ds(rows, rows)], sems.at[3]),
    ]
    for copy in copies:
        copy.start()
    for copy in copies:
        copy.wait()
    blocks = 2 * rows // tile
    chunk = 0
    for out in outs:
        for j in range(out.shape[0] // blocks):
            total = jnp.dot(
                x[...], held[:, chunk * w : (chunk + 1) * w], preferred_element_type=jnp.float32
            )
            total = jnp.maximum(total + row[:, pl.ds(at + chunk * w, w)], 0.0)
            total = total.astype(out.dtype).reshape(blocks, tile, w)
            out[j * blocks : (j + 1) * blocks] = total
            chunk += 1


def transform(core, x_own, x_other, weight, bias, first, sizes, tile, w, limit):
    any_spec = pl.BlockSpec(memory_space=pl.ANY)
    rows, width = x_own.shape
    blocks = 2 * rows // tile
    chunks = sum(sizes)
    return pl.pallas_call(
        functools.partial(message_kernel, first),
        out_shape=tuple(jax.ShapeDtypeStruct((n * blocks, tile, w), jnp.bfloat16) for n in sizes),
        in_specs=[pl.BlockSpec(memory_space=pltpu.SMEM)] + [any_spec] * 4,
        out_specs=tuple(pl.BlockSpec(memory_space=pltpu.VMEM) for n in sizes),
        scratch_shapes=[
            pltpu.VMEM((2 * rows, width), jnp.bfloat16),
            pltpu.VMEM((width, chunks * w), jnp.bfloat16),
            pltpu.VMEM((1, bias.shape[0]), jnp.float32),
            pltpu.SemaphoreType.DMA((4,)),
        ],
        compiler_params=pltpu.CompilerParams(vmem_limit_bytes=limit * 1024 * 1024),
        cost_estimate=pl.CostEstimate(
            flops=32 * rows * width * chunks * w,
            bytes_accessed=4 * rows * width + 2 * width * chunks * w,
            transcendentals=0,
        ),
    )(core.astype(jnp.int32).reshape(1), x_own, x_other, weight, bias.reshape(1, -1))


def finish_kernel(hidden, near, got, weight, out):
    total = hidden[...]
    w = near.shape[1]
    total += jnp.dot(near[...], weight[:w], preferred_element_type=jnp.float32)
    total += jnp.dot(got[...], weight[w:], preferred_element_type=jnp.float32)
    total = jnp.maximum(total, 0.0)
    mean = jnp.mean(total * total, axis=1, keepdims=True)
    out[...] = total / jnp.sqrt(mean + 1e-06)


def finish(hidden, near, got, weight):
    rows, width = hidden.shape
    block = 128
    by_row = lambda w: pl.BlockSpec((block, w), lambda i: (i, 0))
    return pl.pallas_call(
        finish_kernel,
        grid=(rows // block,),
        out_shape=jax.ShapeDtypeStruct(hidden.shape, jnp.float32),
        in_specs=[
            by_row(width),
            by_row(near.shape[1]),
            by_row(near.shape[1]),
            pl.BlockSpec(weight.shape, lambda i: (0, 0)),
        ],
        out_specs=by_row(width),
        compiler_params=pltpu.CompilerParams(vmem_limit_bytes=8 * 1024 * 1024),
    )(hidden, near, got, weight)


def local(
    features,
    walk_counts,
    tile_rows,
    tile_cols,
    live_tiles,
    neigh_weight,
    neigh_bias,
    combine_weight,
    combine_bias,
):
    rows_dev, width = features.shape
    tile = walk_counts.shape[3]
    slots = walk_counts.shape[2]
    half = width // 2
    cw = half // CHUNKS
    blocks = rows_dev // tile
    x_lo, y, z, x_hi, core = (lax.axis_index(a) for a in AXES)

    x_other = swap(features, "core", "other_features_0")
    own0 = transform(
        core, features, x_other, neigh_weight, neigh_bias, 0, (1,), tile, cw, 12
    )[0]
    first = swap(own0, "x_lo", "gather_x_0")
    own1, own_rest = transform(
        core,
        after(features, own0),
        x_other,
        neigh_weight,
        neigh_bias,
        cw,
        (1, CHUNKS - 2),
        tile,
        cw,
        14,
    )

    live = live_tiles[0, 0]
    used = jnp.arange(slots, dtype=jnp.int32) < live
    counts = walk_counts[0, 0]
    c_own = jnp.where(used[:, None, None], counts, 0).astype(jnp.bfloat16)
    pair0 = after(jnp.concatenate([own0, after(first, own1)]), own1)
    rows_own = jnp.where(used, tile_rows[0, 0], 0)
    meta = jnp.stack(
        [rows_own, jnp.where(used, tile_cols[0, 0], 0), jnp.full((slots,), live, jnp.int32)]
    )
    c_other = swap(after(c_own, own0), "core", "other_tiles")
    metas = jnp.stack([meta, swap(after(meta, own0), "core", "other_meta")])
    k = metas[:, 1]
    src = (
        (ring_slot((k // 4) % 4, y, core) * 2 + ((k // 16) ^ x_lo)) * 8
        + jnp.arange(2, dtype=jnp.int32)[:, None] * 4
        + k % 4
    ).reshape(-1)
    b = metas[:, 0]
    ring = ring_slot(b // 16, z, core)
    ring = jnp.where(ring == 0, 3, jnp.where(ring == 3, 0, ring))
    dst = (
        ((ring * 2 + 1 - (((b // 8) % 2) ^ x_hi)) * 2)
        + (((b // 4) % 2) ^ core)
    ) * 4 + b % 4
    dst = dst.reshape(-1)
    lives = metas[:, 2, 0]

    row_sums = jnp.concatenate(
        [jnp.sum(c_own.astype(jnp.float32), axis=2), jnp.sum(c_other.astype(jnp.float32), axis=2)]
    )
    onehot = (jnp.arange(64, dtype=jnp.int32)[:, None] == dst[None, :]).astype(jnp.float32)
    deg = jnp.dot(onehot, row_sums, precision=lax.Precision.HIGHEST).astype(jnp.int32)
    parts = (deg[:, None, :] >> (5 * jnp.arange(4, dtype=jnp.int32))[None, :, None]) & 31
    parts = parts.astype(jnp.bfloat16).reshape(256, tile)

    hidden = (
        jnp.dot(after(features, own0), combine_weight[:width], preferred_element_type=jnp.float32)
        + combine_bias
    )
    later_weight = after(combine_weight, own0)
    w_own = lax.dynamic_slice_in_dim(later_weight, width + core * half, half, 0)
    w_other = lax.dynamic_slice_in_dim(later_weight, width + (1 - core) * half, half, 0)

    second = swap(after(own1, first), "x_lo", "gather_x_1")
    f32, bf16 = jnp.float32, jnp.bfloat16
    near_all, far_all, part_all, pass_all = [], [], [], []
    scale = None

    def far(pair, got, j):
        if j == 1:
            got = after(got, parts)
        near_all.append(jnp.concatenate([pair, got]))
        far_all.append(step(near_all[j], "y", 1, f"gather_far_{j}"))

    far(pair0, step(pair0, "y", 0, "gather_near_0"), 0)
    second = after(second, near_all[0])
    rest = swap(after(own_rest, second), "x_lo", "gather_x_rest")
    size = own0.shape[0]
    split = lambda x: [x[i * size : (i + 1) * size] for i in range(CHUNKS - 2)]
    own = [own0, own1] + split(own_rest)
    partner = [first, second] + split(rest)
    for j in range(1, CHUNKS):
        pair = jnp.concatenate([own[j], partner[j]])
        pair = after(pair, near_all[j - 1], *far_all[: j - 1])
        far(pair, step(pair, "y", 0, f"gather_near_{j}"), j)

    cut = (CHUNKS - 2) * cw
    last_weight = jnp.concatenate([w_own[cut:], w_other[cut:]])

    def tiles(j):
        earlier = (rest, near_all[1], hidden, last_weight) if j == 0 else ()
        if j == 1:
            earlier += (near_all[j + 1],)
        if j >= 2:
            earlier += (pass_all[0],)
        with jax.named_scope(f"tiles_{j}"):
            part_all.append(
                tile_sums(
                    after(src, *earlier) if earlier else src,
                    dst,
                    lives,
                    c_own,
                    c_other,
                    parts,
                    j == 0,
                    near_all[j],
                    far_all[j],
                    2**34 if j == 1 else 2**31 if j == 0 else 2**20,
                )
            )

    tiles(0)
    stays = []
    for j in range(CHUNKS):
        send, pass_on, stay = part_all[j]
        size = stay.shape[0] // 2
        got = step(send, "z", 0, f"sum_near_{j}")
        if j == 0:
            tiles(1)
        if j + 1 < CHUNKS:
            got = after(got, part_all[j + 1][0])
        passed = (got[: 2 * size].astype(f32) + pass_on.astype(f32)).astype(bf16)
        pass_all.append(passed)
        stays.append(got[2 * size :].astype(f32) + stay.astype(f32))
        if j == 0:
            for i in range(2, CHUNKS):
                tiles(i)

    means, ready = [], []
    for j in range(CHUNKS):
        stay = stays[j]
        size = stay.shape[0] // 2
        got = step(pass_all[j], "z", 1, f"sum_far_{j}")
        if j == 0:
            got = after(got, part_all[2][0])
        elif j + 1 < CHUNKS:
            got = after(got, pass_all[j + 1])
        passed = (got[:size].astype(f32) + stay[:size]).astype(bf16)
        ready.append((passed, got[size:].astype(f32) + stay[size:]))

    for j, (passed, stay) in enumerate(ready):
        got = swap(passed, "x_hi", f"sum_x_{j}")
        if j + 2 < CHUNKS:
            got = after(got, pass_all[j + 2])
        elif j + 1 < CHUNKS:
            got = after(got, ready[j + 1][0])
        pooled = got.astype(f32) + stay
        if j == 0:
            deg = jnp.sum(
                pooled[8 * tile :].reshape(8, 4, tile)
                * jnp.array([1, 32, 1024, 32768], f32)[None, :, None],
                axis=1,
            )
            scale = 1.0 / (1.0 + deg)
            pooled = pooled[: 8 * tile]
        factor = after(scale, passed)[..., None]
        mean = (pooled.reshape(8, tile, cw) * factor).astype(bf16)
        means.append(mean.reshape(2, rows_dev, cw))

    def both_halves(chunks, name):
        near = jnp.concatenate([means[j][0] for j in chunks], axis=1)
        away = jnp.concatenate([means[j][1] for j in chunks], axis=1)
        return near, swap(away, "core", name)

    near, got = both_halves(range(CHUNKS - 2), "mean_core_0")
    hidden = hidden + jnp.dot(near, w_own[:cut], preferred_element_type=f32)
    hidden = hidden + jnp.dot(got, w_other[:cut], preferred_element_type=f32)
    near, got = both_halves(range(CHUNKS - 2, CHUNKS), "mean_core_1")
    return finish(hidden, near, got, last_weight)


def solution(mesh):
    fine = Mesh(mesh.devices.reshape(SIZES), AXES)
    row = AXES[:2]
    col = AXES[2:]
    return jax.shard_map(
        local,
        mesh=fine,
        in_specs=(
            P(AXES, None),
            P(row, col, None, None, None),
            P(row, col, None),
            P(row, col, None),
            P(row, col),
            P(),
            P(),
            P(),
            P(),
        ),
        out_specs=P(AXES, None),
        check_vma=False,
    )
```

```python
import functools

import jax
import jax.numpy as jnp
from jax import lax
from jax.experimental import pallas as pl
from jax.experimental.pallas import tpu as pltpu
from jax.sharding import Mesh, PartitionSpec as P

AXES = ("x_lo", "y", "z", "x_hi", "core")
SIZES = (2, 4, 4, 2, 2)
CHUNKS = 4
GROUP = 4


def swap(x, axis, name):
    with jax.named_scope(name):
        return lax.ppermute(x, axis, [(0, 1), (1, 0)])


def step(x, axis, second, name):
    pairs = []
    for i in range(4):
        for c in range(2):
            to = i ^ 1 if c == second else 3 - i
            pairs.append((i * 2 + c, to * 2 + c))
    with jax.named_scope(name):
        return lax.ppermute(x, (axis, "core"), pairs)


def after(x, *earlier):
    return lax.optimization_barrier((x, *earlier))[0]


def ring_slot(place, here, core):
    first = jnp.where(core == 0, here ^ 1, 3 - here)
    second = jnp.where(core == 0, 3 - here, here ^ 1)
    return jnp.where(
        place == here, 0, jnp.where(place == first, 1, jnp.where(place == second, 2, 3))
    )


def tile_kernel(src_ref, dst_ref, live_ref, c_own, c_other, pieces_ref, near, far, *refs):
    send, pass_on, stay, acc = refs

    @pl.loop(0, 64)
    def _(i):
        acc[i] = jnp.zeros(acc.shape[1:], jnp.float32)

    slots, tile = c_own.shape[:2]
    for q, counts in enumerate((c_own, c_other)):

        def body(g, carry, q=q, counts=counts):
            terms = []
            for i in range(GROUP):
                s = g * GROUP + i
                at = src_ref[q * slots + s]
                block = lax.select(at < 32, near[at & 31], far[at & 31])
                terms.append(jnp.dot(counts[s], block, preferred_element_type=jnp.float32))
            for i in range(GROUP):
                at = dst_ref[q * slots + g * GROUP + i]
                acc[at] = acc[at] + terms[i]
            return carry

        lax.fori_loop(0, (live_ref[q] + GROUP - 1) // GROUP, body, 0)

    size = stay.shape[0] // 2
    extra = size - 8 * tile
    for part in range(8):
        out = (send, send, send, send, pass_on, pass_on, stay, stay)[part]
        base = (part if part < 4 else part % 2) * size

        @pl.loop(0, 8)
        def _(i, part=part, out=out, base=base):
            at = pl.multiple_of(base + i * tile, 16)
            out[pl.ds(at, tile)] = acc[part * 8 + i].astype(out.dtype)

        if extra:
            out[pl.ds(base + 8 * tile, extra)] = pieces_ref[pl.ds(part * extra, extra)].astype(
                out.dtype
            )


def tile_sums(src, dst, live, c_own, c_other, pieces, with_pieces, near, far, cost):
    tile, w = near.shape[-2:]
    vmem = pl.BlockSpec(memory_space=pltpu.VMEM)
    smem = pl.BlockSpec(memory_space=pltpu.SMEM)
    slots = c_own.shape[0]
    size = 8 * tile + (pieces.shape[0] // 8 if with_pieces else 0)
    return pl.pallas_call(
        tile_kernel,
        out_shape=(
            jax.ShapeDtypeStruct((4 * size, w), jnp.bfloat16),
            jax.ShapeDtypeStruct((2 * size, w), jnp.bfloat16),
            jax.ShapeDtypeStruct((2 * size, w), jnp.bfloat16),
        ),
        in_specs=[smem] * 3 + [vmem] * 5,
        out_specs=(vmem,) * 3,
        scratch_shapes=[pltpu.VMEM((64, tile, w), jnp.float32)],
        compiler_params=pltpu.CompilerParams(vmem_limit_bytes=48 * 1024 * 1024),
        cost_estimate=pl.CostEstimate(
            flops=cost, bytes_accessed=64 * tile * w, transcendentals=0
        ),
    )(src, dst, live, c_own, c_other, pieces, near, far)


def message_kernel(first, core_ref, x_own, x_other, weight, bias, *refs):
    outs, (x, held, row, sems) = refs[:-4], refs[-4:]
    half = weight.shape[1] // 2
    rows, size = x_own.shape[0], held.shape[1]
    tile, w = outs[0].shape[1:]
    at = pl.multiple_of(core_ref[0] * half + first, 128)
    copies = [
        pltpu.make_async_copy(x_own, x.at[pl.ds(0, rows)], sems.at[0]),
        pltpu.make_async_copy(weight.at[:, pl.ds(at, size)], held, sems.at[1]),
        pltpu.make_async_copy(bias, row, sems.at[2]),
        pltpu.make_async_copy(x_other, x.at[pl.ds(rows, rows)], sems.at[3]),
    ]
    for copy in copies:
        copy.start()
    for copy in copies:
        copy.wait()
    blocks = 2 * rows // tile
    chunk = 0
    for out in outs:
        for j in range(out.shape[0] // blocks):
            total = jnp.dot(
                x[...], held[:, chunk * w : (chunk + 1) * w], preferred_element_type=jnp.float32
            )
            total = jnp.maximum(total + row[:, pl.ds(at + chunk * w, w)], 0.0)
            total = total.astype(out.dtype).reshape(blocks, tile, w)
            out[j * blocks : (j + 1) * blocks] = total
            chunk += 1


def transform(core, x_own, x_other, weight, bias, first, sizes, tile, w, limit):
    any_spec = pl.BlockSpec(memory_space=pl.ANY)
    rows, width = x_own.shape
    blocks = 2 * rows // tile
    chunks = sum(sizes)
    return pl.pallas_call(
        functools.partial(message_kernel, first),
        out_shape=tuple(jax.ShapeDtypeStruct((n * blocks, tile, w), jnp.bfloat16) for n in sizes),
        in_specs=[pl.BlockSpec(memory_space=pltpu.SMEM)] + [any_spec] * 4,
        out_specs=tuple(pl.BlockSpec(memory_space=pltpu.VMEM) for n in sizes),
        scratch_shapes=[
            pltpu.VMEM((2 * rows, width), jnp.bfloat16),
            pltpu.VMEM((width, chunks * w), jnp.bfloat16),
            pltpu.VMEM((1, bias.shape[0]), jnp.float32),
            pltpu.SemaphoreType.DMA((4,)),
        ],
        compiler_params=pltpu.CompilerParams(vmem_limit_bytes=limit * 1024 * 1024),
        cost_estimate=pl.CostEstimate(
            flops=32 * rows * width * chunks * w,
            bytes_accessed=4 * rows * width + 2 * width * chunks * w,
            transcendentals=0,
        ),
    )(core.astype(jnp.int32).reshape(1), x_own, x_other, weight, bias.reshape(1, -1))


def finish_kernel(hidden, near, got, weight, out):
    total = hidden[...]
    w = near.shape[1]
    total += jnp.dot(near[...], weight[:w], preferred_element_type=jnp.float32)
    total += jnp.dot(got[...], weight[w:], preferred_element_type=jnp.float32)
    total = jnp.maximum(total, 0.0)
    mean = jnp.mean(total * total, axis=1, keepdims=True)
    out[...] = total / jnp.sqrt(mean + 1e-06)


def finish(hidden, near, got, weight):
    rows, width = hidden.shape
    block = 128
    by_row = lambda w: pl.BlockSpec((block, w), lambda i: (i, 0))
    return pl.pallas_call(
        finish_kernel,
        grid=(rows // block,),
        out_shape=jax.ShapeDtypeStruct(hidden.shape, jnp.float32),
        in_specs=[
            by_row(width),
            by_row(near.shape[1]),
            by_row(near.shape[1]),
            pl.BlockSpec(weight.shape, lambda i: (0, 0)),
        ],
        out_specs=by_row(width),
        compiler_params=pltpu.CompilerParams(vmem_limit_bytes=8 * 1024 * 1024),
    )(hidden, near, got, weight)


def local(
    features,
    walk_counts,
    tile_rows,
    tile_cols,
    live_tiles,
    neigh_weight,
    neigh_bias,
    combine_weight,
    combine_bias,
):
    rows_dev, width = features.shape
    tile = walk_counts.shape[3]
    slots = walk_counts.shape[2]
    half = width // 2
    cw = half // CHUNKS
    blocks = rows_dev // tile
    x_lo, y, z, x_hi, core = (lax.axis_index(a) for a in AXES)

    x_other = swap(features, "core", "other_features_0")
    own0 = transform(
        core, features, x_other, neigh_weight, neigh_bias, 0, (1,), tile, cw, 12
    )[0]
    first = swap(own0, "x_lo", "gather_x_0")
    own1, own_rest = transform(
        core,
        after(features, own0),
        x_other,
        neigh_weight,
        neigh_bias,
        cw,
        (1, CHUNKS - 2),
        tile,
        cw,
        14,
    )

    live = live_tiles[0, 0]
    used = jnp.arange(slots, dtype=jnp.int32) < live
    counts = walk_counts[0, 0]
    c_own = jnp.where(used[:, None, None], counts, 0).astype(jnp.bfloat16)
    pair0 = after(jnp.concatenate([own0, after(first, own1)]), own1)
    rows_own = jnp.where(used, tile_rows[0, 0], 0)
    meta = jnp.stack(
        [rows_own, jnp.where(used, tile_cols[0, 0], 0), jnp.full((slots,), live, jnp.int32)]
    )
    c_other = swap(after(c_own, own0), "core", "other_tiles")
    metas = jnp.stack([meta, swap(after(meta, own0), "core", "other_meta")])
    k = metas[:, 1]
    src = (
        (ring_slot((k // 4) % 4, y, core) * 2 + ((k // 16) ^ x_lo)) * 8
        + jnp.arange(2, dtype=jnp.int32)[:, None] * 4
        + k % 4
    ).reshape(-1)
    b = metas[:, 0]
    ring = ring_slot(b // 16, z, core)
    ring = jnp.where(ring == 0, 3, jnp.where(ring == 3, 0, ring))
    dst = (
        ((ring * 2 + 1 - (((b // 8) % 2) ^ x_hi)) * 2)
        + (((b // 4) % 2) ^ core)
    ) * 4 + b % 4
    dst = dst.reshape(-1)
    lives = metas[:, 2, 0]

    row_sums = jnp.concatenate(
        [jnp.sum(c_own.astype(jnp.float32), axis=2), jnp.sum(c_other.astype(jnp.float32), axis=2)]
    )
    onehot = (jnp.arange(64, dtype=jnp.int32)[:, None] == dst[None, :]).astype(jnp.float32)
    deg = jnp.dot(onehot, row_sums, precision=lax.Precision.HIGHEST).astype(jnp.int32)
    parts = (deg[:, None, :] >> (5 * jnp.arange(4, dtype=jnp.int32))[None, :, None]) & 31
    parts = parts.astype(jnp.bfloat16).reshape(256, tile)

    hidden = (
        jnp.dot(after(features, own0), combine_weight[:width], preferred_element_type=jnp.float32)
        + combine_bias
    )
    later_weight = after(combine_weight, own0)
    w_own = lax.dynamic_slice_in_dim(later_weight, width + core * half, half, 0)
    w_other = lax.dynamic_slice_in_dim(later_weight, width + (1 - core) * half, half, 0)

    second = swap(after(own1, first), "x_lo", "gather_x_1")
    f32, bf16 = jnp.float32, jnp.bfloat16
    near_all, far_all, part_all, pass_all = [], [], [], []
    scale = None

    def far(pair, got, j):
        if j == 1:
            got = after(got, parts)
        near_all.append(jnp.concatenate([pair, got]))
        far_all.append(step(near_all[j], "y", 1, f"gather_far_{j}"))

    far(pair0, step(pair0, "y", 0, "gather_near_0"), 0)
    second = after(second, near_all[0])
    rest = swap(after(own_rest, second), "x_lo", "gather_x_rest")
    size = own0.shape[0]
    split = lambda x: [x[i * size : (i + 1) * size] for i in range(CHUNKS - 2)]
    own = [own0, own1] + split(own_rest)
    partner = [first, second] + split(rest)
    for j in range(1, CHUNKS):
        pair = jnp.concatenate([own[j], partner[j]])
        pair = after(pair, near_all[j - 1], *far_all[: j - 1])
        far(pair, step(pair, "y", 0, f"gather_near_{j}"), j)

    cut = (CHUNKS - 2) * cw
    last_weight = jnp.concatenate([w_own[cut:], w_other[cut:]])

    def tiles(j):
        earlier = (rest, near_all[1], hidden, last_weight) if j == 0 else ()
        if j == 1:
            earlier += (near_all[j + 1],)
        if j >= 2:
            earlier += (pass_all[0],)
        with jax.named_scope(f"tiles_{j}"):
            part_all.append(
                tile_sums(
                    after(src, *earlier) if earlier else src,
                    dst,
                    lives,
                    c_own,
                    c_other,
                    parts,
                    j == 0,
                    near_all[j],
                    far_all[j],
                    2**34 if j == 1 else 2**31 if j == 0 else 2**20,
                )
            )

    tiles(0)
    stays = []
    for j in range(CHUNKS):
        send, pass_on, stay = part_all[j]
        size = stay.shape[0] // 2
        got = step(send, "z", 0, f"sum_near_{j}")
        if j == 0:
            tiles(1)
        if j + 1 < CHUNKS:
            got = after(got, part_all[j + 1][0])
        passed = (got[: 2 * size].astype(f32) + pass_on.astype(f32)).astype(bf16)
        pass_all.append(passed)
        stays.append(got[2 * size :].astype(f32) + stay.astype(f32))
        if j == 0:
            for i in range(2, CHUNKS):
                tiles(i)

    means, ready = [], []
    for j in range(CHUNKS):
        stay = stays[j]
        size = stay.shape[0] // 2
        got = step(pass_all[j], "z", 1, f"sum_far_{j}")
        if j == 0:
            got = after(got, part_all[2][0])
        elif j + 1 < CHUNKS:
            got = after(got, pass_all[j + 1])
        passed = (got[:size].astype(f32) + stay[:size]).astype(bf16)
        ready.append((passed, got[size:].astype(f32) + stay[size:]))

    for j, (passed, stay) in enumerate(ready):
        got = swap(passed, "x_hi", f"sum_x_{j}")
        if j + 2 < CHUNKS:
            got = after(got, pass_all[j + 2])
        elif j + 1 < CHUNKS:
            got = after(got, ready[j + 1][0])
        pooled = got.astype(f32) + stay
        if j == 0:
            deg = jnp.sum(
                pooled[8 * tile :].reshape(8, 4, tile)
                * jnp.array([1, 32, 1024, 32768], f32)[None, :, None],
                axis=1,
            )
            scale = 1.0 / (1.0 + deg)
            pooled = pooled[: 8 * tile]
        factor = after(scale, passed)[..., None]
        mean = (pooled.reshape(8, tile, cw) * factor).astype(bf16)
        means.append(mean.reshape(2, rows_dev, cw))

    def both_halves(chunks, name):
        near = jnp.concatenate([means[j][0] for j in chunks], axis=1)
        away = jnp.concatenate([means[j][1] for j in chunks], axis=1)
        return near, swap(away, "core", name)

    near, got = both_halves(range(CHUNKS - 2), "mean_core_0")
    hidden = hidden + jnp.dot(near, w_own[:cut], preferred_element_type=f32)
    hidden = hidden + jnp.dot(got, w_other[:cut], preferred_element_type=f32)
    near, got = both_halves(range(CHUNKS - 2, CHUNKS), "mean_core_1")
    return finish(hidden, near, got, last_weight)


def solution(mesh):
    fine = Mesh(mesh.devices.reshape(SIZES), AXES)
    row = AXES[:2]
    col = AXES[2:]
    return jax.shard_map(
        local,
        mesh=fine,
        in_specs=(
            P(AXES, None),
            P(row, col, None, None, None),
            P(row, col, None),
            P(row, col, None),
            P(row, col),
            P(),
            P(),
            P(),
            P(),
        ),
        out_specs=P(AXES, None),
        check_vma=False,
    )
```
